32 devices in a mesh: dp: 2 (over x), row: 4 (over y, core), col: 4 (over z).
Axes of the slice: x: 2, y: 2, z: 4, core: 2. Of those that a mesh axis runs over, the one named last changes fastest.
Arguments:
- tokens: bfloat16 [8192, 2048], P(('dp', 'row'), 'col'), may hold values from -6 to 6
- segment_ids: int32 [8, 1024], P(('dp', 'col')), may hold values from 0 to 7, never falling along the last dimension, each value on 1 to 512 neighbouring positions
- norm1_gain: float32 [2048], P('col'), may hold values from 0.1 to 1.9
- norm1_bias: float32 [2048], P('col'), may hold values from -4 to 4
- norm2_gain: float32 [2048], P('col'), may hold values from 0.1 to 1.9
- norm2_bias: float32 [2048], P('col'), may hold values from -4 to 4
- qkv_weight: bfloat16 [2048, 6144], P('col', 'row'), may hold values from -0.125 to 0.125
- qkv_bias: float32 [6144], P('row'), may hold values from -6 to 6
- out_weight: bfloat16 [2048, 2048], P('row', 'col'), may hold values from -0.5 to 0.5
- out_bias: float32 [2048], P('col'), may hold values from -4 to 4
- up_weight: bfloat16 [2048, 8192], P('col', 'row'), may hold values from -0.125 to 0.125
- up_bias: float32 [8192], P('row'), may hold values from -6 to 6
- down_weight: bfloat16 [8192, 2048], P('row', 'col'), may hold values from -0.0625 to 0.0625
- down_bias: float32 [2048], P('col'), may hold values from -4 to 4
- cotangent: bfloat16 [8192, 2048], P(('dp', 'row'), 'col'), may hold values from -6 to 6
Outputs:
- mixed: bfloat16 [8192, 2048], P(('dp', 'row'), 'col')
- input_grad: float32 [8192, 2048], P(('dp', 'row'), 'col')
- norm1_gain_grad: float32 [2048], P('col')
- norm1_bias_grad: float32 [2048], P('col')
- norm2_gain_grad: float32 [2048], P('col')
- norm2_bias_grad: float32 [2048], P('col')
- qkv_weight_grad: float32 [2048, 6144], P('col', 'row')
- qkv_bias_grad: float32 [6144], P('row')
- out_weight_grad: float32 [2048, 2048], P('row', 'col')
- out_bias_grad: float32 [2048], P('col')
- up_weight_grad: float32 [2048, 8192], P('col', 'row')
- up_bias_grad: float32 [8192], P('row')
- down_weight_grad: float32 [8192, 2048], P('row', 'col')
- down_bias_grad: float32 [2048], P('col')
The draws below stay inside these ranges and needn't reach their ends.
Inputs may be any that keep to these rules, and one draw needn't show every extreme that they name: `segment_ids`: within each sequence the numbers never fall; a document holds 1 to 512 tokens of the sequence.
All inputs are finite; a program needn't handle non-finite values.
Results may differ from the reference program's by a relative error of at most 0.011.
Values may be sent and summed in bfloat16 or wider, within the bound.
No kernel may reach another device: no remote copies, remote signals or barrier semaphores. Data moves between devices by JAX's collectives and lax.ppermute only.
A program may use at most 384 MiB of HBM per device.

```python
import math
import jax
import jax.numpy as jnp
import numpy as np
from jax import lax

D = 2048
FF = 8192
HEADS = 8
LEN = 1024
HEAD_DIM = 256
ROTARY = 64
SEQS = 8
TOKENS = 8192


def shard_levels(own_key, shape, split, least, top_value):
    loudness = 1.0
    for dim, parts in split:
        steps = jax.random.uniform(jax.random.fold_in(jax.random.fold_in(own_key, 6), dim), (parts,), jnp.float32, least / len(split), top_value / len(split))
        loudness = loudness * jnp.repeat(jnp.exp(steps), shape[dim] // parts).reshape((-1,) + (1,) * (len(shape) - 1 - dim))
    return loudness


def length_profile(amount, total, bound, slope):
    loads = [(1 << 20) // math.isqrt(standing ** slope) + 1 for standing in range(2, amount + 1)]
    spare, given = total - bound - (amount - 1), [1] * (amount - 1)
    while spare > 0:
        candidates = [i for i in range(amount - 1) if given[i] < bound]
        pool, budget = sum([loads[i] for i in candidates]), spare
        for i in candidates:
            more = min(bound - given[i], max(1, budget * loads[i] // pool), spare)
            given[i] = given[i] + more
            spare = spare - more
    return np.array([bound] + given)


def uneven_parts(own_key, amount, total, limit, slope):
    if amount == 2:
        one = jax.random.randint(own_key, (), max(1, total - limit), min(limit, total - 1) + 1)
        return jnp.stack([one, total - one])
    lengths = jnp.asarray(length_profile(amount, total, limit, slope), jnp.int32)
    couples = (amount - 1) // 2
    source_of, sink = lengths[1:1 + 2 * couples:2], lengths[2:2 + 2 * couples:2]
    room = jnp.minimum(source_of - 1, limit - sink)
    shifted = jax.random.randint(jax.random.fold_in(own_key, 1), (couples,), 0, 1 << 20) % (room + 1)
    lengths = lengths.at[1:1 + 2 * couples:2].set(source_of - shifted).at[2:2 + 2 * couples:2].set(sink + shifted)
    return lengths[jax.random.permutation(jax.random.fold_in(own_key, 2), amount)]


def normal_values(key, extent, scale, most, cuts=(), kind=jnp.bfloat16):
    drawn = scale * jax.random.normal(key, extent, jnp.float32)
    if cuts:
        drawn = drawn * shard_levels(key, extent, cuts, -0.22, 0.18)
    return jnp.clip(drawn, -most, most).astype(kind)


def setup_inputs(seed: int = 0) -> dict:
    key_of = jax.random.split(jax.random.key(seed), 16)
    return {
        "tokens": normal_values(key_of[0], (TOKENS, D), 1.0, 6.0, ((0, 8), (1, 4))),
        "segment_ids": jax.vmap(lambda own: jnp.searchsorted(jnp.cumsum(uneven_parts(own, max(4, LEN // 128), LEN, LEN // 2, 1)), jnp.arange(LEN), side="right"))(jax.random.split(key_of[1], SEQS)).reshape((SEQS, LEN)).astype(jnp.int32),
        "norm1_gain": jnp.clip(1.0 + 0.18 * jax.random.normal(key_of[2], (D,), jnp.float32), 0.1, 1.9),
        "norm1_bias": normal_values(key_of[3], (D,), 0.3, 4.0, ((0, 4),), jnp.float32),
        "norm2_gain": jnp.clip(1.0 + 0.18 * jax.random.normal(key_of[4], (D,), jnp.float32), 0.1, 1.9),
        "norm2_bias": normal_values(key_of[5], (D,), 0.3, 4.0, ((0, 4),), jnp.float32),
        "qkv_weight": normal_values(key_of[6], (D, 3 * D), D ** -0.5, 0.125, ((0, 4), (1, 4))),
        "qkv_bias": normal_values(key_of[7], (3 * D,), 0.5, 6.0, ((0, 4),), jnp.float32),
        "out_weight": normal_values(key_of[8], (D, D), (D // 16) ** -0.5, 0.5, ((0, 4), (1, 4))),
        "out_bias": normal_values(key_of[9], (D,), 0.3, 4.0, ((0, 4),), jnp.float32),
        "up_weight": normal_values(key_of[10], (D, FF), D ** -0.5, 0.125, ((0, 4), (1, 4))),
        "up_bias": normal_values(key_of[11], (FF,), 0.5, 6.0, ((0, 4),), jnp.float32),
        "down_weight": normal_values(key_of[12], (FF, D), FF ** -0.5, 0.0625, ((0, 4), (1, 4))),
        "down_bias": normal_values(key_of[13], (D,), 0.3, 4.0, ((0, 4),), jnp.float32),
        "cotangent": normal_values(key_of[14], (TOKENS, D), 1.0, 6.0, ((0, 8), (1, 4))),
    }


EPS = 1e-05
BASE = 10000.0
HIGHEST = lax.Precision.HIGHEST

@jax.custom_vjp
def low(v):
    return lax.optimization_barrier(v.astype(jnp.bfloat16)).astype(jnp.float32)

@jax.custom_vjp
def low_back(v):
    return v

def low_keep(v):
    return (low(v), None)

def low_pass(kept, grad):
    return (grad,)

def back_keep(v):
    return (v, None)

def back_low(kept, grad):
    return (low(grad),)
low.defvjp(low_keep, low_pass)
low_back.defvjp(back_keep, back_low)

def tables(length):
    half = ROTARY // 2
    places = jnp.arange(length).astype(jnp.float32)
    freqs = BASE ** (-(jnp.arange(half).astype(jnp.float32) * 2.0) / ROTARY)
    angles = places[:, None] * freqs[None, :]
    return (jnp.cos(angles)[:, None, :], jnp.sin(angles)[:, None, :])

def rotate(part, cosine, sine):
    half = ROTARY // 2
    first_half = part[..., :half]
    second_half = part[..., half:ROTARY]
    return jnp.concatenate([first_half * cosine - second_half * sine, second_half * cosine + first_half * sine, part[..., ROTARY:]], -1)

def attend(qkv, segs):
    groups = segs.shape[0]
    shaped = qkv.reshape(groups, LEN, HEADS, 3, HEAD_DIM)
    cosine, sine = tables(LEN)
    query = low(rotate(shaped[:, :, :, 0], cosine, sine))
    keys = low(rotate(shaped[:, :, :, 1], cosine, sine))
    values = low(shaped[:, :, :, 2])
    raw = jnp.einsum('gqhd,gkhd->ghqk', query, keys, precision=HIGHEST)
    scores = low_back(raw) * HEAD_DIM ** (-0.5)
    causal = jnp.arange(LEN)[:, None] >= jnp.arange(LEN)[None, :]
    allowed = (segs[:, :, None] == segs[:, None, :]) & causal[None]
    masked = jnp.where(allowed[:, None], scores, -1e+30)
    peak = lax.optimization_barrier(jnp.max(masked, -1, keepdims=True))
    expos = jnp.exp(masked - peak)
    probs = low(expos / lax.optimization_barrier(jnp.sum(expos, -1, keepdims=True)))
    result = jnp.einsum('ghqk,gkhd->gqhd', probs, values, precision=HIGHEST)
    return low(low_back(result.reshape(groups * LEN, D)))

def forward(inputs, segs, gain_one, bias_one, gain_two, bias_two, w_qkv, b_qkv, w_out, b_out, w_up, b_up, w_down, b_down):
    mean = lax.optimization_barrier(jnp.mean(inputs, -1, keepdims=True))
    centred = inputs - mean
    variance = lax.optimization_barrier(jnp.mean(centred * centred, -1, keepdims=True))
    normed = centred * lax.rsqrt(variance + EPS)
    first = low(normed * gain_one + bias_one)
    second = low(normed * gain_two + bias_two)
    qkv = low_back(jnp.dot(first, w_qkv, precision=HIGHEST) + b_qkv)
    attended = attend(qkv, segs)
    up_value = low_back(jnp.dot(second, w_up, precision=HIGHEST) + b_up)
    activ = low(jax.nn.gelu(up_value, approximate=False))
    attn_part = jnp.dot(attended, w_out, precision=HIGHEST) + b_out
    mlp_part = jnp.dot(activ, w_down, precision=HIGHEST) + b_down
    return inputs + attn_part + mlp_part

def reference(tokens, segment_ids, norm1_gain, norm1_bias, norm2_gain, norm2_bias, qkv_weight, qkv_bias, out_weight, out_bias, up_weight, up_bias, down_weight, down_bias, cotangent):
    group = math.gcd(SEQS, max(1, 4096 // LEN))
    steps_count = SEQS // group
    params = tuple((p.astype(jnp.float32) for p in (norm1_gain, norm1_bias, norm2_gain, norm2_bias, qkv_weight, qkv_bias, out_weight, out_bias, up_weight, up_bias, down_weight, down_bias)))
    inputs = tokens.astype(jnp.float32).reshape(steps_count, group * LEN, D)
    segs = segment_ids.astype(jnp.int32).reshape(steps_count, group, LEN)
    grads_in = cotangent.astype(jnp.float32).reshape(steps_count, group * LEN, D)

    def one_group(totals, item):
        block_in, block_segs, block_grad = item

        def closed(value, *weights):
            return forward(value, block_segs, *weights)
        result, pull = jax.vjp(closed, block_in, *params)
        grads = pull(block_grad)
        summed = tuple((a + b for a, b in zip(totals, grads[1:])))
        return (summed, (result.astype(jnp.bfloat16), grads[0]))
    start = tuple((jnp.zeros_like(p) for p in params))
    totals, (results, input_grads) = lax.scan(one_group, start, (inputs, segs, grads_in))
    return (results.reshape(TOKENS, D), input_grads.reshape(TOKENS, D), totals[0], totals[1], totals[2], totals[3], totals[4], totals[5], totals[6], totals[7], totals[8], totals[9], totals[10], totals[11])
```

```python
import jax
import jax.numpy as jnp
from jax import lax
from jax.sharding import PartitionSpec as P

LEN = 1024
HEAD_DIM = 256
ROTARY = 64


EPS = 1e-05
BASE = 10000.0
LOW = jnp.bfloat16
FULL = jnp.float32


def tables(length):
    half = ROTARY // 2
    places = jnp.arange(length).astype(jnp.float32)
    freqs = BASE ** (-(jnp.arange(half).astype(jnp.float32) * 2.0) / ROTARY)
    angles = places[:, None] * freqs[None, :]
    return (jnp.cos(angles)[:, None, :], jnp.sin(angles)[:, None, :])


def rotate(part, cosine, sine):
    half = ROTARY // 2
    first_half = part[..., :half]
    second_half = part[..., half:ROTARY]
    return jnp.concatenate(
        [
            first_half * cosine - second_half * sine,
            second_half * cosine + first_half * sine,
            part[..., ROTARY:],
        ],
        -1,
    )


def allowed_pairs(segs):
    causal = jnp.arange(LEN)[:, None] >= jnp.arange(LEN)[None, :]
    return (segs[:, None] == segs[None, :]) & causal


def masked_scores(query, keys, segs):
    raw = jnp.einsum("qhd,khd->hqk", query, keys, preferred_element_type=FULL)
    return jnp.where(allowed_pairs(segs)[None], raw * HEAD_DIM ** (-0.5), -1e30)


def attend_forward(block):
    query, keys, values, segs = block
    masked = masked_scores(query, keys, segs)
    peak = jnp.max(masked, -1, keepdims=True)
    expos = jnp.exp(masked - peak)
    total = jnp.sum(expos, -1, keepdims=True)
    probs = (expos / total).astype(LOW)
    result = jnp.einsum("hqk,khd->qhd", probs, values, preferred_element_type=FULL)
    return (result, (peak + jnp.log(total))[..., 0])


def attend_backward(block):
    query, keys, values, logsum, segs, grad_out = block
    masked = masked_scores(query, keys, segs)
    probs = jnp.exp(masked - logsum[..., None])
    probs_grad = jnp.einsum("qhd,khd->hqk", grad_out, values, preferred_element_type=FULL)
    values_grad = jnp.einsum(
        "hqk,qhd->khd", probs.astype(LOW), grad_out, preferred_element_type=FULL
    )
    score_grad = probs * (probs_grad - jnp.sum(probs * probs_grad, -1, keepdims=True))
    raw_grad = (score_grad * HEAD_DIM ** (-0.5)).astype(LOW)
    query_grad = jnp.einsum("hqk,khd->qhd", raw_grad, keys, preferred_element_type=FULL)
    keys_grad = jnp.einsum("hqk,qhd->khd", raw_grad, query, preferred_element_type=FULL)
    return (query_grad, keys_grad, values_grad)


def exact_gelu(value):
    return jax.nn.gelu(value, approximate=False)


def dot(a, b):
    return jnp.dot(a, b, preferred_element_type=FULL)


def swapped(n):
    return [0, 2, 1, 3] if n == 4 else list(range(n))


class Plan:
    def __init__(self, part):
        self.nd, self.nr, self.nc = (lax.axis_size(a) for a in ("dp", "row", "col"))
        self.d, self.r, self.c = (lax.axis_index(a) for a in ("dp", "row", "col"))
        self.part = part
        self.piece = part // self.nd
        self.f = swapped(self.nr)
        self.pairs = [
            (r * self.nc + c, self.f[c] * self.nc + self.f[r])
            for r in range(self.nr)
            for c in range(self.nc)
        ]

    def swap(self, v):
        return jnp.asarray(self.f, jnp.int32)[v]

    def turn(self, x):
        return lax.ppermute(x, ("row", "col"), self.pairs)

    def flip(self, x, bits):
        return lax.ppermute(x, "row", [(r, r ^ bits) for r in range(self.nr)])

    def shift(self, x, s):
        return lax.ppermute(x, "dp", [(d, (d + s) % self.nd) for d in range(self.nd)])

    def chunk_start(self, s, q):
        return self.swap(self.r ^ q) * self.part + lax.rem(self.d - s + self.nd, self.nd) * self.piece

    def to_chunks(self, whole):
        return jnp.concatenate(
            [
                lax.dynamic_slice_in_dim(whole, self.chunk_start(s, q), self.piece, whole.ndim - 1)
                for s in range(self.nd)
                for q in range(self.nr)
            ],
            -1,
        )

    def part_of(self, chunked, j):
        q = self.swap(j) ^ self.r
        return jnp.concatenate(
            [
                lax.dynamic_slice_in_dim(
                    chunked,
                    (lax.rem(self.d - h + self.nd, self.nd) * self.nr + q) * self.piece,
                    self.piece,
                    chunked.ndim - 1,
                )
                for h in range(self.nd)
            ],
            -1,
        )

    def spread(self, block, axis):
        own = self.turn(
            lax.dynamic_slice_in_dim(block, self.d * self.piece, self.piece, axis)
        )
        half = self.piece // 2
        by_y = self.flip(own, 2)
        chunks = {(0, 0): own, (0, 2): by_y}
        for s in range(1, self.nd):
            by_x = self.shift(own, s)
            chunks[s, 0] = by_x
            chunks[s, 2] = jnp.concatenate(
                [
                    self.shift(lax.slice_in_dim(by_y, 0, half, axis=axis), s),
                    self.flip(lax.slice_in_dim(by_x, half, self.piece, axis=axis), 2),
                ],
                axis,
            )
        for s in range(self.nd):
            for q in (0, 2):
                chunks[s, q + 1] = self.flip(chunks[s, q], 1)
        return jnp.concatenate(
            [chunks[s, q] for s in range(self.nd) for q in range(self.nr)], axis
        )

    def collect(self, grad, axis):
        def chunk(s, q):
            at = (s * self.nr + q) * self.piece
            return lax.slice_in_dim(grad, at, at + self.piece, axis=axis)

        def add(a, *others):
            total = a.astype(FULL)
            for other in others:
                total = total + other.astype(FULL)
            return total.astype(LOW)

        half = self.piece // 2

        def lower(x):
            return lax.slice_in_dim(x, 0, half, axis=axis)

        def upper(x):
            return lax.slice_in_dim(x, half, self.piece, axis=axis)

        by_core = {
            (s, q): add(chunk(s, q), self.flip(chunk(s, q + 1).astype(LOW), 1))
            for s in range(self.nd)
            for q in (0, 2)
        }
        rest = range(1, self.nd)
        first = {
            q: add(lower(by_core[0, q]), *[self.shift(lower(by_core[s, q]), self.nd - s) for s in rest])
            for q in (0, 2)
        }
        low_sum = add(first[0], self.flip(first[2], 2))
        second = {
            s: add(upper(by_core[s, 0]), self.flip(upper(by_core[s, 2]), 2)) for s in range(self.nd)
        }
        high_sum = add(second[0], *[self.shift(second[s], self.nd - s) for s in rest])
        mine = self.turn(jnp.concatenate([low_sum, high_sum], axis))
        shape = list(mine.shape)
        shape[axis] = self.part
        result = jnp.zeros(shape, LOW)
        for s in range(self.nd):
            piece = mine if s == 0 else self.shift(mine, s)
            at = lax.rem(self.d - s + self.nd, self.nd) * self.piece
            result = lax.dynamic_update_slice_in_dim(result, piece, at, axis)
        return result.astype(FULL)

    def right(self, x):
        return lax.ppermute(x, "col", [(i, i + 1) for i in range(self.nc - 1)])

    def left(self, x):
        return lax.ppermute(x, "col", [(i + 1, i) for i in range(self.nc - 1)])

    def gather_col(self, x):
        from_left, from_right = [x], [x]
        for _ in range(self.nc - 1):
            from_left.append(self.right(from_left[-1]))
            from_right.append(self.left(from_right[-1]))
        parts = []
        for j in range(self.nc):
            value = x
            for c in range(self.nc):
                if c > j:
                    value = jnp.where(self.c == c, from_left[c - j], value)
                elif c < j:
                    value = jnp.where(self.c == c, from_right[j - c], value)
            parts.append(value)
        return jnp.concatenate(parts, -1)

    def scatter_col(self, total):
        low = total.astype(LOW)
        result = self.part_of(total, self.c)
        for send, way in ((self.right, 1), (self.left, -1)):
            carried = None
            for step in range(1, self.nc):
                j = jnp.clip(self.c + way * (self.nc - step), 0, self.nc - 1)
                piece = self.part_of(low, j)
                if carried is not None:
                    piece = (piece.astype(FULL) + carried.astype(FULL)).astype(LOW)
                carried = send(piece)
            result = result + carried.astype(FULL)
        return result


def local(
    tokens,
    segment_ids,
    norm1_gain,
    norm1_bias,
    norm2_gain,
    norm2_bias,
    qkv_weight,
    qkv_bias,
    out_weight,
    out_bias,
    up_weight,
    up_bias,
    down_weight,
    down_bias,
    cotangent,
):
    rows, part = tokens.shape
    plan = Plan(part)
    width = part * plan.nc
    qkv_cols = qkv_weight.shape[1]
    up_cols = up_weight.shape[1]
    seqs = rows // LEN
    heads = qkv_cols // (3 * HEAD_DIM)

    segs = lax.ppermute(
        segment_ids,
        ("row", "col"),
        [(r * plan.nc + c, c * plan.nc + r) for r in range(plan.nr) for c in range(plan.nc)],
    )
    biases = plan.turn(jnp.concatenate([qkv_bias, up_bias]))
    norm_params = plan.to_chunks(
        plan.gather_col(jnp.stack([norm1_gain, norm1_bias, norm2_gain, norm2_bias]))
    )
    gain1, bias1, gain2, bias2 = norm_params

    qkv_all = plan.spread(qkv_weight, 0)
    inputs_low = plan.to_chunks(plan.gather_col(tokens))
    up_all = plan.spread(up_weight, 0)
    out_all = plan.spread(out_weight, 1)
    down_all = plan.spread(down_weight, 1)
    grad_low = plan.to_chunks(plan.gather_col(cotangent))

    inputs = inputs_low.astype(FULL)
    mean = jnp.sum(inputs, 1, keepdims=True) / width
    variance = jnp.sum(inputs * inputs, 1, keepdims=True) / width - mean * mean
    inv_std = lax.rsqrt(variance + EPS)
    normed = (inputs - mean) * inv_std
    first = (normed * gain1 + bias1).astype(LOW)
    second = (normed * gain2 + bias2).astype(LOW)

    qkv_pre = dot(first, qkv_all) + biases[:qkv_cols]
    up_pre = dot(second, up_all) + biases[qkv_cols:]
    shaped = qkv_pre.reshape(seqs, LEN, heads, 3, HEAD_DIM)
    cosine, sine = tables(LEN)

    def rotate_pair(query_in, keys_in):
        return (rotate(query_in, cosine, sine), rotate(keys_in, cosine, sine))

    (query_rot, keys_rot), rotate_pull = jax.vjp(
        rotate_pair, shaped[:, :, :, 0], shaped[:, :, :, 1]
    )
    query = query_rot.astype(LOW)
    keys = keys_rot.astype(LOW)
    values = shaped[:, :, :, 2].astype(LOW)
    attended, logsum = lax.map(attend_forward, (query, keys, values, segs))
    attn_low = attended.reshape(rows, heads * HEAD_DIM).astype(LOW)
    activ, gelu_pull = jax.vjp(exact_gelu, up_pre)
    act_low = activ.astype(LOW)
    branch = plan.scatter_col(dot(attn_low, out_all) + dot(act_low, down_all))
    mixed = (tokens.astype(FULL) + branch + out_bias + down_bias).astype(LOW)

    out_weight_grad = plan.collect(
        jnp.einsum("ta,tb->ab", attn_low, grad_low, preferred_element_type=FULL).astype(LOW), 1
    )
    down_weight_grad = plan.collect(
        jnp.einsum("ta,tb->ab", act_low, grad_low, preferred_element_type=FULL).astype(LOW), 1
    )
    output_bias_grad = jnp.sum(cotangent, 0, dtype=FULL)
    attn_grad = (
        jnp.einsum("tb,ab->ta", grad_low, out_all, preferred_element_type=FULL)
        .astype(LOW)
        .reshape(seqs, LEN, heads, HEAD_DIM)
    )
    act_grad = jnp.einsum("tb,ab->ta", grad_low, down_all, preferred_element_type=FULL)
    up_grad = gelu_pull(act_grad)[0].astype(LOW)
    query_grad, keys_grad, values_grad = lax.map(
        attend_backward, (query, keys, values, logsum, segs, attn_grad)
    )
    query_pre_grad, keys_pre_grad = rotate_pull((query_grad, keys_grad))
    qkv_grad = (
        jnp.stack([query_pre_grad, keys_pre_grad, values_grad], 3)
        .reshape(rows, qkv_cols)
        .astype(LOW)
    )
    first_grad = jnp.einsum("tn,dn->td", qkv_grad, qkv_all, preferred_element_type=FULL)
    second_grad = jnp.einsum("tn,dn->td", up_grad, up_all, preferred_element_type=FULL)
    normed_grad = first_grad * gain1 + second_grad * gain2
    mine = plan.scatter_col(normed_grad)
    grad_stats = lax.psum(
        jnp.stack([jnp.sum(normed_grad, 1), jnp.sum(normed_grad * normed, 1)]), "col"
    )
    own_normed = (tokens.astype(FULL) - mean) * inv_std
    input_grad = cotangent.astype(FULL) + inv_std * (
        mine - grad_stats[0][:, None] / width - own_normed * (grad_stats[1][:, None] / width)
    )
    qkv_weight_grad = plan.collect(
        jnp.einsum("td,tn->dn", first, qkv_grad, preferred_element_type=FULL).astype(LOW), 0
    )
    up_weight_grad = plan.collect(
        jnp.einsum("td,tn->dn", second, up_grad, preferred_element_type=FULL).astype(LOW), 0
    )

    sums = jnp.stack(
        [
            jnp.sum(first_grad * normed, 0),
            jnp.sum(first_grad, 0),
            jnp.sum(second_grad * normed, 0),
            jnp.sum(second_grad, 0),
        ]
    )
    sums = jnp.concatenate([plan.part_of(sums, j) for j in range(plan.nc)], -1)
    sums = lax.psum_scatter(sums, "col", scatter_dimension=1, tiled=True)
    small = lax.psum(
        jnp.concatenate(
            [
                sums.reshape(-1),
                output_bias_grad,
                jnp.sum(qkv_grad, 0, dtype=FULL),
                jnp.sum(up_grad, 0, dtype=FULL),
            ]
        ),
        ("dp", "row"),
    )
    norm_sums = small[: 4 * part].reshape(4, part)
    output_bias_grad = small[4 * part : 5 * part]
    bias_grads = plan.turn(small[5 * part :])
    return (
        mixed,
        input_grad,
        norm_sums[0],
        norm_sums[1],
        norm_sums[2],
        norm_sums[3],
        qkv_weight_grad,
        bias_grads[:qkv_cols],
        out_weight_grad,
        output_bias_grad,
        up_weight_grad,
        bias_grads[qkv_cols:],
        down_weight_grad,
        output_bias_grad,
    )


def solution(mesh):
    in_specs = (
        P(("dp", "row"), "col"),
        P(("dp", "col"), None),
        P("col"),
        P("col"),
        P("col"),
        P("col"),
        P("col", "row"),
        P("row"),
        P("row", "col"),
        P("col"),
        P("col", "row"),
        P("row"),
        P("row", "col"),
        P("col"),
        P(("dp", "row"), "col"),
    )
    out_specs = (
        P(("dp", "row"), "col"),
        P(("dp", "row"), "col"),
        P("col"),
        P("col"),
        P("col"),
        P("col"),
        P("col", "row"),
        P("row"),
        P("row", "col"),
        P("col"),
        P("col", "row"),
        P("row"),
        P("row", "col"),
        P("col"),
    )
    return jax.shard_map(local, mesh=mesh, in_specs=in_specs, out_specs=out_specs, check_vma=False)
```

```python
import functools

import jax
import jax.numpy as jnp
from jax import lax
from jax.experimental import pallas as pl
from jax.experimental.pallas import tpu as pltpu
from jax.sharding import PartitionSpec as P

LEN = 1024
HEAD_DIM = 256
ROTARY = 64


EPS = 1e-05
BASE = 10000.0
LOW = jnp.bfloat16
FULL = jnp.float32


SCOPED = 48 * 2**20
SPAN = 256


def params(count=1):
    return pltpu.CompilerParams(
        dimension_semantics=("arbitrary",) * count, vmem_limit_bytes=SCOPED
    )


CHEAP = pl.CostEstimate(flops=2 * 10**9, bytes_accessed=10**6, transcendentals=0)


def nn(a, b):
    return jnp.dot(a, b, preferred_element_type=FULL)


def nt(a, b):
    return lax.dot_general(a, b, (((1,), (1,)), ((), ())), preferred_element_type=FULL)


def tn(a, b):
    return lax.dot_general(a, b, (((0,), (0,)), ((), ())), preferred_element_type=FULL)


def whole(shape):
    return pl.BlockSpec(shape, lambda *_: (0,) * len(shape))


def norm_kernel(x_ref, par_ref, first_ref, second_ref, mean_ref, inv_ref):
    x = x_ref[...].astype(FULL)
    width = x.shape[1]
    mean = jnp.sum(x, 1, keepdims=True) / width
    centred = x - mean
    variance = jnp.sum(centred * centred, 1, keepdims=True) / width
    inv = lax.rsqrt(variance + EPS)
    normed = centred * inv
    first_ref[...] = (normed * par_ref[0:1, :] + par_ref[1:2, :]).astype(LOW)
    second_ref[...] = (normed * par_ref[2:3, :] + par_ref[3:4, :]).astype(LOW)
    mean_ref[...] = jnp.broadcast_to(mean, mean_ref.shape)
    inv_ref[...] = jnp.broadcast_to(inv, inv_ref.shape)


def norms(x, par, rows):
    width = x.shape[1]
    tile = 128
    wide = pl.BlockSpec((tile, width), lambda i: (i, 0))
    thin = pl.BlockSpec((tile, 128), lambda i: (i, 0))
    return pl.pallas_call(
        norm_kernel,
        grid=(rows // tile,),
        in_specs=[wide, whole(par.shape)],
        out_specs=[wide, wide, thin, thin],
        out_shape=[jax.ShapeDtypeStruct((rows, width), LOW)] * 2
        + [jax.ShapeDtypeStruct((rows, 128), FULL)] * 2,
        compiler_params=params(),
        cost_estimate=CHEAP,
        name="norms",
    )(x, par)


def turn_features(value, table_ref, at, sign):
    half = ROTARY // 2
    head = value[:, :128]
    cosine = table_ref[0, at, :]
    down = table_ref[1, at, :] * sign
    up = table_ref[2, at, :] * sign
    head = head * cosine + pltpu.roll(head, 128 - half, 1) * down + pltpu.roll(head, half, 1) * up
    return jnp.concatenate([head, value[:, 128:]], 1)


def nn2(x_ref, at, near_ref, far_ref):
    half = near_ref.shape[0]
    return nn(x_ref[at, :half], near_ref[...]) + nn(x_ref[at, half:], far_ref[...])


def column_pair(weight, cols, skip=0):
    rows = weight[0].shape[0]
    return [pl.BlockSpec((rows, cols), lambda j: (0, j + skip))] * 2


def qkv_kernel(x_ref, near_ref, far_ref, b_ref, table_ref, out_ref):
    rows = x_ref.shape[0]
    kind = lax.rem(pl.program_id(0), 3)
    for m in range(rows // SPAN):
        at = pl.ds(m * SPAN, SPAN)
        place = pl.ds(m * SPAN % LEN, SPAN)
        value = nn2(x_ref, at, near_ref, far_ref) + b_ref[...]
        turned = turn_features(value, table_ref, place, 1.0)
        out_ref[0, at, :] = jnp.where(kind == 2, value, turned).astype(LOW)


def project_qkv(first, weight, bias, table):
    rows = first.shape[0]
    tiles = weight[0].shape[1] // HEAD_DIM
    return pl.pallas_call(
        qkv_kernel,
        grid=(tiles,),
        in_specs=[
            whole(first.shape),
            *column_pair(weight, HEAD_DIM),
            pl.BlockSpec((1, HEAD_DIM), lambda j: (0, j)),
            whole(table.shape),
        ],
        out_specs=pl.BlockSpec((1, rows, HEAD_DIM), lambda j: (j, 0, 0)),
        out_shape=jax.ShapeDtypeStruct((tiles, rows, HEAD_DIM), LOW),
        compiler_params=params(),
        cost_estimate=CHEAP,
        name="project_qkv",
    )(first, *weight, bias.reshape(1, -1), table)


def key_range(i):
    low = max(0, (i * SPAN - 511) // SPAN)
    return low * SPAN, (i + 1) * SPAN


def masked(query, keys, seg_col, seg_row, start, low):
    raw = nt(query, keys) * HEAD_DIM ** (-0.5)
    shape = raw.shape
    q_at = lax.broadcasted_iota(jnp.int32, shape, 0) + (start - low)
    k_at = lax.broadcasted_iota(jnp.int32, shape, 1)
    return jnp.where((q_at >= k_at) & (seg_col == seg_row), raw, -1e30)


def attend_kernel(q_ref, k_ref, v_ref, col_ref, row_ref, out_ref, log_ref):
    for i in range(LEN // SPAN):
        low, high = key_range(i)
        at = pl.ds(i * SPAN, SPAN)
        span = pl.ds(low, high - low)
        scores = masked(
            q_ref[0, at, :], k_ref[0, span, :], col_ref[0, at, 0:1], row_ref[0, :, span], i * SPAN, low
        )
        peak = jnp.max(scores, 1, keepdims=True)
        expos = jnp.exp(scores - peak)
        total = jnp.sum(expos, 1, keepdims=True)
        probs = (expos * (1.0 / total)).astype(LOW)
        out_ref[at, :] = nn(probs, v_ref[0, span, :]).astype(LOW)
        log_ref[0, at, :] = jnp.broadcast_to(peak + jnp.log(total), (SPAN, 128))


def attend(qkv, seg_col, seg_row):
    tiles, rows, _ = qkv.shape
    heads, seqs = tiles // 3, rows // LEN

    def part(kind):
        return pl.BlockSpec((1, LEN, HEAD_DIM), lambda h, s: (3 * h + kind, s, 0))

    return pl.pallas_call(
        attend_kernel,
        grid=(heads, seqs),
        in_specs=[
            part(0),
            part(1),
            part(2),
            pl.BlockSpec((1, LEN, 128), lambda h, s: (s, 0, 0)),
            pl.BlockSpec((1, 1, LEN), lambda h, s: (s, 0, 0)),
        ],
        out_specs=[
            pl.BlockSpec((LEN, HEAD_DIM), lambda h, s: (s, h)),
            pl.BlockSpec((1, LEN, 128), lambda h, s: (h, s, 0)),
        ],
        out_shape=[
            jax.ShapeDtypeStruct((rows, heads * HEAD_DIM), LOW),
            jax.ShapeDtypeStruct((heads, rows, 128), FULL),
        ],
        compiler_params=params(2),
        cost_estimate=CHEAP,
        name="attend",
    )(qkv, qkv, qkv, seg_col, seg_row)


def attend_back_kernel(
    q_ref, k_ref, v_ref, g_ref, log_ref, col_ref, row_ref, table_ref, out_ref, sum_ref, dk_ref, dv_ref
):
    @pl.when(pl.program_id(1) == 0)
    def _():
        sum_ref[...] = jnp.zeros_like(sum_ref)

    def put(at, kind, value):
        value = value.astype(LOW)
        span = pl.ds(kind * HEAD_DIM, HEAD_DIM)
        out_ref[at, span] = value
        sum_ref[:, span] += jnp.sum(value.astype(FULL), 0, keepdims=True)

    dk_ref[...] = jnp.zeros_like(dk_ref)
    dv_ref[...] = jnp.zeros_like(dv_ref)
    for i in range(LEN // SPAN):
        low, high = key_range(i)
        at = pl.ds(i * SPAN, SPAN)
        span = pl.ds(low, high - low)
        query, keys, grad = q_ref[0, at, :], k_ref[0, span, :], g_ref[at, :]
        scores = masked(
            query, keys, col_ref[0, at, 0:1], row_ref[0, :, span], i * SPAN, low
        )
        probs = jnp.exp(scores - log_ref[0, at, 0:1])
        probs_grad = nt(grad, v_ref[0, span, :])
        inner = jnp.sum(probs * probs_grad, 1, keepdims=True)
        raw_grad = (probs * (probs_grad - inner) * HEAD_DIM ** (-0.5)).astype(LOW)
        dv_ref[span, :] += tn(probs.astype(LOW), grad)
        dk_ref[span, :] += tn(raw_grad, query)
        dq = nn(raw_grad, keys)
        put(at, 0, turn_features(dq, table_ref, at, -1.0))
    for i in range(LEN // SPAN):
        at = pl.ds(i * SPAN, SPAN)
        put(at, 1, turn_features(dk_ref[at, :], table_ref, at, -1.0))
        put(at, 2, dv_ref[at, :])


def attend_back(qkv, grad, logs, seg_col, seg_row, table):
    tiles, rows, _ = qkv.shape
    heads, seqs = tiles // 3, rows // LEN

    def part(kind):
        return pl.BlockSpec((1, LEN, HEAD_DIM), lambda h, s: (3 * h + kind, s, 0))

    return pl.pallas_call(
        attend_back_kernel,
        grid=(heads, seqs),
        in_specs=[
            part(0),
            part(1),
            part(2),
            pl.BlockSpec((LEN, HEAD_DIM), lambda h, s: (s, h)),
            pl.BlockSpec((1, LEN, 128), lambda h, s: (h, s, 0)),
            pl.BlockSpec((1, LEN, 128), lambda h, s: (s, 0, 0)),
            pl.BlockSpec((1, 1, LEN), lambda h, s: (s, 0, 0)),
            whole(table.shape),
        ],
        out_specs=[
            pl.BlockSpec((LEN, 3 * HEAD_DIM), lambda h, s: (s, h)),
            pl.BlockSpec((1, 3 * HEAD_DIM), lambda h, s: (0, h)),
        ],
        out_shape=[
            jax.ShapeDtypeStruct((rows, tiles * HEAD_DIM), LOW),
            jax.ShapeDtypeStruct((1, tiles * HEAD_DIM), FULL),
        ],
        scratch_shapes=[pltpu.VMEM((LEN, HEAD_DIM), FULL)] * 2,
        compiler_params=params(2),
        cost_estimate=CHEAP,
        name="attend_back",
    )(qkv, qkv, qkv, grad, logs, seg_col, seg_row, table)


def up_kernel(x_ref, near_ref, far_ref, b_ref, act_ref, slope_ref):
    rows = x_ref.shape[0]
    for m in range(rows // SPAN):
        at = pl.ds(m * SPAN, SPAN)
        value = nn2(x_ref, at, near_ref, far_ref) + b_ref[...]
        share = 0.5 * (1.0 + lax.erf(value * 0.5**0.5))
        act_ref[at, :] = (value * share).astype(LOW)
        bell = jnp.exp(value * value * -0.5) * 0.3989422804014327
        slope_ref[at, :] = (share + value * bell).astype(LOW)


def project_up(second, weight, bias):
    rows = second.shape[0]
    cols = weight[0].shape[1]
    tall = pl.BlockSpec((rows, SPAN), lambda j: (0, j))
    return pl.pallas_call(
        up_kernel,
        grid=(cols // SPAN,),
        in_specs=[
            whole(second.shape),
            *column_pair(weight, SPAN),
            pl.BlockSpec((1, SPAN), lambda j: (0, j)),
        ],
        out_specs=[tall, tall],
        out_shape=[jax.ShapeDtypeStruct((rows, cols), LOW)] * 2,
        compiler_params=params(),
        cost_estimate=CHEAP,
        name="project_up",
    )(second, *weight, bias.reshape(1, -1))


def row_pair(weight):
    rows, cols = weight[0].shape
    count = rows // SPAN
    return [
        pl.BlockSpec((SPAN, cols), lambda j, *_: (jnp.minimum(j, count - 1), 0)),
        pl.BlockSpec((SPAN, cols), lambda j, *_: (jnp.maximum(j - count, 0), 0)),
    ]


def either(near_ref, far_ref, count, body):
    j = pl.program_id(0)

    @pl.when(j < count)
    def _():
        body(near_ref)

    @pl.when(j >= count)
    def _():
        body(far_ref)


def back_kernel(places_ref, x_ref, near_ref, far_ref, out_ref, *, count):
    def body(w_ref):
        for m in range(x_ref.shape[0] // SPAN):
            at = pl.ds(m * SPAN, SPAN)
            out_ref[0, at, :] = nt(x_ref[at, :], w_ref[...]).astype(LOW)

    either(near_ref, far_ref, count, body)


def project_back(hidden, weight, places, parts):
    rows = hidden.shape[0]
    width = 2 * weight[0].shape[0]
    count = width // SPAN // 2
    return pl.pallas_call(
        functools.partial(back_kernel, count=count),
        grid_spec=pltpu.PrefetchScalarGridSpec(
            num_scalar_prefetch=1,
            grid=(2 * count,),
            in_specs=[whole(hidden.shape), *row_pair(weight)],
            out_specs=pl.BlockSpec((1, rows, SPAN), lambda j, t: (t[0, j], 0, t[1, j])),
        ),
        out_shape=jax.ShapeDtypeStruct((parts, rows, width // parts), LOW),
        compiler_params=params(),
        cost_estimate=CHEAP,
        name="project_back",
    )(places, hidden, *weight)


def plain_kernel(x_ref, near_ref, far_ref, out_ref):
    for m in range(x_ref.shape[0] // SPAN):
        at = pl.ds(m * SPAN, SPAN)
        out_ref[at, :] = nn2(x_ref, at, near_ref, far_ref).astype(LOW)


def slope_kernel(x_ref, near_ref, far_ref, slope_ref, out_ref, sum_ref):
    total = jnp.zeros(sum_ref.shape, FULL)
    for m in range(x_ref.shape[0] // SPAN):
        at = pl.ds(m * SPAN, SPAN)
        value = nn2(x_ref, at, near_ref, far_ref) * slope_ref[at, :].astype(FULL)
        value = value.astype(LOW)
        out_ref[at, :] = value
        total = total + jnp.sum(value.astype(FULL), 0, keepdims=True)
    sum_ref[...] = total


def attn_grads(grad, weight, cols):
    rows = grad.shape[0]
    return pl.pallas_call(
        plain_kernel,
        grid=(cols // SPAN,),
        in_specs=[whole(grad.shape), *column_pair(weight, SPAN)],
        out_specs=pl.BlockSpec((rows, SPAN), lambda j: (0, j)),
        out_shape=jax.ShapeDtypeStruct((rows, cols), LOW),
        compiler_params=params(),
        cost_estimate=CHEAP,
        name="attn_grads",
    )(grad, *weight)


def up_grads(grad, weight, slope):
    rows, cols = slope.shape
    skip = (weight[0].shape[1] - cols) // SPAN
    tall = pl.BlockSpec((rows, SPAN), lambda j: (0, j))
    return pl.pallas_call(
        slope_kernel,
        grid=(cols // SPAN,),
        in_specs=[whole(grad.shape), *column_pair(weight, SPAN, skip), tall],
        out_specs=[tall, pl.BlockSpec((1, SPAN), lambda j: (0, j))],
        out_shape=[jax.ShapeDtypeStruct((rows, cols), LOW), jax.ShapeDtypeStruct((1, cols), FULL)],
        compiler_params=params(),
        cost_estimate=CHEAP,
        name="up_grads",
    )(grad, *weight, slope)


def input_kernel(
    places_ref, qg_ref, ug_ref, qn_ref, qf_ref, un_ref, uf_ref, x_ref, mean_ref, inv_ref, par_ref,
    out_ref, sums_ref, row_ref, *, count
):
    @pl.when(pl.program_id(0) == 0)
    def _():
        row_ref[...] = jnp.zeros_like(row_ref)

    def body(w_refs):
        wq_ref, wu_ref = w_refs
        sums = [jnp.zeros((1, SPAN), FULL) for _ in range(4)]
        for m in range(qg_ref.shape[0] // SPAN):
            at = pl.ds(m * SPAN, SPAN)
            first_grad = nt(qg_ref[at, :], wq_ref[...])
            second_grad = nt(ug_ref[at, :], wu_ref[...])
            normed = (x_ref[at, :].astype(FULL) - mean_ref[at, 0:1]) * inv_ref[at, 0:1]
            total = first_grad * par_ref[0:1, :] + second_grad * par_ref[2:3, :]
            out_ref[0, at, :] = total.astype(LOW)
            for n, value in enumerate((first_grad * normed, first_grad, second_grad * normed, second_grad)):
                sums[n] = sums[n] + jnp.sum(value, 0, keepdims=True)
            for n, value in enumerate((total, total * normed)):
                row_ref[n, at, :] += sum(value[:, o : o + 128] for o in range(0, SPAN, 128))
        sums_ref[0] = jnp.concatenate(sums, 0)

    either((qn_ref, un_ref), (qf_ref, uf_ref), count, body)


def input_grads(qkv_grad, up_grad, qkv_weight, up_weight, x, mean, inv, par, places, parts):
    rows, width = qkv_grad.shape[0], x.shape[1]
    count = width // SPAN // 2
    return pl.pallas_call(
        functools.partial(input_kernel, count=count),
        grid_spec=pltpu.PrefetchScalarGridSpec(
            num_scalar_prefetch=1,
            grid=(2 * count,),
            in_specs=[
                whole(qkv_grad.shape),
                whole(up_grad.shape),
                *row_pair(qkv_weight),
                *row_pair(up_weight),
                pl.BlockSpec((rows, SPAN), lambda j, t: (0, j)),
                whole(mean.shape),
                whole(inv.shape),
                pl.BlockSpec((4, SPAN), lambda j, t: (0, j)),
            ],
            out_specs=[
                pl.BlockSpec((1, rows, SPAN), lambda j, t: (t[0, j], 0, t[1, j])),
                pl.BlockSpec((1, 4, SPAN), lambda j, t: (t[0, j], 0, t[1, j])),
                whole((2, rows, 128)),
            ],
        ),
        out_shape=[
            jax.ShapeDtypeStruct((parts, rows, width // parts), LOW),
            jax.ShapeDtypeStruct((parts, 4, width // parts), FULL),
            jax.ShapeDtypeStruct((2, rows, 128), FULL),
        ],
        compiler_params=params(),
        cost_estimate=CHEAP,
        name="input_grads",
    )(places, qkv_grad, up_grad, *qkv_weight, *up_weight, x, mean, inv, par)


def weight_kernel(a_ref, b_ref, near_ref, far_ref, *, count):
    value = tn(a_ref[...], b_ref[...]).astype(LOW)
    j = pl.program_id(0)

    @pl.when(j < count)
    def _():
        near_ref[...] = value

    @pl.when(j >= count)
    def _():
        far_ref[...] = value


def weight_grads(a, b):
    rows, width = a.shape
    cols = b.shape[1]
    count = width // SPAN // 2
    return pl.pallas_call(
        functools.partial(weight_kernel, count=count),
        grid=(2 * count,),
        in_specs=[pl.BlockSpec((rows, SPAN), lambda j: (0, j)), whole(b.shape)],
        out_specs=row_pair([jax.ShapeDtypeStruct((width // 2, cols), LOW)]),
        out_shape=[jax.ShapeDtypeStruct((width // 2, cols), LOW)] * 2,
        compiler_params=params(),
        cost_estimate=CHEAP,
        name="weight_grads",
    )(a, b)


def rotary_table():
    half = ROTARY // 2
    places = jnp.arange(LEN).astype(FULL)
    freqs = BASE ** (-(jnp.arange(half).astype(FULL) * 2.0) / ROTARY)
    angles = places[:, None] * freqs[None, :]
    cosine, sine = jnp.cos(angles), jnp.sin(angles)
    rest = 128 - ROTARY
    zeros = jnp.zeros_like(sine)
    pad = jnp.zeros((LEN, rest), FULL)
    return jnp.stack(
        [
            jnp.concatenate([cosine, cosine, pad + 1.0], 1),
            jnp.concatenate([-sine, zeros, pad], 1),
            jnp.concatenate([zeros, sine, pad], 1),
        ]
    )


def arrange_kernel(table_ref, *refs):
    out_ref = refs[-1]
    source = table_ref[0, pl.program_id(0)]
    for n, x_ref in enumerate(refs[:-1]):

        @pl.when(source == n)
        def _():
            out_ref[...] = x_ref[...]


def arranged(blocks, table, piece):
    rows = blocks[0].shape[0]
    count = table.shape[1]
    at = jnp.arange(count, dtype=jnp.int32)
    used = table[0][None, :] == jnp.arange(len(blocks), dtype=jnp.int32)[:, None]
    before = used[:, None, :] & (at[None, None, :] <= at[None, :, None])
    last = jnp.max(jnp.where(before, at[None, None, :], -1), 2, keepdims=True)
    spots = jnp.sum(jnp.where(last == at[None, None, :], table[1][None, None, :], 0), 2)
    table = jnp.concatenate([table, spots], 0)

    def spec(n):
        return pl.BlockSpec((rows, piece), lambda i, t: (0, t[2 + n, i]))

    return pl.pallas_call(
        arrange_kernel,
        grid_spec=pltpu.PrefetchScalarGridSpec(
            num_scalar_prefetch=1,
            grid=(count,),
            in_specs=[spec(n) for n in range(len(blocks))],
            out_specs=pl.BlockSpec((rows, piece), lambda i, t: (0, i)),
        ),
        out_shape=jax.ShapeDtypeStruct((rows, count * piece), blocks[0].dtype),
        compiler_params=params(),
        cost_estimate=CHEAP,
        name="arrange",
    )(table, *blocks)


def join_kernel(spot_ref, *refs, count, cuts):
    ins, outs = refs[:count], refs[count:]
    turn = len(cuts) > 0
    source = spot_ref[pl.program_id(0)]
    for n, x_ref in enumerate(ins):

        @pl.when(source == n)
        def _():
            if not turn:
                outs[0][...] = x_ref[...].astype(FULL)
            else:
                for out_ref, start in zip(outs, cuts):
                    for o in range(0, out_ref.shape[0], SPAN):
                        value = x_ref[:, start + o : start + o + SPAN].astype(FULL)
                        out_ref[o : o + SPAN, :] = value.T


def joined(pieces, spots, widths=()):
    piece, cols = pieces[0].shape
    count = len(pieces)
    cuts = [sum(widths[:n]) for n in range(len(widths))]
    if widths:
        specs = [pl.BlockSpec((w, piece), lambda h, t: (0, h)) for w in widths]
        shapes = [jax.ShapeDtypeStruct((w, piece * count), FULL) for w in widths]
    else:
        specs = [pl.BlockSpec((piece, cols), lambda h, t: (h, 0))]
        shapes = [jax.ShapeDtypeStruct((piece * count, cols), FULL)]
    return pl.pallas_call(
        functools.partial(join_kernel, count=count, cuts=cuts),
        grid_spec=pltpu.PrefetchScalarGridSpec(
            num_scalar_prefetch=1,
            grid=(count,),
            in_specs=[whole((piece, cols))] * count,
            out_specs=specs,
        ),
        out_shape=shapes,
        compiler_params=params(),
        cost_estimate=CHEAP,
        name="join",
    )(spots, *pieces)


def attach_kernel(x_ref, small_ref, out_ref):
    rows = x_ref.shape[0]
    out_ref[:rows, :] = x_ref[...]
    out_ref[rows:, :] = small_ref[...]


def attach(x, small):
    rows = x.shape[0] + small.shape[0]
    return pl.pallas_call(
        attach_kernel,
        in_specs=[pl.BlockSpec(memory_space=pltpu.VMEM)] * 2,
        out_specs=pl.BlockSpec(memory_space=pltpu.VMEM),
        out_shape=jax.ShapeDtypeStruct((rows, x.shape[1]), x.dtype),
        compiler_params=pltpu.CompilerParams(vmem_limit_bytes=SCOPED),
        cost_estimate=CHEAP,
        name="attach",
    )(x, small)


def swapped(v):
    return (v & 1) * 2 + (v >> 1)


class Order:
    def __init__(self):
        self.token = ()

    def gate(self, *xs):
        out = lax.optimization_barrier(tuple(xs) + self.token)[: len(xs)]
        return out[0] if len(xs) == 1 else out

    def wait(self, *xs):
        out = lax.optimization_barrier(tuple(xs) + self.token)[: len(xs)]
        self.token = tuple(jax.tree.leaves(out))
        return out[0] if len(xs) == 1 else out

    def run(self, function, first, *rest):
        out = function(self.gate(first), *rest)
        self.token = (out[0],) if isinstance(out, (tuple, list)) else (out,)
        return out


class Plan:
    def __init__(self, part):
        self.nd, self.nr, self.nc = (lax.axis_size(a) for a in ("dp", "row", "col"))
        self.d, self.r, self.c = (lax.axis_index(a) for a in ("dp", "row", "col"))
        self.part = part
        self.piece = part // self.nd
        self.ny = self.nr // 2
        spots = [(r, c) for r in range(self.nr) for c in range(self.nc)]
        self.pairs = [(r * self.nc + c, (r ^ swapped(c)) * self.nc + swapped(r)) for r, c in spots]
        self.plane_pairs = [(r * self.nc + c, (r ^ swapped(c)) * self.nc + c) for r, c in spots]
        self.line_pairs = [(r * self.nc + c, r * self.nc + (swapped(r) ^ c)) for r, c in spots]
        e = jnp.arange(2 * self.nd * self.ny, dtype=jnp.int32)
        k, step, y = e // (self.nd * self.ny), e // self.ny % self.nd, e % self.ny
        self.places = jnp.stack(
            [swapped(self.r ^ (2 * y + k)) ^ self.c, lax.rem(self.d - step + self.nd, self.nd)]
        ).astype(jnp.int32)

    def turn(self, x):
        return lax.ppermute(x, ("row", "col"), self.pairs)

    def turn_back(self, x):
        return lax.ppermute(x, ("row", "col"), [(b, a) for a, b in self.pairs])

    def turn_plane(self, x):
        return lax.ppermute(x, ("row", "col"), self.plane_pairs)

    def turn_line(self, x):
        return lax.ppermute(x, ("row", "col"), self.line_pairs)

    def flip(self, x):
        return lax.ppermute(x, "row", [(r, r ^ 1) for r in range(self.nr)])

    def hop_y(self, x):
        return lax.ppermute(x, "row", [(r, r ^ 2) for r in range(self.nr)])

    def hop_x(self, x, s):
        return lax.ppermute(x, "dp", [(d, (d + s) % self.nd) for d in range(self.nd)])

    def roll(self, x, s):
        return lax.ppermute(x, "col", [(i, (i + s) % self.nc) for i in range(self.nc)])

    def rolls(self, x):
        return self.roll(x, 1), self.roll(x, -1)

    def two_away(self, ahead, behind):
        return (
            lax.ppermute(ahead, "col", [(1, 2), (2, 3)]),
            lax.ppermute(behind, "col", [(2, 1), (1, 0)]),
        )

    def arrange(self, own, one, two):
        away = lax.rem(self.c - self.places[0] + self.nc, self.nc)
        right = jnp.where(self.c >= 2, 2, 4)
        table = jnp.stack([jnp.where(away == 2, right, away), self.places[1]])
        blocks = [own, one[0], two[0], one[1], two[1]]
        if self.piece % 128 == 0:
            return arranged(blocks, table, self.piece)
        blocks = jnp.stack(blocks)
        chunks = [
            lax.dynamic_slice(
                blocks, [table[0, i], 0, table[1, i] * self.piece], (1, own.shape[0], self.piece)
            )[0]
            for i in range(table.shape[1])
        ]
        return jnp.concatenate(chunks, -1)

    def spots(self, width):
        if self.piece == SPAN:
            return self.places, self.nc
        count = width // SPAN
        return jnp.stack([jnp.zeros(count, jnp.int32), jnp.arange(count, dtype=jnp.int32)]), 1

    def to_parts(self, value):
        if value.shape[0] == self.nc:
            return value
        parts = []
        for j in range(self.nc):
            x = self.r ^ swapped(self.c ^ j)
            pieces = []
            for h in range(self.nd):
                s = lax.rem(self.d - h + self.nd, self.nd)
                at = ((lax.rem(x, 2) * self.nd + s) * self.ny + x // 2) * self.piece
                pieces.append(lax.dynamic_slice_in_dim(value[0], at, self.piece, 1))
            parts.append(jnp.concatenate(pieces, -1))
        return jnp.stack(parts)

    def own_piece(self, block):
        return lax.dynamic_slice_in_dim(block, self.d * self.piece, self.piece, 0)

    def spread_one(self, own):
        return [self.hop_x(own, s) for s in range(1, self.nd)], self.hop_y(own)

    def spread_two(self, by_x, by_y):
        half = self.piece // 2
        return [
            (self.hop_y(x[:half]), self.hop_x(by_y[half:], s + 1)) for s, x in enumerate(by_x)
        ]

    def spread_end(self, own, by_x, by_y, both):
        rest = [own, by_y]
        for x, pair in zip(by_x, both):
            rest += [x, jnp.concatenate(pair, 0)]
        return jnp.concatenate(rest, 0), [self.flip(v) for v in rest]

    def collect_one(self, near, flipped):
        shape = (self.nd, self.ny, 2, self.piece // 2, near.shape[1])
        near = (near.astype(FULL) + flipped.astype(FULL)).astype(LOW).reshape(shape)
        by_x = [self.hop_x(near[s, :, 0], -s) for s in range(1, self.nd)]
        by_y = self.hop_y(near[:, 1, 1])
        return near, by_x, by_y

    def collect_two(self, near, by_x, by_y):
        low = total(near[0, :, 0], *by_x)
        high = total(near[:, 0, 1], by_y)
        return low, high, self.hop_y(low[1]), [self.hop_x(high[s], -s) for s in range(1, self.nd)]

    def collect_end(self, low, high, by_y, by_x):
        return jnp.concatenate([total(low[0], by_y), total(high[0], *by_x)], 0)

    def join(self, mine):
        return [self.hop_x(mine, s) for s in range(1, self.nd)]

    def join_end(self, mine, others, widths=()):
        places = jnp.arange(self.nd)
        spots = lax.rem(self.d - places + self.nd, self.nd).astype(jnp.int32)
        pieces = [mine, *others]
        if widths and self.piece % 128:
            whole_grad = joined(pieces, spots)[0].T
            return whole_grad[: widths[0]], whole_grad[widths[0] :]
        return joined(pieces, spots, widths)

    def pick(self, parts, offset):
        j = jnp.clip(self.c + offset, 0, self.nc - 1)
        return lax.dynamic_index_in_dim(parts, j, 0, False)

    def pick_around(self, parts, offset):
        j = lax.rem(self.c + offset + self.nc, self.nc)
        return lax.dynamic_index_in_dim(parts, j, 0, False)

    def sum_one(self, parts):
        return (
            lax.ppermute(self.pick(parts, 2), "col", [(0, 1), (1, 2)]),
            lax.ppermute(self.pick(parts, -2), "col", [(3, 2), (2, 1)]),
        )

    def sum_two(self, parts, moved):
        return (
            self.roll(total(self.pick_around(parts, 1), moved[0]), 1),
            self.roll(total(self.pick_around(parts, -1), moved[1]), -1),
        )


def total(*values):
    return sum(v.astype(FULL) for v in values).astype(LOW)


def split_exact(value):
    parts = []
    for _ in range(3):
        part = lax.reduce_precision(value, 8, 7)
        parts.append(part.astype(LOW))
        value = value - part
    return jnp.concatenate(parts, 0)


def local(
    tokens,
    segment_ids,
    norm1_gain,
    norm1_bias,
    norm2_gain,
    norm2_bias,
    qkv_weight,
    qkv_bias,
    out_weight,
    out_bias,
    up_weight,
    up_bias,
    down_weight,
    down_bias,
    cotangent,
):
    rows, part = tokens.shape
    plan, order = Plan(part), Order()
    width = part * plan.nc
    places, parts = plan.spots(width)
    qkv_cols = qkv_weight.shape[1]
    attn_cols = out_weight.shape[0]
    up_cols = up_weight.shape[1]

    turned_qkv = plan.turn(plan.own_piece(qkv_weight))
    small = split_exact(jnp.stack([norm1_gain, norm1_bias, norm2_gain, norm2_bias]))
    own = attach(tokens, jnp.concatenate([small, jnp.zeros((16 - small.shape[0], part), LOW)], 0))
    one = plan.rolls(own)
    rest = jnp.concatenate(
        [
            plan.own_piece(up_weight),
            plan.own_piece(out_weight.T),
            plan.own_piece(down_weight.T),
        ],
        1,
    )
    rest = plan.turn_plane(rest)
    biases = plan.turn(jnp.concatenate([qkv_bias, up_bias]))
    table = rotary_table()
    output_bias_grad = jnp.sum(cotangent, 0, dtype=FULL)
    turned_qkv, table, output_bias_grad = order.wait(turned_qkv, table, output_bias_grad)
    qkv_x, qkv_y = plan.spread_one(turned_qkv)
    biases, rest, *one = order.wait(biases, rest, *one)
    two = plan.two_away(*one)
    turned_up = plan.turn_line(rest[:, :up_cols])
    qkv_y, *qkv_x = order.wait(qkv_y, *qkv_x)
    qkv_both = order.wait(plan.spread_two(qkv_x, qkv_y))
    qkv_near, qkv_far = plan.spread_end(turned_qkv, qkv_x, qkv_y, qkv_both)
    turned_up, *two = order.wait(turned_up, *two)
    turned_back = plan.turn_line(order.gate(rest[:, up_cols:]))
    grad_one = plan.rolls(order.gate(cotangent))
    up_x, up_y = plan.spread_one(turned_up)
    segs = lax.ppermute(
        order.gate(segment_ids),
        ("row", "col"),
        [(r * plan.nc + c, c * plan.nc + r) for r in range(plan.nr) for c in range(plan.nc)],
    )
    x = order.run(plan.arrange, own, one, two)
    small = x[rows : rows + 12].astype(FULL)
    par = (small[0:4] + small[4:8]) + small[8:12]
    first, second, mean, inv = order.run(norms, x, par, rows)
    qkv_far, segs = order.wait(qkv_far, segs)
    seg_col = jnp.broadcast_to(segs[:, :, None], segs.shape + (128,))
    seg_row = segs[:, None, :]
    qkv_w = (qkv_near, jnp.concatenate(qkv_far, 0))
    qkv = order.run(project_qkv, first, qkv_w, biases[:qkv_cols], table)
    up_y, *up_x = order.wait(up_y, *up_x)
    up_both = plan.spread_two(up_x, up_y)
    attn, logs = order.run(attend, qkv, seg_col, seg_row)
    turned_back, *grad_one = order.wait(turned_back, *grad_one)
    back_x, back_y = plan.spread_one(turned_back)
    grad_two = plan.two_away(*grad_one)
    up_both = order.wait(up_both)
    up_near, up_far = plan.spread_end(turned_up, up_x, up_y, up_both)
    up_far = order.wait(up_far)
    up_w = (up_near, jnp.concatenate(up_far, 0))
    act, slope = order.run(project_up, second, up_w, biases[qkv_cols:])
    hidden = jnp.concatenate([attn, act], 1)
    back_y, *back_x = order.wait(back_y, *back_x)
    back_both = plan.spread_two(back_x, back_y)
    grad_two = order.wait(*grad_two)
    grad = order.run(plan.arrange, cotangent, grad_one, grad_two)
    back_both = order.wait(back_both)
    back_near, back_far = plan.spread_end(turned_back, back_x, back_y, back_both)

    back_g = order.run(weight_grads, grad, hidden)
    back_far = order.wait(back_far)
    back_w = (back_near, jnp.concatenate(back_far, 0))
    branch = plan.to_parts(order.run(project_back, hidden, back_w, places, parts))
    back_flip = plan.flip(order.gate(back_g[1]))
    branch_one = plan.sum_one(branch)
    attn_grad = order.run(attn_grads, grad, back_w, attn_cols)
    up_grad, up_bias_grad = order.run(up_grads, grad, back_w, slope)
    back_flip = order.wait(back_flip)
    back_c, back_x, back_y = plan.collect_one(back_g[0], back_flip)
    branch_one = order.wait(*branch_one)
    branch_two = plan.sum_two(branch, branch_one)
    up_g = order.run(weight_grads, second, up_grad)
    qkv_grad, qkv_bias_grad = order.run(
        attend_back, qkv, attn_grad, logs, seg_col, seg_row, table
    )
    back_y, *back_x = order.wait(back_y, *back_x)
    up_flip = plan.flip(order.gate(up_g[1]))
    back_low, back_high, back_y, back_x = plan.collect_two(back_c, back_x, back_y)
    qkv_g = order.run(weight_grads, first, qkv_grad)
    up_flip = order.wait(up_flip)
    up_c, up_x, up_y = plan.collect_one(up_g[0], up_flip)
    back_y, *back_x = order.wait(back_y, *back_x)
    turned_back = plan.turn_back(plan.collect_end(back_low, back_high, back_y, back_x))
    normed_grad, sums, row_sums = order.run(
        input_grads, qkv_grad, up_grad, qkv_w, up_w, x, mean, inv, par, places, parts
    )
    turned_back, *branch_two = order.wait(turned_back, *branch_two)
    back_joined = plan.join(turned_back)
    mine = plan.to_parts(normed_grad)
    mine_one = plan.sum_one(mine)
    qkv_flip = plan.flip(order.gate(qkv_g[1]))
    up_y, *up_x = order.wait(up_y, *up_x)
    up_low, up_high, up_y, up_x = plan.collect_two(up_c, up_x, up_y)
    mixed = plan.pick(branch, 0).astype(FULL) + sum(v.astype(FULL) for v in branch_two)
    mixed = (tokens.astype(FULL) + mixed + (out_bias + down_bias)).astype(LOW)
    mixed = order.wait(mixed)
    mine_one = order.wait(*mine_one)
    mine_two = plan.sum_two(mine, mine_one)
    up_y, *up_x = order.wait(up_y, *up_x)
    turned_up = plan.turn_back(plan.collect_end(up_low, up_high, up_y, up_x))
    qkv_flip = order.wait(qkv_flip)
    qkv_c, qkv_x, qkv_y = plan.collect_one(qkv_g[0], qkv_flip)
    qkv_y, *qkv_x = order.wait(qkv_y, *qkv_x)
    qkv_low, qkv_high, qkv_y, qkv_x = plan.collect_two(qkv_c, qkv_x, qkv_y)
    back_joined = order.wait(back_joined)
    out_g, down_g = plan.join_end(
        turned_back, back_joined, (attn_cols, turned_back.shape[1] - attn_cols)
    )
    qkv_y, *qkv_x = order.wait(qkv_y, *qkv_x)
    turned_qkv = plan.turn_back(plan.collect_end(qkv_low, qkv_high, qkv_y, qkv_x))
    sums = plan.to_parts(sums).reshape(plan.nc, 4 * part)
    row_sums = jnp.sum(row_sums, 2).reshape(-1)
    sums = jnp.concatenate([sums, jnp.broadcast_to(row_sums[None], (plan.nc, 2 * rows))], 1)
    sums_moved = [plan.roll(plan.pick_around(sums, s), s) for s in range(1, plan.nc)]
    turned_up, *mine_two = order.wait(turned_up, *mine_two)
    up_joined = plan.join(turned_up)
    sums_moved = order.wait(*sums_moved)
    sums = plan.pick(sums, 0) + sum(sums_moved)
    small = jnp.concatenate(
        [sums[: 4 * part], output_bias_grad, qkv_bias_grad[0], up_bias_grad[0]]
    )
    small_flip = order.wait(plan.flip(small))
    small = small + small_flip
    small_hop = plan.hop_y(small)
    grad_stats = sums[4 * part :].reshape(2, rows, 1)
    mine = plan.pick(mine, 0).astype(FULL) + sum(v.astype(FULL) for v in mine_two)
    mean, inv = mean[:, :1], inv[:, :1]
    own_normed = (tokens.astype(FULL) - mean) * inv
    input_grad = cotangent.astype(FULL) + inv * (
        mine - grad_stats[0] / width - own_normed * (grad_stats[1] / width)
    )
    input_grad = order.wait(input_grad)
    small = small + order.wait(small_hop)
    small_join = [plan.hop_x(small, s) for s in range(1, plan.nd)]
    turned_qkv = order.wait(turned_qkv)
    qkv_joined = plan.join(turned_qkv)
    small = small + sum(order.wait(small_join))
    bias_grads = plan.turn_back(small[5 * part :])
    up_joined = order.wait(up_joined)
    up_g = plan.join_end(turned_up, up_joined)[0]
    qkv_g = plan.join_end(turned_qkv, qkv_joined)[0]
    norm_sums = small[: 4 * part].reshape(4, part)
    output_bias_grad = small[4 * part : 5 * part]
    return (
        mixed,
        input_grad,
        norm_sums[0],
        norm_sums[1],
        norm_sums[2],
        norm_sums[3],
        qkv_g,
        bias_grads[:qkv_cols],
        out_g,
        output_bias_grad,
        up_g,
        bias_grads[qkv_cols:],
        down_g,
        output_bias_grad,
    )


def solution(mesh):
    in_specs = (
        P(("dp", "row"), "col"),
        P(("dp", "col"), None),
        P("col"),
        P("col"),
        P("col"),
        P("col"),
        P("col", "row"),
        P("row"),
        P("row", "col"),
        P("col"),
        P("col", "row"),
        P("row"),
        P("row", "col"),
        P("col"),
        P(("dp", "row"), "col"),
    )
    out_specs = (
        P(("dp", "row"), "col"),
        P(("dp", "row"), "col"),
        P("col"),
        P("col"),
        P("col"),
        P("col"),
        P("col", "row"),
        P("row"),
        P("row", "col"),
        P("col"),
        P("col", "row"),
        P("row"),
        P("row", "col"),
        P("col"),
    )
    return jax.shard_map(local, mesh=mesh, in_specs=in_specs, out_specs=out_specs, check_vma=False)
```

```python
import functools

import jax
import jax.numpy as jnp
from jax import lax
from jax.experimental import pallas as pl
from jax.experimental.pallas import tpu as pltpu
from jax.sharding import PartitionSpec as P

LEN = 1024
HEAD_DIM = 256
ROTARY = 64


EPS = 1e-05
BASE = 10000.0
LOW = jnp.bfloat16
FULL = jnp.float32


SCOPED = 48 * 2**20
SPAN = 256


def params(count=1):
    return pltpu.CompilerParams(
        dimension_semantics=("arbitrary",) * count, vmem_limit_bytes=SCOPED
    )


CHEAP = pl.CostEstimate(flops=10**8, bytes_accessed=10**5, transcendentals=0)


def nn(a, b):
    return jnp.dot(a, b, preferred_element_type=FULL)


def nt(a, b):
    return lax.dot_general(a, b, (((1,), (1,)), ((), ())), preferred_element_type=FULL)


def tn(a, b):
    return lax.dot_general(a, b, (((0,), (0,)), ((), ())), preferred_element_type=FULL)


def whole(shape):
    return pl.BlockSpec(shape, lambda *_: (0,) * len(shape))


def norm_kernel(x_ref, par_ref, first_ref, second_ref, mean_ref, inv_ref):
    x = x_ref[...].astype(FULL)
    width = x.shape[1]
    mean = jnp.sum(x, 1, keepdims=True) / width
    centred = x - mean
    variance = jnp.sum(centred * centred, 1, keepdims=True) / width
    inv = lax.rsqrt(variance + EPS)
    normed = centred * inv
    first_ref[...] = (normed * par_ref[0:1, :] + par_ref[1:2, :]).astype(LOW)
    second_ref[...] = (normed * par_ref[2:3, :] + par_ref[3:4, :]).astype(LOW)
    mean_ref[...] = jnp.broadcast_to(mean, mean_ref.shape)
    inv_ref[...] = jnp.broadcast_to(inv, inv_ref.shape)


def norms(x, par, rows):
    width = x.shape[1]
    tile = 128
    wide = pl.BlockSpec((tile, width), lambda i: (i, 0))
    thin = pl.BlockSpec((tile, 128), lambda i: (i, 0))
    return pl.pallas_call(
        norm_kernel,
        grid=(rows // tile,),
        in_specs=[wide, whole(par.shape)],
        out_specs=[wide, wide, thin, thin],
        out_shape=[jax.ShapeDtypeStruct((rows, width), LOW)] * 2
        + [jax.ShapeDtypeStruct((rows, 128), FULL)] * 2,
        compiler_params=params(),
        cost_estimate=CHEAP,
        name="norms",
    )(x, par)


def turn_features(value, table_ref, at, sign):
    half = ROTARY // 2
    head = value[:, :128]
    cosine = table_ref[0, at, :]
    down = table_ref[1, at, :] * sign
    up = table_ref[2, at, :] * sign
    head = head * cosine + pltpu.roll(head, 128 - half, 1) * down + pltpu.roll(head, half, 1) * up
    return jnp.concatenate([head, value[:, 128:]], 1)


def nn2(x_ref, at, near_ref, far_ref):
    half = near_ref.shape[0]
    return nn(x_ref[at, :half], near_ref[...]) + nn(x_ref[at, half:], far_ref[...])


def column_pair(weight, cols, skip=0):
    rows = weight[0].shape[0]
    return [pl.BlockSpec((rows, cols), lambda j: (0, j + skip))] * 2


def qkv_kernel(x_ref, near_ref, far_ref, b_ref, table_ref, out_ref):
    rows = x_ref.shape[0]
    kind = lax.rem(pl.program_id(0), 3)
    for m in range(rows // SPAN):
        at = pl.ds(m * SPAN, SPAN)
        place = pl.ds(m * SPAN % LEN, SPAN)
        value = nn2(x_ref, at, near_ref, far_ref) + b_ref[...]
        turned = turn_features(value, table_ref, place, 1.0)
        out_ref[0, at, :] = jnp.where(kind == 2, value, turned).astype(LOW)


def project_qkv(first, weight, bias, table):
    rows = first.shape[0]
    tiles = weight[0].shape[1] // HEAD_DIM
    return pl.pallas_call(
        qkv_kernel,
        grid=(tiles,),
        in_specs=[
            whole(first.shape),
            *column_pair(weight, HEAD_DIM),
            pl.BlockSpec((1, HEAD_DIM), lambda j: (0, j)),
            whole(table.shape),
        ],
        out_specs=pl.BlockSpec((1, rows, HEAD_DIM), lambda j: (j, 0, 0)),
        out_shape=jax.ShapeDtypeStruct((tiles, rows, HEAD_DIM), LOW),
        compiler_params=params(),
        cost_estimate=CHEAP,
        name="project_qkv",
    )(first, *weight, bias.reshape(1, -1), table)


def key_range(i):
    low = max(0, (i * SPAN - 511) // SPAN)
    return low * SPAN, (i + 1) * SPAN


def masked(query, keys, seg_col, seg_row, start, low):
    raw = nt(query, keys) * HEAD_DIM ** (-0.5)
    shape = raw.shape
    q_at = lax.broadcasted_iota(jnp.int32, shape, 0) + (start - low)
    k_at = lax.broadcasted_iota(jnp.int32, shape, 1)
    return jnp.where((q_at >= k_at) & (seg_col == seg_row), raw, -1e30)


def attend_kernel(q_ref, k_ref, v_ref, col_ref, row_ref, out_ref, log_ref):
    for i in range(LEN // SPAN):
        low, high = key_range(i)
        at = pl.ds(i * SPAN, SPAN)
        span = pl.ds(low, high - low)
        scores = masked(
            q_ref[0, at, :], k_ref[0, span, :], col_ref[0, at, 0:1], row_ref[0, :, span], i * SPAN, low
        )
        peak = jnp.max(scores, 1, keepdims=True)
        expos = jnp.exp(scores - peak)
        total = jnp.sum(expos, 1, keepdims=True)
        probs = (expos * (1.0 / total)).astype(LOW)
        out_ref[at, :] = nn(probs, v_ref[0, span, :]).astype(LOW)
        log_ref[0, at, :] = jnp.broadcast_to(peak + jnp.log(total), (SPAN, 128))


def attend(qkv, seg_col, seg_row):
    tiles, rows, _ = qkv.shape
    heads, seqs = tiles // 3, rows // LEN

    def part(kind):
        return pl.BlockSpec((1, LEN, HEAD_DIM), lambda h, s: (3 * h + kind, s, 0))

    return pl.pallas_call(
        attend_kernel,
        grid=(heads, seqs),
        in_specs=[
            part(0),
            part(1),
            part(2),
            pl.BlockSpec((1, LEN, 128), lambda h, s: (s, 0, 0)),
            pl.BlockSpec((1, 1, LEN), lambda h, s: (s, 0, 0)),
        ],
        out_specs=[
            pl.BlockSpec((LEN, HEAD_DIM), lambda h, s: (s, h)),
            pl.BlockSpec((1, LEN, 128), lambda h, s: (h, s, 0)),
        ],
        out_shape=[
            jax.ShapeDtypeStruct((rows, heads * HEAD_DIM), LOW),
            jax.ShapeDtypeStruct((heads, rows, 128), FULL),
        ],
        compiler_params=params(2),
        cost_estimate=CHEAP,
        name="attend",
    )(qkv, qkv, qkv, seg_col, seg_row)


def attend_back_kernel(
    q_ref, k_ref, v_ref, g_ref, log_ref, col_ref, row_ref, table_ref, out_ref, sum_ref, dk_ref, dv_ref
):
    @pl.when(pl.program_id(1) == 0)
    def _():
        sum_ref[...] = jnp.zeros_like(sum_ref)

    def put(at, kind, value):
        value = value.astype(LOW)
        span = pl.ds(kind * HEAD_DIM, HEAD_DIM)
        out_ref[at, span] = value
        sum_ref[:, span] += jnp.sum(value.astype(FULL), 0, keepdims=True)

    dk_ref[...] = jnp.zeros_like(dk_ref)
    dv_ref[...] = jnp.zeros_like(dv_ref)
    for i in range(LEN // SPAN):
        low, high = key_range(i)
        at = pl.ds(i * SPAN, SPAN)
        span = pl.ds(low, high - low)
        query, keys, grad = q_ref[0, at, :], k_ref[0, span, :], g_ref[at, :]
        scores = masked(
            query, keys, col_ref[0, at, 0:1], row_ref[0, :, span], i * SPAN, low
        )
        probs = jnp.exp(scores - log_ref[0, at, 0:1])
        probs_grad = nt(grad, v_ref[0, span, :])
        inner = jnp.sum(probs * probs_grad, 1, keepdims=True)
        raw_grad = (probs * (probs_grad - inner) * HEAD_DIM ** (-0.5)).astype(LOW)
        dv_ref[span, :] += tn(probs.astype(LOW), grad)
        dk_ref[span, :] += tn(raw_grad, query)
        dq = nn(raw_grad, keys)
        put(at, 0, turn_features(dq, table_ref, at, -1.0))
    for i in range(LEN // SPAN):
        at = pl.ds(i * SPAN, SPAN)
        put(at, 1, turn_features(dk_ref[at, :], table_ref, at, -1.0))
        put(at, 2, dv_ref[at, :])


def attend_back(qkv, grad, logs, seg_col, seg_row, table):
    tiles, rows, _ = qkv.shape
    heads, seqs = tiles // 3, rows // LEN

    def part(kind):
        return pl.BlockSpec((1, LEN, HEAD_DIM), lambda h, s: (3 * h + kind, s, 0))

    return pl.pallas_call(
        attend_back_kernel,
        grid=(heads, seqs),
        in_specs=[
            part(0),
            part(1),
            part(2),
            pl.BlockSpec((LEN, HEAD_DIM), lambda h, s: (s, h)),
            pl.BlockSpec((1, LEN, 128), lambda h, s: (h, s, 0)),
            pl.BlockSpec((1, LEN, 128), lambda h, s: (s, 0, 0)),
            pl.BlockSpec((1, 1, LEN), lambda h, s: (s, 0, 0)),
            whole(table.shape),
        ],
        out_specs=[
            pl.BlockSpec((LEN, 3 * HEAD_DIM), lambda h, s: (s, h)),
            pl.BlockSpec((1, 3 * HEAD_DIM), lambda h, s: (0, h)),
        ],
        out_shape=[
            jax.ShapeDtypeStruct((rows, tiles * HEAD_DIM), LOW),
            jax.ShapeDtypeStruct((1, tiles * HEAD_DIM), FULL),
        ],
        scratch_shapes=[pltpu.VMEM((LEN, HEAD_DIM), FULL)] * 2,
        compiler_params=params(2),
        cost_estimate=CHEAP,
        name="attend_back",
    )(qkv, qkv, qkv, grad, logs, seg_col, seg_row, table)


def up_kernel(x_ref, near_ref, far_ref, b_ref, act_ref, slope_ref):
    rows = x_ref.shape[0]
    for m in range(rows // SPAN):
        at = pl.ds(m * SPAN, SPAN)
        value = nn2(x_ref, at, near_ref, far_ref) + b_ref[...]
        share = 0.5 * (1.0 + lax.erf(value * 0.5**0.5))
        act_ref[at, :] = (value * share).astype(LOW)
        bell = jnp.exp(value * value * -0.5) * 0.3989422804014327
        slope_ref[at, :] = (share + value * bell).astype(LOW)


def project_up(second, weight, bias):
    rows = second.shape[0]
    cols = weight[0].shape[1]
    tall = pl.BlockSpec((rows, SPAN), lambda j: (0, j))
    return pl.pallas_call(
        up_kernel,
        grid=(cols // SPAN,),
        in_specs=[
            whole(second.shape),
            *column_pair(weight, SPAN),
            pl.BlockSpec((1, SPAN), lambda j: (0, j)),
        ],
        out_specs=[tall, tall],
        out_shape=[jax.ShapeDtypeStruct((rows, cols), LOW)] * 2,
        compiler_params=params(),
        cost_estimate=CHEAP,
        name="project_up",
    )(second, *weight, bias.reshape(1, -1))


def row_pair(weight, row=lambda j, t: t[0, j]):
    rows, cols = weight[0].shape
    count = rows // SPAN
    return [
        pl.BlockSpec((SPAN, cols), lambda j, t: (jnp.minimum(row(j, t), count - 1), 0)),
        pl.BlockSpec((SPAN, cols), lambda j, t: (jnp.maximum(row(j, t) - count, 0), 0)),
    ]


def either(place, near_ref, far_ref, count, body):
    @pl.when(place < count)
    def _():
        body(near_ref)

    @pl.when(place >= count)
    def _():
        body(far_ref)


def back_kernel(tiles_ref, x_ref, near_ref, far_ref, out_ref, *, count):
    def body(w_ref):
        for m in range(x_ref.shape[0] // SPAN):
            at = pl.ds(m * SPAN, SPAN)
            out_ref[0, at, :] = nt(x_ref[at, :], w_ref[...]).astype(LOW)

    either(tiles_ref[0, pl.program_id(0)], near_ref, far_ref, count, body)


def project_back(hidden, weight, tiles, parts, part):
    rows = hidden.shape[0]
    return pl.pallas_call(
        functools.partial(back_kernel, count=weight[0].shape[0] // SPAN),
        grid_spec=pltpu.PrefetchScalarGridSpec(
            num_scalar_prefetch=1,
            grid=(tiles.shape[1],),
            in_specs=[whole(hidden.shape), *row_pair(weight)],
            out_specs=pl.BlockSpec((1, rows, SPAN), lambda j, t: (t[1, j], 0, t[2, j])),
        ),
        out_shape=jax.ShapeDtypeStruct((parts, rows, part), LOW),
        compiler_params=params(),
        cost_estimate=CHEAP,
        name="project_back",
    )(tiles, hidden, *weight)


def plain_kernel(x_ref, near_ref, far_ref, out_ref):
    for m in range(x_ref.shape[0] // SPAN):
        at = pl.ds(m * SPAN, SPAN)
        out_ref[at, :] = nn2(x_ref, at, near_ref, far_ref).astype(LOW)


def slope_kernel(x_ref, near_ref, far_ref, slope_ref, out_ref, sum_ref):
    total = jnp.zeros(sum_ref.shape, FULL)
    for m in range(x_ref.shape[0] // SPAN):
        at = pl.ds(m * SPAN, SPAN)
        value = nn2(x_ref, at, near_ref, far_ref) * slope_ref[at, :].astype(FULL)
        value = value.astype(LOW)
        out_ref[at, :] = value
        total = total + jnp.sum(value.astype(FULL), 0, keepdims=True)
    sum_ref[...] = total


def attn_grads(grad, weight, cols):
    rows = grad.shape[0]
    return pl.pallas_call(
        plain_kernel,
        grid=(cols // SPAN,),
        in_specs=[whole(grad.shape), *column_pair(weight, SPAN)],
        out_specs=pl.BlockSpec((rows, SPAN), lambda j: (0, j)),
        out_shape=jax.ShapeDtypeStruct((rows, cols), LOW),
        compiler_params=params(),
        cost_estimate=CHEAP,
        name="attn_grads",
    )(grad, *weight)


def up_grads(grad, weight, slope):
    rows, cols = slope.shape
    skip = (weight[0].shape[1] - cols) // SPAN
    tall = pl.BlockSpec((rows, SPAN), lambda j: (0, j))
    return pl.pallas_call(
        slope_kernel,
        grid=(cols // SPAN,),
        in_specs=[whole(grad.shape), *column_pair(weight, SPAN, skip), tall],
        out_specs=[tall, pl.BlockSpec((1, SPAN), lambda j: (0, j))],
        out_shape=[jax.ShapeDtypeStruct((rows, cols), LOW), jax.ShapeDtypeStruct((1, cols), FULL)],
        compiler_params=params(),
        cost_estimate=CHEAP,
        name="up_grads",
    )(grad, *weight, slope)


def input_kernel(
    tiles_ref, qg_ref, ug_ref, qn_ref, qf_ref, un_ref, uf_ref, x_ref, mean_ref, inv_ref, par_ref,
    out_ref, sums_ref, row_ref, *, count
):
    @pl.when(pl.program_id(0) == 0)
    def _():
        row_ref[...] = jnp.zeros_like(row_ref)

    def body(w_refs):
        wq_ref, wu_ref = w_refs
        sums = [jnp.zeros((1, SPAN), FULL) for _ in range(4)]
        for m in range(qg_ref.shape[0] // SPAN):
            at = pl.ds(m * SPAN, SPAN)
            first_grad = nt(qg_ref[at, :], wq_ref[...])
            second_grad = nt(ug_ref[at, :], wu_ref[...])
            normed = (x_ref[at, :].astype(FULL) - mean_ref[at, 0:1]) * inv_ref[at, 0:1]
            total = first_grad * par_ref[0:1, :] + second_grad * par_ref[2:3, :]
            out_ref[0, at, :] = total.astype(LOW)
            for n, value in enumerate((first_grad * normed, first_grad, second_grad * normed, second_grad)):
                sums[n] = sums[n] + jnp.sum(value, 0, keepdims=True)
            for n, value in enumerate((total, total * normed)):
                row_ref[n, at, :] += sum(value[:, o : o + 128] for o in range(0, SPAN, 128))
        sums_ref[0] = jnp.concatenate(sums, 0)

    either(tiles_ref[0, pl.program_id(0)], (qn_ref, un_ref), (qf_ref, uf_ref), count, body)


def input_grads(qkv_grad, up_grad, qkv_weight, up_weight, x, mean, inv, par, tiles, parts, part):
    rows = qkv_grad.shape[0]
    return pl.pallas_call(
        functools.partial(input_kernel, count=qkv_weight[0].shape[0] // SPAN),
        grid_spec=pltpu.PrefetchScalarGridSpec(
            num_scalar_prefetch=1,
            grid=(tiles.shape[1],),
            in_specs=[
                whole(qkv_grad.shape),
                whole(up_grad.shape),
                *row_pair(qkv_weight),
                *row_pair(up_weight),
                pl.BlockSpec((rows, SPAN), lambda j, t: (0, t[0, j])),
                whole(mean.shape),
                whole(inv.shape),
                pl.BlockSpec((4, SPAN), lambda j, t: (0, t[0, j])),
            ],
            out_specs=[
                pl.BlockSpec((1, rows, SPAN), lambda j, t: (t[1, j], 0, t[2, j])),
                pl.BlockSpec((1, 4, SPAN), lambda j, t: (t[1, j], 0, t[2, j])),
                whole((2, rows, 128)),
            ],
        ),
        out_shape=[
            jax.ShapeDtypeStruct((parts, rows, part), LOW),
            jax.ShapeDtypeStruct((parts, 4, part), FULL),
            jax.ShapeDtypeStruct((2, rows, 128), FULL),
        ],
        compiler_params=params(),
        cost_estimate=CHEAP,
        name="input_grads",
    )(tiles, qkv_grad, up_grad, *qkv_weight, *up_weight, x, mean, inv, par)


def weight_kernel(spots_ref, a_ref, b_ref, out_ref):
    out_ref[...] = tn(a_ref[...], b_ref[...]).astype(LOW)


def weight_grads(a, b, spots):
    rows, width = a.shape
    cols = b.shape[1]
    return pl.pallas_call(
        weight_kernel,
        grid_spec=pltpu.PrefetchScalarGridSpec(
            num_scalar_prefetch=1,
            grid=(width // SPAN,),
            in_specs=[pl.BlockSpec((rows, SPAN), lambda j, t: (0, j)), whole(b.shape)],
            out_specs=pl.BlockSpec((SPAN, cols), lambda j, t: (t[j], 0)),
        ),
        out_shape=jax.ShapeDtypeStruct((width, cols), LOW),
        compiler_params=params(),
        cost_estimate=CHEAP,
        name="weight_grads",
    )(spots, a, b)


def halves_kernel(a_ref, b_ref, near_ref, far_ref, *, count):
    value = tn(a_ref[...], b_ref[...]).astype(LOW)
    j = pl.program_id(0)

    @pl.when(j < count)
    def _():
        near_ref[...] = value

    @pl.when(j >= count)
    def _():
        far_ref[...] = value


def weight_halves(a, b):
    rows, width = a.shape
    cols = b.shape[1]
    count = width // SPAN // 2
    return pl.pallas_call(
        functools.partial(halves_kernel, count=count),
        grid=(2 * count,),
        in_specs=[pl.BlockSpec((rows, SPAN), lambda j: (0, j)), whole(b.shape)],
        out_specs=[
            pl.BlockSpec((SPAN, cols), lambda j: (jnp.minimum(j, count - 1), 0)),
            pl.BlockSpec((SPAN, cols), lambda j: (jnp.maximum(j - count, 0), 0)),
        ],
        out_shape=[jax.ShapeDtypeStruct((width // 2, cols), LOW)] * 2,
        compiler_params=params(),
        cost_estimate=CHEAP,
        name="weight_halves",
    )(a, b)


def reorder_kernel(spots_ref, x_ref, near_ref, far_ref):
    half = pl.num_programs(0) // 2

    @pl.when(pl.program_id(0) < half)
    def _():
        near_ref[...] = x_ref[...]

    @pl.when(pl.program_id(0) >= half)
    def _():
        far_ref[...] = x_ref[...]


def reordered(x, spots):
    rows, cols = x.shape
    count = rows // SPAN
    return pl.pallas_call(
        reorder_kernel,
        grid_spec=pltpu.PrefetchScalarGridSpec(
            num_scalar_prefetch=1,
            grid=(count,),
            in_specs=[pl.BlockSpec((SPAN, cols), lambda j, t: (t[j], 0))],
            out_specs=row_pair([jax.ShapeDtypeStruct((rows // 2, cols), LOW)], lambda j, t: j),
        ),
        out_shape=[jax.ShapeDtypeStruct((rows // 2, cols), LOW)] * 2,
        compiler_params=params(),
        cost_estimate=CHEAP,
        name="reorder",
    )(spots, x)


def rotary_table():
    half = ROTARY // 2
    places = jnp.arange(LEN).astype(FULL)
    freqs = BASE ** (-(jnp.arange(half).astype(FULL) * 2.0) / ROTARY)
    angles = places[:, None] * freqs[None, :]
    cosine, sine = jnp.cos(angles), jnp.sin(angles)
    rest = 128 - ROTARY
    zeros = jnp.zeros_like(sine)
    pad = jnp.zeros((LEN, rest), FULL)
    return jnp.stack(
        [
            jnp.concatenate([cosine, cosine, pad + 1.0], 1),
            jnp.concatenate([-sine, zeros, pad], 1),
            jnp.concatenate([zeros, sine, pad], 1),
        ]
    )


def arrange_kernel(table_ref, *refs):
    out_ref = refs[-1]
    source = table_ref[0, pl.program_id(0)]
    for n, x_ref in enumerate(refs[:-1]):

        @pl.when(source == n)
        def _():
            out_ref[...] = x_ref[...]


def arranged(blocks, table, piece):
    rows = blocks[0].shape[0]
    count = table.shape[1]
    at = jnp.arange(count, dtype=jnp.int32)
    used = table[0][None, :] == jnp.arange(len(blocks), dtype=jnp.int32)[:, None]
    before = used[:, None, :] & (at[None, None, :] <= at[None, :, None])
    last = jnp.max(jnp.where(before, at[None, None, :], -1), 2, keepdims=True)
    spots = jnp.sum(jnp.where(last == at[None, None, :], table[1][None, None, :], 0), 2)
    table = jnp.concatenate([table, spots], 0)

    def spec(n):
        return pl.BlockSpec((rows, piece), lambda i, t: (0, t[2 + n, i]))

    return pl.pallas_call(
        arrange_kernel,
        grid_spec=pltpu.PrefetchScalarGridSpec(
            num_scalar_prefetch=1,
            grid=(count,),
            in_specs=[spec(n) for n in range(len(blocks))],
            out_specs=pl.BlockSpec((rows, piece), lambda i, t: (0, i)),
        ),
        out_shape=jax.ShapeDtypeStruct((rows, count * piece), blocks[0].dtype),
        compiler_params=params(),
        cost_estimate=CHEAP,
        name="arrange",
    )(table, *blocks)


def join_kernel(spot_ref, *refs, count, cuts, turn):
    ins, outs = refs[:count], refs[count:]
    source = spot_ref[pl.program_id(0)]
    for n, x_ref in enumerate(ins):

        @pl.when(source == n)
        def _():
            for out_ref, start in zip(outs, cuts):
                if not turn:
                    out_ref[...] = x_ref[:, start : start + out_ref.shape[1]].astype(FULL)
                    continue
                for o in range(0, out_ref.shape[0], SPAN):
                    value = x_ref[:, start + o : start + o + SPAN].astype(FULL)
                    out_ref[o : o + SPAN, :] = value.T


def joined(pieces, spots, widths, turn):
    piece, cols = pieces[0].shape
    count = len(pieces)
    cuts = [sum(widths[:n]) for n in range(len(widths))]
    if turn:
        specs = [pl.BlockSpec((w, piece), lambda h, t: (0, h)) for w in widths]
        shapes = [jax.ShapeDtypeStruct((w, piece * count), FULL) for w in widths]
    else:
        specs = [pl.BlockSpec((piece, w), lambda h, t: (h, 0)) for w in widths]
        shapes = [jax.ShapeDtypeStruct((piece * count, w), FULL) for w in widths]
    return pl.pallas_call(
        functools.partial(join_kernel, count=count, cuts=cuts, turn=turn),
        grid_spec=pltpu.PrefetchScalarGridSpec(
            num_scalar_prefetch=1,
            grid=(count,),
            in_specs=[whole((piece, cols))] * count,
            out_specs=specs,
        ),
        out_shape=shapes,
        compiler_params=params(),
        cost_estimate=CHEAP,
        name="join",
    )(spots, *pieces)


def attach_kernel(x_ref, small_ref, out_ref):
    rows = x_ref.shape[0]
    out_ref[:rows, :] = x_ref[...]
    out_ref[rows:, :] = small_ref[...]


def attach(x, small):
    rows = x.shape[0] + small.shape[0]
    return pl.pallas_call(
        attach_kernel,
        in_specs=[pl.BlockSpec(memory_space=pltpu.VMEM)] * 2,
        out_specs=pl.BlockSpec(memory_space=pltpu.VMEM),
        out_shape=jax.ShapeDtypeStruct((rows, x.shape[1]), x.dtype),
        compiler_params=pltpu.CompilerParams(vmem_limit_bytes=SCOPED),
        cost_estimate=CHEAP,
        name="attach",
    )(x, small)


def swapped(v):
    return (v & 1) * 2 + (v >> 1)


def mixed_bits(v):
    return ((v & 1) ^ (v >> 1)) * 2 + (v >> 1)


class Order:
    def __init__(self):
        self.token, self.needs = (), ()

    def gate(self, *xs):
        out = lax.optimization_barrier(tuple(xs) + self.token)[: len(xs)]
        return out[0] if len(xs) == 1 else out

    def wait(self, *xs):
        out = self.gate(xs)
        self.token = tuple(jax.tree.leaves(out))
        return out[0] if len(xs) == 1 else out

    def need(self, *xs):
        self.needs += tuple(jax.tree.leaves(xs))

    def run(self, function, first, *rest):
        first = lax.optimization_barrier((first,) + self.token + self.needs)[0]
        out = function(first, *rest)
        self.token, self.needs = (out[0],) if isinstance(out, (tuple, list)) else (out,), ()
        return out


class Plan:
    def __init__(self, part):
        self.nd, self.nr, self.nc = (lax.axis_size(a) for a in ("dp", "row", "col"))
        self.d, self.r, self.c = (lax.axis_index(a) for a in ("dp", "row", "col"))
        self.part = part
        self.piece = part // self.nd
        self.ny = self.nr // 2
        spots = [(r, c) for r in range(self.nr) for c in range(self.nc)]
        goal = {(r, c): -r % 4 ^ swapped(c) for r, c in spots}
        self.pairs = [(r * self.nc + c, goal[r, c] * self.nc + swapped(r)) for r, c in spots]
        self.plane_pairs = [(r * self.nc + c, goal[r, c] * self.nc + c) for r, c in spots]
        self.line_pairs = [(goal[r, c] * self.nc + c, goal[r, c] * self.nc + swapped(r)) for r, c in spots]
        e = jnp.arange(2 * self.nd * self.ny, dtype=jnp.int32)
        self.straight = jnp.arange(part * self.nc // SPAN, dtype=jnp.int32)
        k, step, y = e // (self.nd * self.ny), e // self.ny % self.nd, e % self.ny
        self.places = jnp.stack(
            [swapped(self.r ^ (2 * y + k) ^ mixed_bits(self.c)), lax.rem(self.d - step + self.nd, self.nd)]
        ).astype(jnp.int32)
        self.blocks = (self.places[1] * self.nr + (self.r ^ (2 * y + k))).astype(jnp.int32)

    def move(self, x, pairs):
        moved = lax.ppermute(x, ("row", "col"), [(a, b) for a, b in pairs if a != b])
        here = self.r * self.nc + self.c
        stays = [here == a for a, b in pairs if a == b]

        def settle(moved, cut=lambda v: v):
            if not stays:
                return cut(moved)
            return jnp.where(functools.reduce(jnp.logical_or, stays), cut(x), cut(moved))

        return moved, settle

    def turn(self, x):
        return self.move(x, self.pairs)

    def turn_back(self, x):
        return self.move(x, [(b, a) for a, b in self.pairs])

    def turn_plane(self, x):
        return self.move(x, self.plane_pairs)

    def turn_line(self, x):
        return self.move(x, self.line_pairs)

    def cross(self, x):
        spots = [(r, c) for r in range(self.nr) for c in range(self.nc)]
        return self.move(x, [(r * self.nc + c, c * self.nc + swapped(r)) for r, c in spots])

    def gather_plane(self, own):
        value = lax.all_gather(own, ("dp", "row"), axis=0, tiled=True)
        if self.piece == SPAN:
            return value

        return self.chunks_of(value, self.blocks)

    def chunks_of(self, value, order):
        return jnp.concatenate(
            [
                lax.dynamic_slice_in_dim(value, order[i] * self.piece, self.piece, 0)
                for i in range(order.shape[0])
            ],
            0,
        )

    def plane_order(self):
        return self.blocks if self.piece == SPAN else self.straight

    def flip(self, x):
        return lax.ppermute(x, "row", [(r, r ^ 1) for r in range(self.nr)])

    def hop_y(self, x):
        return lax.ppermute(x, "row", [(r, r ^ 2) for r in range(self.nr)])

    def hop_x(self, x, s):
        return lax.ppermute(x, "dp", [(d, (d + s) % self.nd) for d in range(self.nd)])

    def roll(self, x, s):
        return lax.ppermute(x, "col", [(i, (i + s) % self.nc) for i in range(self.nc)])

    def rolls(self, x):
        return self.roll(x, 1), self.roll(x, -1)

    def two_away(self, ahead, behind):
        return (
            lax.ppermute(ahead, "col", [(1, 2), (2, 3)]),
            lax.ppermute(behind, "col", [(2, 1), (1, 0)]),
        )

    def arrange(self, own, one, two):
        away = lax.rem(self.c - self.places[0] + self.nc, self.nc)
        right = jnp.where(self.c >= 2, 2, 4)
        table = jnp.stack([jnp.where(away == 2, right, away), self.places[1]])
        blocks = [own, one[0], two[0], one[1], two[1]]
        if self.piece % 128 == 0:
            return arranged(blocks, table, self.piece)
        blocks = jnp.stack(blocks)
        chunks = [
            lax.dynamic_slice(
                blocks, [table[0, i], 0, table[1, i] * self.piece], (1, own.shape[0], self.piece)
            )[0]
            for i in range(table.shape[1])
        ]
        return jnp.concatenate(chunks, -1)

    def tiles(self):
        if self.piece != SPAN:
            e = self.straight
            return None, jnp.stack([e, 0 * e, e])
        far = jnp.array([2, 0, 1, 3], jnp.int32)
        far, step = jnp.repeat(far, self.nd), jnp.tile(jnp.arange(self.nd, dtype=jnp.int32), 4)
        q = self.r ^ mixed_bits(self.c) ^ swapped(far ^ self.c)
        block = ((q & 1) * self.nd + step) * self.ny + (q >> 1)
        place = lax.rem(self.d - step + self.nd, self.nd)
        table = jnp.stack([block, far ^ self.c, place]).astype(jnp.int32)
        first = table[:, : self.nd].at[1].set(0)
        return first, table[:, self.nd :]

    def to_parts(self, value):
        if value.shape[0] == self.nc:
            return value
        parts = []
        for j in range(self.nc):
            x = self.r ^ mixed_bits(self.c) ^ swapped(j)
            pieces = []
            for h in range(self.nd):
                s = lax.rem(self.d - h + self.nd, self.nd)
                at = ((lax.rem(x, 2) * self.nd + s) * self.ny + x // 2) * self.piece
                pieces.append(lax.dynamic_slice_in_dim(value[0], at, self.piece, 1))
            parts.append(jnp.concatenate(pieces, -1))
        return jnp.stack(parts)

    def own_piece(self, block):
        return lax.dynamic_slice_in_dim(block, self.d * self.piece, self.piece, 0)

    def spread_one(self, own):
        return [self.hop_x(own, s) for s in range(1, self.nd)], self.hop_y(own)

    def spread_two(self, by_x, by_y):
        half = self.piece // 2
        return [
            (self.hop_y(x[:half]), self.hop_x(by_y[half:], s + 1)) for s, x in enumerate(by_x)
        ]

    def spread_end(self, own, by_x, by_y, both):
        chunks = [own, by_y]
        for x, pair in zip(by_x, both):
            chunks += [x, *pair]
        return jnp.concatenate(chunks, 0)

    def sum_plane_grad(self, grad):
        if self.piece != SPAN:
            count = self.blocks.shape[0]
            place = self.blocks[None, :] == jnp.arange(count, dtype=jnp.int32)[:, None]
            grad = self.chunks_of(grad, jnp.argmax(place, 1).astype(jnp.int32))
        return lax.psum_scatter(grad, ("dp", "row"), scatter_dimension=0, tiled=True)

    def core_order(self):
        count = self.straight.shape[0]
        return lax.rem(self.straight + lax.rem(self.r, 2) * (count // 2), count)

    def sum_cores(self, grad):
        pairs = [[r, r + 1] for r in range(0, self.nr, 2)]
        return lax.psum_scatter(
            grad, "row", scatter_dimension=0, axis_index_groups=pairs, tiled=True
        )

    def collect_one(self, near, flipped):
        shape = (self.nd, self.ny, 2, self.piece // 2, near.shape[1])
        near = total(near, flipped).reshape(shape)
        by_x = [self.hop_x(near[s, :, 0], -s) for s in range(1, self.nd)]
        by_y = self.hop_y(near[:, 1, 1])
        return near, by_x, by_y

    def collect_two(self, near, by_x, by_y):
        low = total(near[0, :, 0], *by_x)
        high = total(near[:, 0, 1], by_y)
        return low, high, self.hop_y(low[1]), [self.hop_x(high[s], -s) for s in range(1, self.nd)]

    def collect_end(self, low, high, by_y, by_x):
        return jnp.concatenate([total(low[0], by_y), total(high[0], *by_x)], 0)

    def join(self, mine):
        return [self.hop_x(mine, s) for s in range(1, self.nd)]

    def join_end(self, mine, others, widths, turn):
        places = jnp.arange(self.nd)
        spots = lax.rem(self.d - places + self.nd, self.nd).astype(jnp.int32)
        pieces = [mine, *others]
        if turn and self.piece % 128:
            first, second = joined(pieces, spots, widths, False)
            return first.T, second.T
        return joined(pieces, spots, widths, turn)

    def pick(self, parts, offset):
        j = jnp.clip(self.c + offset, 0, self.nc - 1)
        return lax.dynamic_index_in_dim(parts, j, 0, False)

    def pick_around(self, parts, offset):
        j = lax.rem(self.c + offset + self.nc, self.nc)
        return lax.dynamic_index_in_dim(parts, j, 0, False)

    def sum_one(self, far):
        return (
            lax.ppermute(far, "col", [(0, 1), (1, 2)]),
            lax.ppermute(far, "col", [(3, 2), (2, 1)]),
        )

    def sum_two(self, parts, moved):
        return (
            self.roll(total(self.pick_around(parts, 1), moved[0]), 1),
            self.roll(total(self.pick_around(parts, -1), moved[1]), -1),
        )


def total(*values):
    return sum(v.astype(FULL) for v in values).astype(LOW)


def split_exact(value):
    parts = []
    for _ in range(3):
        part = lax.reduce_precision(value, 8, 7)
        parts.append(part.astype(LOW))
        value = value - part
    return jnp.concatenate(parts, 0)


def local(
    tokens,
    segment_ids,
    norm1_gain,
    norm1_bias,
    norm2_gain,
    norm2_bias,
    qkv_weight,
    qkv_bias,
    out_weight,
    out_bias,
    up_weight,
    up_bias,
    down_weight,
    down_bias,
    cotangent,
):
    rows, part = tokens.shape
    plan, order = Plan(part), Order()
    width = part * plan.nc
    first_tiles, rest_tiles = plan.tiles()
    parts = plan.nc if plan.piece == SPAN else 1
    part_cols = width // parts
    qkv_cols = qkv_weight.shape[1]
    attn_cols = out_weight.shape[0]
    up_cols = up_weight.shape[1]

    small = split_exact(jnp.stack([norm1_gain, norm1_bias, norm2_gain, norm2_bias]))
    own = attach(tokens, jnp.concatenate([small, jnp.zeros((16 - small.shape[0], part), LOW)], 0))
    crossed = jnp.concatenate([segment_ids.astype(FULL).reshape(-1), qkv_bias, up_bias])
    crossed, settle_crossed = plan.cross(crossed)
    one = plan.rolls(own)
    rest = jnp.concatenate(
        [
            plan.own_piece(up_weight),
            plan.own_piece(out_weight.T),
            plan.own_piece(down_weight.T),
        ],
        1,
    )
    rest, settle_rest = plan.turn_plane(rest)
    turned_qkv, settle_qkv = plan.turn(plan.own_piece(qkv_weight))
    table = rotary_table()
    turned_qkv, table, crossed, rest, one = order.wait(turned_qkv, table, crossed, rest, one)

    two = plan.two_away(*one)
    turned_up, settle_up = plan.turn_line(settle_rest(rest, lambda v: v[:, :up_cols]))
    turned_qkv = settle_qkv(turned_qkv)
    qkv_x, qkv_y = plan.spread_one(turned_qkv)
    qkv_x, qkv_y = order.wait(qkv_x, qkv_y)

    qkv_both = order.wait(plan.spread_two(qkv_x, qkv_y))
    qkv_near = plan.spread_end(turned_qkv, qkv_x, qkv_y, qkv_both)
    qkv_near, turned_up, two = order.wait(qkv_near, turned_up, two)

    qkv_far = plan.flip(qkv_near)
    up_all = plan.gather_plane(settle_up(turned_up))
    turned_back, settle_back = plan.turn_line(
        order.gate(settle_rest(rest, lambda v: v[:, up_cols:]))
    )
    x = order.run(plan.arrange, own, one, two)
    small = x[rows : rows + 12].astype(FULL)
    par = (small[0:4] + small[4:8]) + small[8:12]
    first, second, mean, inv = order.run(norms, x, par, rows)
    qkv_far = order.wait(qkv_far)
    crossed = settle_crossed(crossed)
    segs = crossed[: segment_ids.size].astype(jnp.int32).reshape(segment_ids.shape)
    biases = crossed[segment_ids.size :]
    seg_col = jnp.broadcast_to(segs[:, :, None], segs.shape + (128,))
    seg_row = segs[:, None, :]
    qkv_w = (qkv_near, qkv_far)
    qkv = order.run(project_qkv, first, qkv_w, biases[:qkv_cols], table)
    turned_back = order.wait(turned_back)

    turned_back = settle_back(turned_back)
    back_x, back_y = plan.spread_one(turned_back)
    grad_one = plan.rolls(order.gate(cotangent))
    attn, logs = order.run(attend, qkv, seg_col, seg_row)
    up_w = order.run(reordered, up_all, plan.plane_order())
    act, slope = order.run(project_up, second, up_w, biases[qkv_cols:])
    hidden = jnp.concatenate([attn, act], 1)
    back_x, back_y = order.wait(back_x, back_y)

    back_both = plan.spread_two(back_x, back_y)
    hidden, back_both, grad_one = order.wait(hidden, back_both, grad_one)

    back_near = plan.spread_end(turned_back, back_x, back_y, back_both)
    back_far = plan.flip(back_near)
    grad_two = plan.two_away(*grad_one)
    back_far = order.wait(back_far)
    back_w = (back_near, back_far)

    if first_tiles is not None:
        branch_far = order.run(project_back, hidden, back_w, first_tiles, 1, part)[0]
        branch_one = plan.sum_one(branch_far)
    branch = plan.to_parts(order.run(project_back, hidden, back_w, rest_tiles, parts, part_cols))
    if first_tiles is None:
        branch_one = plan.sum_one(plan.pick_around(branch, 2))
    order.need(grad_two)
    grad = order.run(plan.arrange, cotangent, grad_one, grad_two)
    branch_one = order.wait(branch_one)

    branch_two = plan.sum_two(branch, branch_one)
    back_g = order.run(weight_grads, grad, hidden, plan.plane_order())
    back_g = plan.sum_plane_grad(back_g)
    attn_grad = order.run(attn_grads, grad, back_w, attn_cols)
    up_grad, up_bias_grad = order.run(up_grads, grad, back_w, slope)
    qkv_grad, qkv_bias_grad = order.run(
        attend_back, qkv, attn_grad, logs, seg_col, seg_row, table
    )
    qkv_g = order.run(weight_halves, first, qkv_grad)
    branch_two = order.wait(branch_two)

    qkv_flip = plan.flip(order.gate(qkv_g[1]))
    biases = jnp.concatenate(
        [jnp.sum(order.gate(cotangent), 0, dtype=FULL), qkv_bias_grad[0], up_bias_grad[0]]
    )
    biases_flip = plan.flip(biases)
    up_g = order.run(weight_halves, second, up_grad)
    mixed = plan.pick(branch, 0).astype(FULL) + sum(v.astype(FULL) for v in branch_two)
    mixed = (tokens.astype(FULL) + mixed + (out_bias + down_bias)).astype(LOW)
    mixed, qkv_flip, biases_flip, back_g = order.wait(mixed, qkv_flip, biases_flip, back_g)

    qkv_c, qkv_x, qkv_y = plan.collect_one(qkv_g[0], qkv_flip)
    up_flip = plan.flip(order.gate(up_g[1]))
    biases = biases + biases_flip
    biases_hop = plan.hop_y(biases)
    turned_back, settle_back = plan.turn_back(back_g)
    grads = (qkv_grad, up_grad, qkv_w, up_w, x, mean, inv, par)
    sums_far, row_far = None, 0.0
    if first_tiles is not None:
        mine_far, sums_far, row_far = order.run(input_grads, *grads, first_tiles, 1, part)
    qkv_x, qkv_y, up_flip, biases_hop = order.wait(qkv_x, qkv_y, up_flip, biases_hop)

    qkv_low, qkv_high, qkv_y, qkv_x = plan.collect_two(qkv_c, qkv_x, qkv_y)
    if first_tiles is not None:
        mine_one = plan.sum_one(order.gate(mine_far[0]))
    mine, sums, row_sums = order.run(input_grads, *grads, rest_tiles, parts, part_cols)
    mine, sums, row_sums = plan.to_parts(mine), plan.to_parts(sums), row_sums + row_far
    if first_tiles is None:
        mine_one = plan.sum_one(plan.pick_around(mine, 2))
    turned_back = settle_back(order.wait(turned_back))
    back_joined = plan.join(turned_back)
    mine_one, qkv_x, qkv_y = order.wait(mine_one, qkv_x, qkv_y)

    mine_two = plan.sum_two(mine, mine_one)
    up_c, up_x, up_y = plan.collect_one(up_g[0], order.gate(up_flip))
    back_joined, up_x, up_y = order.wait(back_joined, up_x, up_y)

    up_low, up_high, up_y, up_x = plan.collect_two(up_c, up_x, up_y)
    turned_qkv, settle_qkv = plan.turn_back(
        order.gate(plan.collect_end(qkv_low, qkv_high, qkv_y, qkv_x))
    )
    out_g, down_g = plan.join_end(
        turned_back, back_joined, (attn_cols, turned_back.shape[1] - attn_cols), True
    )
    out_g, down_g, up_x, up_y, turned_qkv, mine_two = order.wait(
        out_g, down_g, up_x, up_y, turned_qkv, mine_two
    )

    turned_up, settle_up = plan.turn_back(plan.collect_end(up_low, up_high, up_y, up_x))
    turned_qkv = settle_qkv(turned_qkv)
    qkv_joined = plan.join(turned_qkv)
    biases = biases + biases_hop
    biases_join = plan.join(order.gate(biases))
    row_sums = jnp.sum(row_sums, 2).reshape(-1)
    own_sums = [plan.pick_around(sums, n).reshape(-1) for n in range(plan.nc)]
    if sums_far is not None:
        own_sums[2] = sums_far[0].reshape(-1)
    own_sums = [jnp.concatenate([v, row_sums]) for v in own_sums]
    sums_moved = [plan.roll(own_sums[n], n) for n in range(1, plan.nc)]
    biases_join, turned_up, qkv_joined, sums_moved = order.wait(
        biases_join, turned_up, qkv_joined, sums_moved
    )
    biases = biases + sum(biases_join)
    bias_grads, settle_biases = plan.turn_back(biases[part:])

    turned_up = settle_up(turned_up)
    up_joined = plan.join(turned_up)
    sums = own_sums[0] + sum(sums_moved)
    norm_sums, grad_stats = sums[: 4 * part], sums[4 * part :].reshape(2, rows, 1)
    norm_sums = norm_sums + plan.flip(norm_sums)
    norm_sums = norm_sums + plan.hop_y(norm_sums)
    norm_sums = norm_sums + sum(plan.join(norm_sums))
    mine = plan.pick(mine, 0).astype(FULL) + sum(v.astype(FULL) for v in mine_two)
    mean, inv = mean[:, :1], inv[:, :1]
    own_normed = (tokens.astype(FULL) - mean) * inv
    input_grad = cotangent.astype(FULL) + inv * (
        mine - grad_stats[0] / width - own_normed * (grad_stats[1] / width)
    )
    qkv_g = plan.join_end(turned_qkv, qkv_joined, (qkv_cols,), False)[0]
    input_grad, qkv_g, norm_sums, up_joined, bias_grads = order.wait(
        input_grad, qkv_g, norm_sums, up_joined, bias_grads
    )

    up_g = plan.join_end(turned_up, up_joined, (up_cols,), False)[0]
    bias_grads = settle_biases(bias_grads)
    norm_sums = norm_sums.reshape(4, part)
    output_bias_grad = biases[:part]
    return (
        mixed,
        input_grad,
        norm_sums[0],
        norm_sums[1],
        norm_sums[2],
        norm_sums[3],
        qkv_g,
        bias_grads[:qkv_cols],
        out_g,
        output_bias_grad,
        up_g,
        bias_grads[qkv_cols:],
        down_g,
        output_bias_grad,
    )


def solution(mesh):
    in_specs = (
        P(("dp", "row"), "col"),
        P(("dp", "col"), None),
        P("col"),
        P("col"),
        P("col"),
        P("col"),
        P("col", "row"),
        P("row"),
        P("row", "col"),
        P("col"),
        P("col", "row"),
        P("row"),
        P("row", "col"),
        P("col"),
        P(("dp", "row"), "col"),
    )
    out_specs = (
        P(("dp", "row"), "col"),
        P(("dp", "row"), "col"),
        P("col"),
        P("col"),
        P("col"),
        P("col"),
        P("col", "row"),
        P("row"),
        P("row", "col"),
        P("col"),
        P("col", "row"),
        P("row"),
        P("row", "col"),
        P("col"),
    )
    return jax.shard_map(local, mesh=mesh, in_specs=in_specs, out_specs=out_specs, check_vma=False)
```

```python
import functools

import jax
import jax.numpy as jnp
from jax import lax
from jax.experimental import pallas as pl
from jax.experimental.pallas import tpu as pltpu
from jax.sharding import PartitionSpec as P

LEN = 1024
HEAD_DIM = 256
ROTARY = 64


EPS = 1e-05
BASE = 10000.0
LOW = jnp.bfloat16
FULL = jnp.float32


SCOPED = 48 * 2**20
SPAN = 256


def params(count=1):
    return pltpu.CompilerParams(
        dimension_semantics=("arbitrary",) * count, vmem_limit_bytes=SCOPED
    )


CHEAP = pl.CostEstimate(flops=10**8, bytes_accessed=10**5, transcendentals=0)


def nn(a, b):
    return jnp.dot(a, b, preferred_element_type=FULL)


def nt(a, b):
    return lax.dot_general(a, b, (((1,), (1,)), ((), ())), preferred_element_type=FULL)


def tn(a, b):
    return lax.dot_general(a, b, (((0,), (0,)), ((), ())), preferred_element_type=FULL)


def whole(shape):
    return pl.BlockSpec(shape, lambda *_: (0,) * len(shape))


def norm_kernel(x_ref, par_ref, first_ref, second_ref, mean_ref, inv_ref):
    x = x_ref[...].astype(FULL)
    width = x.shape[1]
    mean = jnp.sum(x, 1, keepdims=True) / width
    centred = x - mean
    variance = jnp.sum(centred * centred, 1, keepdims=True) / width
    inv = lax.rsqrt(variance + EPS)
    normed = centred * inv
    first_ref[...] = (normed * par_ref[0:1, :] + par_ref[1:2, :]).astype(LOW)
    second_ref[...] = (normed * par_ref[2:3, :] + par_ref[3:4, :]).astype(LOW)
    mean_ref[...] = jnp.broadcast_to(mean, mean_ref.shape)
    inv_ref[...] = jnp.broadcast_to(inv, inv_ref.shape)


def norms(x, par, rows):
    width = x.shape[1]
    tile = 128
    wide = pl.BlockSpec((tile, width), lambda i: (i, 0))
    thin = pl.BlockSpec((tile, 128), lambda i: (i, 0))
    return pl.pallas_call(
        norm_kernel,
        grid=(rows // tile,),
        in_specs=[wide, whole(par.shape)],
        out_specs=[wide, wide, thin, thin],
        out_shape=[jax.ShapeDtypeStruct((rows, width), LOW)] * 2
        + [jax.ShapeDtypeStruct((rows, 128), FULL)] * 2,
        compiler_params=params(),
        cost_estimate=CHEAP,
        name="norms",
    )(x, par)


def turn_features(value, table_ref, at, sign):
    half = ROTARY // 2
    head = value[:, :128]
    cosine = table_ref[0, at, :]
    down = table_ref[1, at, :] * sign
    up = table_ref[2, at, :] * sign
    head = head * cosine + pltpu.roll(head, 128 - half, 1) * down + pltpu.roll(head, half, 1) * up
    return jnp.concatenate([head, value[:, 128:]], 1)


def nn2(x_ref, at, near_ref, far_ref):
    half = near_ref.shape[0]
    return nn(x_ref[at, :half], near_ref[...]) + nn(x_ref[at, half:], far_ref[...])


def column_pair(weight, cols, skip=0):
    rows = weight[0].shape[0]
    return [pl.BlockSpec((rows, cols), lambda j: (0, j + skip))] * 2


def qkv_kernel(x_ref, near_ref, far_ref, b_ref, table_ref, out_ref):
    rows = x_ref.shape[0]
    kind = lax.rem(pl.program_id(0), 3)
    for m in range(rows // SPAN):
        at = pl.ds(m * SPAN, SPAN)
        place = pl.ds(m * SPAN % LEN, SPAN)
        value = nn2(x_ref, at, near_ref, far_ref) + b_ref[...]
        turned = turn_features(value, table_ref, place, 1.0)
        out_ref[0, at, :] = jnp.where(kind == 2, value, turned).astype(LOW)


def project_qkv(first, weight, bias, table):
    rows = first.shape[0]
    tiles = weight[0].shape[1] // HEAD_DIM
    return pl.pallas_call(
        qkv_kernel,
        grid=(tiles,),
        in_specs=[
            whole(first.shape),
            *column_pair(weight, HEAD_DIM),
            pl.BlockSpec((1, HEAD_DIM), lambda j: (0, j)),
            whole(table.shape),
        ],
        out_specs=pl.BlockSpec((1, rows, HEAD_DIM), lambda j: (j, 0, 0)),
        out_shape=jax.ShapeDtypeStruct((tiles, rows, HEAD_DIM), LOW),
        compiler_params=params(),
        cost_estimate=CHEAP,
        name="project_qkv",
    )(first, *weight, bias.reshape(1, -1), table)


def key_range(i):
    low = max(0, (i * SPAN - 511) // SPAN)
    return low * SPAN, (i + 1) * SPAN


def masked(query, keys, seg_col, seg_row, start, low):
    raw = nt(query, keys) * HEAD_DIM ** (-0.5)
    shape = raw.shape
    q_at = lax.broadcasted_iota(jnp.int32, shape, 0) + (start - low)
    k_at = lax.broadcasted_iota(jnp.int32, shape, 1)
    return jnp.where((q_at >= k_at) & (seg_col == seg_row), raw, -1e30)


def attend_kernel(q_ref, k_ref, v_ref, col_ref, row_ref, out_ref, log_ref):
    for i in range(LEN // SPAN):
        low, high = key_range(i)
        at = pl.ds(i * SPAN, SPAN)
        span = pl.ds(low, high - low)
        scores = masked(
            q_ref[0, at, :], k_ref[0, span, :], col_ref[0, at, 0:1], row_ref[0, :, span], i * SPAN, low
        )
        peak = jnp.max(scores, 1, keepdims=True)
        expos = jnp.exp(scores - peak)
        total = jnp.sum(expos, 1, keepdims=True)
        probs = (expos * (1.0 / total)).astype(LOW)
        out_ref[at, :] = nn(probs, v_ref[0, span, :]).astype(LOW)
        log_ref[0, at, :] = jnp.broadcast_to(peak + jnp.log(total), (SPAN, 128))


def attend(qkv, seg_col, seg_row):
    tiles, rows, _ = qkv.shape
    heads, seqs = tiles // 3, rows // LEN

    def part(kind):
        return pl.BlockSpec((1, LEN, HEAD_DIM), lambda h, s: (3 * h + kind, s, 0))

    return pl.pallas_call(
        attend_kernel,
        grid=(heads, seqs),
        in_specs=[
            part(0),
            part(1),
            part(2),
            pl.BlockSpec((1, LEN, 128), lambda h, s: (s, 0, 0)),
            pl.BlockSpec((1, 1, LEN), lambda h, s: (s, 0, 0)),
        ],
        out_specs=[
            pl.BlockSpec((LEN, HEAD_DIM), lambda h, s: (s, h)),
            pl.BlockSpec((1, LEN, 128), lambda h, s: (h, s, 0)),
        ],
        out_shape=[
            jax.ShapeDtypeStruct((rows, heads * HEAD_DIM), LOW),
            jax.ShapeDtypeStruct((heads, rows, 128), FULL),
        ],
        compiler_params=params(2),
        cost_estimate=CHEAP,
        name="attend",
    )(qkv, qkv, qkv, seg_col, seg_row)


def attend_back_kernel(
    q_ref, k_ref, v_ref, g_ref, log_ref, col_ref, row_ref, table_ref, out_ref, sum_ref, dk_ref, dv_ref
):
    @pl.when(pl.program_id(1) == 0)
    def _():
        sum_ref[...] = jnp.zeros_like(sum_ref)

    def put(at, kind, value):
        value = value.astype(LOW)
        span = pl.ds(kind * HEAD_DIM, HEAD_DIM)
        out_ref[at, span] = value
        sum_ref[:, span] += jnp.sum(value.astype(FULL), 0, keepdims=True)

    dk_ref[...] = jnp.zeros_like(dk_ref)
    dv_ref[...] = jnp.zeros_like(dv_ref)
    for i in range(LEN // SPAN):
        low, high = key_range(i)
        at = pl.ds(i * SPAN, SPAN)
        span = pl.ds(low, high - low)
        query, keys, grad = q_ref[0, at, :], k_ref[0, span, :], g_ref[at, :]
        scores = masked(
            query, keys, col_ref[0, at, 0:1], row_ref[0, :, span], i * SPAN, low
        )
        probs = jnp.exp(scores - log_ref[0, at, 0:1])
        probs_grad = nt(grad, v_ref[0, span, :])
        inner = jnp.sum(probs * probs_grad, 1, keepdims=True)
        raw_grad = (probs * (probs_grad - inner) * HEAD_DIM ** (-0.5)).astype(LOW)
        dv_ref[span, :] += tn(probs.astype(LOW), grad)
        dk_ref[span, :] += tn(raw_grad, query)
        dq = nn(raw_grad, keys)
        put(at, 0, turn_features(dq, table_ref, at, -1.0))
    for i in range(LEN // SPAN):
        at = pl.ds(i * SPAN, SPAN)
        put(at, 1, turn_features(dk_ref[at, :], table_ref, at, -1.0))
        put(at, 2, dv_ref[at, :])


def attend_back(qkv, grad, logs, seg_col, seg_row, table):
    tiles, rows, _ = qkv.shape
    heads, seqs = tiles // 3, rows // LEN

    def part(kind):
        return pl.BlockSpec((1, LEN, HEAD_DIM), lambda h, s: (3 * h + kind, s, 0))

    return pl.pallas_call(
        attend_back_kernel,
        grid=(heads, seqs),
        in_specs=[
            part(0),
            part(1),
            part(2),
            pl.BlockSpec((LEN, HEAD_DIM), lambda h, s: (s, h)),
            pl.BlockSpec((1, LEN, 128), lambda h, s: (h, s, 0)),
            pl.BlockSpec((1, LEN, 128), lambda h, s: (s, 0, 0)),
            pl.BlockSpec((1, 1, LEN), lambda h, s: (s, 0, 0)),
            whole(table.shape),
        ],
        out_specs=[
            pl.BlockSpec((LEN, 3 * HEAD_DIM), lambda h, s: (s, h)),
            pl.BlockSpec((1, 3 * HEAD_DIM), lambda h, s: (0, h)),
        ],
        out_shape=[
            jax.ShapeDtypeStruct((rows, tiles * HEAD_DIM), LOW),
            jax.ShapeDtypeStruct((1, tiles * HEAD_DIM), FULL),
        ],
        scratch_shapes=[pltpu.VMEM((LEN, HEAD_DIM), FULL)] * 2,
        compiler_params=params(2),
        cost_estimate=CHEAP,
        name="attend_back",
    )(qkv, qkv, qkv, grad, logs, seg_col, seg_row, table)


def up_kernel(x_ref, near_ref, far_ref, b_ref, act_ref, slope_ref):
    rows = x_ref.shape[0]
    for m in range(rows // SPAN):
        at = pl.ds(m * SPAN, SPAN)
        value = nn2(x_ref, at, near_ref, far_ref) + b_ref[...]
        share = 0.5 * (1.0 + lax.erf(value * 0.5**0.5))
        act_ref[at, :] = (value * share).astype(LOW)
        bell = jnp.exp(value * value * -0.5) * 0.3989422804014327
        slope_ref[at, :] = (share + value * bell).astype(LOW)


def project_up(second, weight, bias):
    rows = second.shape[0]
    cols = weight[0].shape[1]
    tall = pl.BlockSpec((rows, SPAN), lambda j: (0, j))
    return pl.pallas_call(
        up_kernel,
        grid=(cols // SPAN,),
        in_specs=[
            whole(second.shape),
            *column_pair(weight, SPAN),
            pl.BlockSpec((1, SPAN), lambda j: (0, j)),
        ],
        out_specs=[tall, tall],
        out_shape=[jax.ShapeDtypeStruct((rows, cols), LOW)] * 2,
        compiler_params=params(),
        cost_estimate=CHEAP,
        name="project_up",
    )(second, *weight, bias.reshape(1, -1))


def row_pair(weight, row=lambda j, t: t[0, j]):
    rows, cols = weight[0].shape
    count = rows // SPAN
    return [
        pl.BlockSpec((SPAN, cols), lambda j, t: (jnp.minimum(row(j, t), count - 1), 0)),
        pl.BlockSpec((SPAN, cols), lambda j, t: (jnp.maximum(row(j, t) - count, 0), 0)),
    ]


def either(place, near_ref, far_ref, count, body):
    @pl.when(place < count)
    def _():
        body(near_ref)

    @pl.when(place >= count)
    def _():
        body(far_ref)


def back_kernel(tiles_ref, x_ref, near_ref, far_ref, out_ref, *, count):
    def body(w_ref):
        for m in range(x_ref.shape[0] // SPAN):
            at = pl.ds(m * SPAN, SPAN)
            out_ref[0, at, :] = nt(x_ref[at, :], w_ref[...]).astype(LOW)

    either(tiles_ref[0, pl.program_id(0)], near_ref, far_ref, count, body)


def project_back(hidden, weight, tiles, parts, part):
    rows = hidden.shape[0]
    return pl.pallas_call(
        functools.partial(back_kernel, count=weight[0].shape[0] // SPAN),
        grid_spec=pltpu.PrefetchScalarGridSpec(
            num_scalar_prefetch=1,
            grid=(tiles.shape[1],),
            in_specs=[whole(hidden.shape), *row_pair(weight)],
            out_specs=pl.BlockSpec((1, rows, SPAN), lambda j, t: (t[1, j], 0, t[2, j])),
        ),
        out_shape=jax.ShapeDtypeStruct((parts, rows, part), LOW),
        compiler_params=params(),
        cost_estimate=CHEAP,
        name="project_back",
    )(tiles, hidden, *weight)


def plain_kernel(x_ref, near_ref, far_ref, out_ref):
    for m in range(x_ref.shape[0] // SPAN):
        at = pl.ds(m * SPAN, SPAN)
        out_ref[at, :] = nn2(x_ref, at, near_ref, far_ref).astype(LOW)


def slope_kernel(x_ref, near_ref, far_ref, slope_ref, out_ref, sum_ref):
    total = jnp.zeros(sum_ref.shape, FULL)
    for m in range(x_ref.shape[0] // SPAN):
        at = pl.ds(m * SPAN, SPAN)
        value = nn2(x_ref, at, near_ref, far_ref) * slope_ref[at, :].astype(FULL)
        value = value.astype(LOW)
        out_ref[at, :] = value
        total = total + jnp.sum(value.astype(FULL), 0, keepdims=True)
    sum_ref[...] = total


def attn_grads(grad, weight, cols):
    rows = grad.shape[0]
    return pl.pallas_call(
        plain_kernel,
        grid=(cols // SPAN,),
        in_specs=[whole(grad.shape), *column_pair(weight, SPAN)],
        out_specs=pl.BlockSpec((rows, SPAN), lambda j: (0, j)),
        out_shape=jax.ShapeDtypeStruct((rows, cols), LOW),
        compiler_params=params(),
        cost_estimate=CHEAP,
        name="attn_grads",
    )(grad, *weight)


def up_grads(grad, weight, slope):
    rows, cols = slope.shape
    skip = (weight[0].shape[1] - cols) // SPAN
    tall = pl.BlockSpec((rows, SPAN), lambda j: (0, j))
    return pl.pallas_call(
        slope_kernel,
        grid=(cols // SPAN,),
        in_specs=[whole(grad.shape), *column_pair(weight, SPAN, skip), tall],
        out_specs=[tall, pl.BlockSpec((1, SPAN), lambda j: (0, j))],
        out_shape=[jax.ShapeDtypeStruct((rows, cols), LOW), jax.ShapeDtypeStruct((1, cols), FULL)],
        compiler_params=params(),
        cost_estimate=CHEAP,
        name="up_grads",
    )(grad, *weight, slope)


def input_kernel(
    tiles_ref, qg_ref, ug_ref, qn_ref, qf_ref, un_ref, uf_ref, x_ref, mean_ref, inv_ref, par_ref,
    out_ref, sums_ref, row_ref, *, count
):
    @pl.when(pl.program_id(0) == 0)
    def _():
        row_ref[...] = jnp.zeros_like(row_ref)

    def body(w_refs):
        wq_ref, wu_ref = w_refs
        sums = [jnp.zeros((1, SPAN), FULL) for _ in range(4)]
        for m in range(qg_ref.shape[0] // SPAN):
            at = pl.ds(m * SPAN, SPAN)
            first_grad = nt(qg_ref[at, :], wq_ref[...])
            second_grad = nt(ug_ref[at, :], wu_ref[...])
            normed = (x_ref[at, :].astype(FULL) - mean_ref[at, 0:1]) * inv_ref[at, 0:1]
            total = first_grad * par_ref[0:1, :] + second_grad * par_ref[2:3, :]
            out_ref[0, at, :] = total.astype(LOW)
            for n, value in enumerate((first_grad * normed, first_grad, second_grad * normed, second_grad)):
                sums[n] = sums[n] + jnp.sum(value, 0, keepdims=True)
            for n, value in enumerate((total, total * normed)):
                row_ref[n, at, :] += sum(value[:, o : o + 128] for o in range(0, SPAN, 128))
        sums_ref[0] = jnp.concatenate(sums, 0)

    either(tiles_ref[0, pl.program_id(0)], (qn_ref, un_ref), (qf_ref, uf_ref), count, body)


def input_grads(qkv_grad, up_grad, qkv_weight, up_weight, x, mean, inv, par, tiles, parts, part):
    rows = qkv_grad.shape[0]
    return pl.pallas_call(
        functools.partial(input_kernel, count=qkv_weight[0].shape[0] // SPAN),
        grid_spec=pltpu.PrefetchScalarGridSpec(
            num_scalar_prefetch=1,
            grid=(tiles.shape[1],),
            in_specs=[
                whole(qkv_grad.shape),
                whole(up_grad.shape),
                *row_pair(qkv_weight),
                *row_pair(up_weight),
                pl.BlockSpec((rows, SPAN), lambda j, t: (0, t[0, j])),
                whole(mean.shape),
                whole(inv.shape),
                pl.BlockSpec((4, SPAN), lambda j, t: (0, t[0, j])),
            ],
            out_specs=[
                pl.BlockSpec((1, rows, SPAN), lambda j, t: (t[1, j], 0, t[2, j])),
                pl.BlockSpec((1, 4, SPAN), lambda j, t: (t[1, j], 0, t[2, j])),
                whole((2, rows, 128)),
            ],
        ),
        out_shape=[
            jax.ShapeDtypeStruct((parts, rows, part), LOW),
            jax.ShapeDtypeStruct((parts, 4, part), FULL),
            jax.ShapeDtypeStruct((2, rows, 128), FULL),
        ],
        compiler_params=params(),
        cost_estimate=CHEAP,
        name="input_grads",
    )(tiles, qkv_grad, up_grad, *qkv_weight, *up_weight, x, mean, inv, par)


def weight_kernel(spots_ref, a_ref, b_ref, out_ref):
    out_ref[...] = tn(a_ref[...], b_ref[...]).astype(LOW)


def weight_grads(a, b, spots):
    rows, width = a.shape
    cols = b.shape[1]
    return pl.pallas_call(
        weight_kernel,
        grid_spec=pltpu.PrefetchScalarGridSpec(
            num_scalar_prefetch=1,
            grid=(width // SPAN,),
            in_specs=[pl.BlockSpec((rows, SPAN), lambda j, t: (0, j)), whole(b.shape)],
            out_specs=pl.BlockSpec((SPAN, cols), lambda j, t: (t[j], 0)),
        ),
        out_shape=jax.ShapeDtypeStruct((width, cols), LOW),
        compiler_params=params(),
        cost_estimate=CHEAP,
        name="weight_grads",
    )(spots, a, b)


def halves_kernel(a_ref, b_ref, near_ref, far_ref, *, count):
    value = tn(a_ref[...], b_ref[...]).astype(LOW)
    j = pl.program_id(0)

    @pl.when(j < count)
    def _():
        near_ref[...] = value

    @pl.when(j >= count)
    def _():
        far_ref[...] = value


def weight_halves(a, b):
    rows, width = a.shape
    cols = b.shape[1]
    count = width // SPAN // 2
    return pl.pallas_call(
        functools.partial(halves_kernel, count=count),
        grid=(2 * count,),
        in_specs=[pl.BlockSpec((rows, SPAN), lambda j: (0, j)), whole(b.shape)],
        out_specs=[
            pl.BlockSpec((SPAN, cols), lambda j: (jnp.minimum(j, count - 1), 0)),
            pl.BlockSpec((SPAN, cols), lambda j: (jnp.maximum(j - count, 0), 0)),
        ],
        out_shape=[jax.ShapeDtypeStruct((width // 2, cols), LOW)] * 2,
        compiler_params=params(),
        cost_estimate=CHEAP,
        name="weight_halves",
    )(a, b)


def reorder_kernel(spots_ref, x_ref, near_ref, far_ref):
    half = pl.num_programs(0) // 2

    @pl.when(pl.program_id(0) < half)
    def _():
        near_ref[...] = x_ref[...]

    @pl.when(pl.program_id(0) >= half)
    def _():
        far_ref[...] = x_ref[...]


def reordered(x, spots):
    rows, cols = x.shape
    count = rows // SPAN
    return pl.pallas_call(
        reorder_kernel,
        grid_spec=pltpu.PrefetchScalarGridSpec(
            num_scalar_prefetch=1,
            grid=(count,),
            in_specs=[pl.BlockSpec((SPAN, cols), lambda j, t: (t[j], 0))],
            out_specs=row_pair([jax.ShapeDtypeStruct((rows // 2, cols), LOW)], lambda j, t: j),
        ),
        out_shape=[jax.ShapeDtypeStruct((rows // 2, cols), LOW)] * 2,
        compiler_params=params(),
        cost_estimate=CHEAP,
        name="reorder",
    )(spots, x)


def rotary_table():
    half = ROTARY // 2
    places = jnp.arange(LEN).astype(FULL)
    freqs = BASE ** (-(jnp.arange(half).astype(FULL) * 2.0) / ROTARY)
    angles = places[:, None] * freqs[None, :]
    cosine, sine = jnp.cos(angles), jnp.sin(angles)
    rest = 128 - ROTARY
    zeros = jnp.zeros_like(sine)
    pad = jnp.zeros((LEN, rest), FULL)
    return jnp.stack(
        [
            jnp.concatenate([cosine, cosine, pad + 1.0], 1),
            jnp.concatenate([-sine, zeros, pad], 1),
            jnp.concatenate([zeros, sine, pad], 1),
        ]
    )


def arrange_kernel(table_ref, *refs):
    out_ref = refs[-1]
    source = table_ref[0, pl.program_id(0)]
    for n, x_ref in enumerate(refs[:-1]):

        @pl.when(source == n)
        def _():
            out_ref[...] = x_ref[...]


def arranged(blocks, table, piece):
    rows = blocks[0].shape[0]
    count = table.shape[1]
    at = jnp.arange(count, dtype=jnp.int32)
    used = table[0][None, :] == jnp.arange(len(blocks), dtype=jnp.int32)[:, None]
    before = used[:, None, :] & (at[None, None, :] <= at[None, :, None])
    last = jnp.max(jnp.where(before, at[None, None, :], -1), 2, keepdims=True)
    spots = jnp.sum(jnp.where(last == at[None, None, :], table[1][None, None, :], 0), 2)
    table = jnp.concatenate([table, spots], 0)

    def spec(n):
        return pl.BlockSpec((rows, piece), lambda i, t: (0, t[2 + n, i]))

    return pl.pallas_call(
        arrange_kernel,
        grid_spec=pltpu.PrefetchScalarGridSpec(
            num_scalar_prefetch=1,
            grid=(count,),
            in_specs=[spec(n) for n in range(len(blocks))],
            out_specs=pl.BlockSpec((rows, piece), lambda i, t: (0, i)),
        ),
        out_shape=jax.ShapeDtypeStruct((rows, count * piece), blocks[0].dtype),
        compiler_params=params(),
        cost_estimate=CHEAP,
        name="arrange",
    )(table, *blocks)


def join_kernel(spot_ref, *refs, count, cuts, turn):
    ins, outs = refs[:count], refs[count:]
    source = spot_ref[pl.program_id(0)]
    for n, x_ref in enumerate(ins):

        @pl.when(source == n)
        def _():
            for out_ref, start in zip(outs, cuts):
                if not turn:
                    out_ref[...] = x_ref[:, start : start + out_ref.shape[1]].astype(FULL)
                    continue
                for o in range(0, out_ref.shape[0], SPAN):
                    value = x_ref[:, start + o : start + o + SPAN].astype(FULL)
                    out_ref[o : o + SPAN, :] = value.T


def joined(pieces, spots, widths, turn):
    piece, cols = pieces[0].shape
    count = len(pieces)
    cuts = [sum(widths[:n]) for n in range(len(widths))]
    if turn:
        specs = [pl.BlockSpec((w, piece), lambda h, t: (0, h)) for w in widths]
        shapes = [jax.ShapeDtypeStruct((w, piece * count), FULL) for w in widths]
    else:
        specs = [pl.BlockSpec((piece, w), lambda h, t: (h, 0)) for w in widths]
        shapes = [jax.ShapeDtypeStruct((piece * count, w), FULL) for w in widths]
    return pl.pallas_call(
        functools.partial(join_kernel, count=count, cuts=cuts, turn=turn),
        grid_spec=pltpu.PrefetchScalarGridSpec(
            num_scalar_prefetch=1,
            grid=(count,),
            in_specs=[whole((piece, cols))] * count,
            out_specs=specs,
        ),
        out_shape=shapes,
        compiler_params=params(),
        cost_estimate=CHEAP,
        name="join",
    )(spots, *pieces)


def attach_kernel(x_ref, small_ref, out_ref):
    rows = x_ref.shape[0]
    out_ref[:rows, :] = x_ref[...]
    out_ref[rows:, :] = small_ref[...]


def attach(x, small):
    rows = x.shape[0] + small.shape[0]
    return pl.pallas_call(
        attach_kernel,
        in_specs=[pl.BlockSpec(memory_space=pltpu.VMEM)] * 2,
        out_specs=pl.BlockSpec(memory_space=pltpu.VMEM),
        out_shape=jax.ShapeDtypeStruct((rows, x.shape[1]), x.dtype),
        compiler_params=pltpu.CompilerParams(vmem_limit_bytes=SCOPED),
        cost_estimate=CHEAP,
        name="attach",
    )(x, small)


def swapped(v):
    return (v & 1) * 2 + (v >> 1)


def mixed_bits(v):
    return ((v & 1) ^ (v >> 1)) * 2 + (v >> 1)


class Order:
    def __init__(self):
        self.token, self.needs = (), ()

    def gate(self, *xs):
        out = lax.optimization_barrier(tuple(xs) + self.token)[: len(xs)]
        return out[0] if len(xs) == 1 else out

    def wait(self, *xs):
        out = self.gate(xs)
        self.token = tuple(jax.tree.leaves(out))
        return out[0] if len(xs) == 1 else out

    def need(self, *xs):
        self.needs += tuple(jax.tree.leaves(xs))

    def run(self, function, first, *rest):
        first = lax.optimization_barrier((first,) + self.token + self.needs)[0]
        out = function(first, *rest)
        self.token, self.needs = (out[0],) if isinstance(out, (tuple, list)) else (out,), ()
        return out


class Plan:
    def __init__(self, part):
        self.nd, self.nr, self.nc = (lax.axis_size(a) for a in ("dp", "row", "col"))
        self.d, self.r, self.c = (lax.axis_index(a) for a in ("dp", "row", "col"))
        self.part = part
        self.piece = part // self.nd
        self.ny = self.nr // 2
        spots = [(r, c) for r in range(self.nr) for c in range(self.nc)]
        goal = {(r, c): -r % 4 ^ swapped(c) for r, c in spots}
        self.pairs = [(r * self.nc + c, goal[r, c] * self.nc + swapped(r)) for r, c in spots]
        self.plane_pairs = [(r * self.nc + c, goal[r, c] * self.nc + c) for r, c in spots]
        self.line_pairs = [(goal[r, c] * self.nc + c, goal[r, c] * self.nc + swapped(r)) for r, c in spots]
        e = jnp.arange(2 * self.nd * self.ny, dtype=jnp.int32)
        self.straight = jnp.arange(part * self.nc // SPAN, dtype=jnp.int32)
        k, step, y = e // (self.nd * self.ny), e // self.ny % self.nd, e % self.ny
        self.places = jnp.stack(
            [swapped(self.r ^ (2 * y + k) ^ mixed_bits(self.c)), lax.rem(self.d - step + self.nd, self.nd)]
        ).astype(jnp.int32)
        self.blocks = (self.places[1] * self.nr + (self.r ^ (2 * y + k))).astype(jnp.int32)

    def move(self, x, pairs):
        moved = lax.ppermute(x, ("row", "col"), [(a, b) for a, b in pairs if a != b])
        here = self.r * self.nc + self.c
        stays = [here == a for a, b in pairs if a == b]

        def settle(moved, cut=lambda v: v):
            if not stays:
                return cut(moved)
            return jnp.where(functools.reduce(jnp.logical_or, stays), cut(x), cut(moved))

        return moved, settle

    def turn(self, x):
        return self.move(x, self.pairs)

    def turn_back(self, x):
        return self.move(x, [(b, a) for a, b in self.pairs])

    def turn_plane(self, x):
        return self.move(x, self.plane_pairs)

    def turn_line(self, x):
        return self.move(x, self.line_pairs)

    def cross(self, x):
        spots = [(r, c) for r in range(self.nr) for c in range(self.nc)]
        return self.move(x, [(r * self.nc + c, c * self.nc + swapped(r)) for r, c in spots])

    def gather_plane(self, own):
        value = lax.all_gather(own, ("dp", "row"), axis=0, tiled=True)
        if self.piece == SPAN:
            return value

        return self.chunks_of(value, self.blocks)

    def chunks_of(self, value, order):
        return jnp.concatenate(
            [
                lax.dynamic_slice_in_dim(value, order[i] * self.piece, self.piece, 0)
                for i in range(order.shape[0])
            ],
            0,
        )

    def plane_order(self):
        return self.blocks if self.piece == SPAN else self.straight

    def flip(self, x):
        return lax.ppermute(x, "row", [(r, r ^ 1) for r in range(self.nr)])

    def hop_y(self, x):
        return lax.ppermute(x, "row", [(r, r ^ 2) for r in range(self.nr)])

    def hop_x(self, x, s):
        return lax.ppermute(x, "dp", [(d, (d + s) % self.nd) for d in range(self.nd)])

    def roll(self, x, s):
        return lax.ppermute(x, "col", [(i, (i + s) % self.nc) for i in range(self.nc)])

    def rolls(self, x):
        return self.roll(x, 1), self.roll(x, -1)

    def two_away(self, ahead, behind):
        return (
            lax.ppermute(ahead, "col", [(1, 2), (2, 3)]),
            lax.ppermute(behind, "col", [(2, 1), (1, 0)]),
        )

    def arrange(self, own, one, two):
        away = lax.rem(self.c - self.places[0] + self.nc, self.nc)
        right = jnp.where(self.c >= 2, 2, 4)
        table = jnp.stack([jnp.where(away == 2, right, away), self.places[1]])
        blocks = [own, one[0], two[0], one[1], two[1]]
        if self.piece % 128 == 0:
            return arranged(blocks, table, self.piece)
        blocks = jnp.stack(blocks)
        chunks = [
            lax.dynamic_slice(
                blocks, [table[0, i], 0, table[1, i] * self.piece], (1, own.shape[0], self.piece)
            )[0]
            for i in range(table.shape[1])
        ]
        return jnp.concatenate(chunks, -1)

    def tiles(self):
        if self.piece != SPAN:
            e = self.straight
            return None, jnp.stack([e, 0 * e, e])
        far = jnp.array([2, 0, 1, 3], jnp.int32)
        far, step = jnp.repeat(far, self.nd), jnp.tile(jnp.arange(self.nd, dtype=jnp.int32), 4)
        q = self.r ^ mixed_bits(self.c) ^ swapped(far ^ self.c)
        block = ((q & 1) * self.nd + step) * self.ny + (q >> 1)
        place = lax.rem(self.d - step + self.nd, self.nd)
        table = jnp.stack([block, far ^ self.c, place]).astype(jnp.int32)
        first = table[:, : self.nd].at[1].set(0)
        return first, table[:, self.nd :]

    def to_parts(self, value):
        if value.shape[0] == self.nc:
            return value
        parts = []
        for j in range(self.nc):
            x = self.r ^ mixed_bits(self.c) ^ swapped(j)
            pieces = []
            for h in range(self.nd):
                s = lax.rem(self.d - h + self.nd, self.nd)
                at = ((lax.rem(x, 2) * self.nd + s) * self.ny + x // 2) * self.piece
                pieces.append(lax.dynamic_slice_in_dim(value[0], at, self.piece, 1))
            parts.append(jnp.concatenate(pieces, -1))
        return jnp.stack(parts)

    def own_piece(self, block):
        return lax.dynamic_slice_in_dim(block, self.d * self.piece, self.piece, 0)

    def spread_one(self, own):
        return [self.hop_x(own, s) for s in range(1, self.nd)], self.hop_y(own)

    def spread_two(self, by_x, by_y):
        half = self.piece // 2
        return [
            (self.hop_y(x[:half]), self.hop_x(by_y[half:], s + 1)) for s, x in enumerate(by_x)
        ]

    def spread_end(self, own, by_x, by_y, both):
        chunks = [own, by_y]
        for x, pair in zip(by_x, both):
            chunks += [x, *pair]
        return jnp.concatenate(chunks, 0)

    def sum_plane_grad(self, grad):
        if self.piece != SPAN:
            count = self.blocks.shape[0]
            place = self.blocks[None, :] == jnp.arange(count, dtype=jnp.int32)[:, None]
            grad = self.chunks_of(grad, jnp.argmax(place, 1).astype(jnp.int32))
        return lax.psum_scatter(grad, ("dp", "row"), scatter_dimension=0, tiled=True)

    def core_order(self):
        count = self.straight.shape[0]
        return lax.rem(self.straight + lax.rem(self.r, 2) * (count // 2), count)

    def sum_cores(self, grad):
        pairs = [[r, r + 1] for r in range(0, self.nr, 2)]
        return lax.psum_scatter(
            grad, "row", scatter_dimension=0, axis_index_groups=pairs, tiled=True
        )

    def collect_one(self, near, flipped):
        shape = (self.nd, self.ny, 2, self.piece // 2, near.shape[1])
        near = total(near, flipped).reshape(shape)
        by_x = [self.hop_x(near[s, :, 0], -s) for s in range(1, self.nd)]
        by_y = self.hop_y(near[:, 1, 1])
        return near, by_x, by_y

    def collect_two(self, near, by_x, by_y):
        low = total(near[0, :, 0], *by_x)
        high = total(near[:, 0, 1], by_y)
        return low, high, self.hop_y(low[1]), [self.hop_x(high[s], -s) for s in range(1, self.nd)]

    def collect_end(self, low, high, by_y, by_x):
        return jnp.concatenate([total(low[0], by_y), total(high[0], *by_x)], 0)

    def join(self, mine):
        return [self.hop_x(mine, s) for s in range(1, self.nd)]

    def join_end(self, mine, others, widths, turn):
        places = jnp.arange(self.nd)
        spots = lax.rem(self.d - places + self.nd, self.nd).astype(jnp.int32)
        pieces = [mine, *others]
        if turn and self.piece % 128:
            first, second = joined(pieces, spots, widths, False)
            return first.T, second.T
        return joined(pieces, spots, widths, turn)

    def pick(self, parts, offset):
        j = jnp.clip(self.c + offset, 0, self.nc - 1)
        return lax.dynamic_index_in_dim(parts, j, 0, False)

    def pick_around(self, parts, offset):
        j = lax.rem(self.c + offset + self.nc, self.nc)
        return lax.dynamic_index_in_dim(parts, j, 0, False)

    def sum_one(self, far):
        return (
            lax.ppermute(far, "col", [(0, 1), (1, 2)]),
            lax.ppermute(far, "col", [(3, 2), (2, 1)]),
        )

    def sum_two(self, parts, moved):
        return (
            self.roll(total(self.pick_around(parts, 1), moved[0]), 1),
            self.roll(total(self.pick_around(parts, -1), moved[1]), -1),
        )


def total(*values):
    return sum(v.astype(FULL) for v in values).astype(LOW)


def split_exact(value):
    parts = []
    for _ in range(3):
        part = lax.reduce_precision(value, 8, 7)
        parts.append(part.astype(LOW))
        value = value - part
    return jnp.concatenate(parts, 0)


def local(
    tokens,
    segment_ids,
    norm1_gain,
    norm1_bias,
    norm2_gain,
    norm2_bias,
    qkv_weight,
    qkv_bias,
    out_weight,
    out_bias,
    up_weight,
    up_bias,
    down_weight,
    down_bias,
    cotangent,
):
    rows, part = tokens.shape
    plan, order = Plan(part), Order()
    width = part * plan.nc
    first_tiles, rest_tiles = plan.tiles()
    parts = plan.nc if plan.piece == SPAN else 1
    part_cols = width // parts
    qkv_cols = qkv_weight.shape[1]
    attn_cols = out_weight.shape[0]
    up_cols = up_weight.shape[1]

    small = split_exact(jnp.stack([norm1_gain, norm1_bias, norm2_gain, norm2_bias]))
    own = attach(tokens, jnp.concatenate([small, jnp.zeros((16 - small.shape[0], part), LOW)], 0))
    crossed = jnp.concatenate([segment_ids.astype(FULL).reshape(-1), qkv_bias, up_bias])
    crossed, settle_crossed = plan.cross(crossed)
    one = plan.rolls(own)
    rest = jnp.concatenate(
        [
            plan.own_piece(up_weight),
            plan.own_piece(out_weight.T),
            plan.own_piece(down_weight.T),
        ],
        1,
    )
    rest, settle_rest = plan.turn_plane(rest)
    turned_qkv, settle_qkv = plan.turn(plan.own_piece(qkv_weight))
    table = rotary_table()
    turned_qkv, table, crossed, rest, one = order.wait(turned_qkv, table, crossed, rest, one)

    two = plan.two_away(*one)
    turned_up, settle_up = plan.turn_line(settle_rest(rest, lambda v: v[:, :up_cols]))
    turned_qkv = settle_qkv(turned_qkv)
    qkv_x, qkv_y = plan.spread_one(turned_qkv)
    qkv_x, qkv_y = order.wait(qkv_x, qkv_y)

    qkv_both = order.wait(plan.spread_two(qkv_x, qkv_y))
    qkv_near = plan.spread_end(turned_qkv, qkv_x, qkv_y, qkv_both)
    qkv_near, turned_up, two = order.wait(qkv_near, turned_up, two)

    qkv_far = plan.flip(qkv_near)
    up_all = plan.gather_plane(settle_up(turned_up))
    turned_back, settle_back = plan.turn_line(
        order.gate(settle_rest(rest, lambda v: v[:, up_cols:]))
    )
    x = order.run(plan.arrange, own, one, two)
    small = x[rows : rows + 12].astype(FULL)
    par = (small[0:4] + small[4:8]) + small[8:12]
    first, second, mean, inv = order.run(norms, x, par, rows)
    qkv_far = order.wait(qkv_far)
    crossed = settle_crossed(crossed)
    segs = crossed[: segment_ids.size].astype(jnp.int32).reshape(segment_ids.shape)
    biases = crossed[segment_ids.size :]
    seg_col = jnp.broadcast_to(segs[:, :, None], segs.shape + (128,))
    seg_row = segs[:, None, :]
    qkv_w = (qkv_near, qkv_far)
    qkv = order.run(project_qkv, first, qkv_w, biases[:qkv_cols], table)
    turned_back = order.wait(turned_back)

    turned_back = settle_back(turned_back)
    back_x, back_y = plan.spread_one(turned_back)
    grad_one = plan.rolls(order.gate(cotangent))
    attn, logs = order.run(attend, qkv, seg_col, seg_row)
    up_w = order.run(reordered, up_all, plan.plane_order())
    back_x, back_y = order.wait(back_x, back_y)

    back_both = plan.spread_two(back_x, back_y)
    act, slope = order.run(project_up, second, up_w, biases[qkv_cols:])
    hidden = jnp.concatenate([attn, act], 1)
    hidden, back_both, grad_one = order.wait(hidden, back_both, grad_one)

    back_near = plan.spread_end(turned_back, back_x, back_y, back_both)
    back_far = plan.flip(back_near)
    grad_two = plan.two_away(*grad_one)
    back_far = order.wait(back_far)
    back_w = (back_near, back_far)

    if first_tiles is not None:
        branch_far = order.run(project_back, hidden, back_w, first_tiles, 1, part)[0]
        branch_one = plan.sum_one(branch_far)
    branch = plan.to_parts(order.run(project_back, hidden, back_w, rest_tiles, parts, part_cols))
    if first_tiles is None:
        branch_one = plan.sum_one(plan.pick_around(branch, 2))
    order.need(grad_two)
    grad = order.run(plan.arrange, cotangent, grad_one, grad_two)
    back_g = order.run(weight_grads, grad, hidden, plan.plane_order())
    branch_one = order.wait(branch_one)

    branch_two = plan.sum_two(branch, branch_one)
    back_g = plan.sum_plane_grad(order.gate(back_g))
    attn_grad = order.run(attn_grads, grad, back_w, attn_cols)
    up_grad, up_bias_grad = order.run(up_grads, grad, back_w, slope)
    qkv_grad, qkv_bias_grad = order.run(
        attend_back, qkv, attn_grad, logs, seg_col, seg_row, table
    )
    qkv_g = order.run(weight_halves, first, qkv_grad)
    branch_two = order.wait(branch_two)

    qkv_flip = plan.flip(order.gate(qkv_g[1]))
    biases = jnp.concatenate(
        [jnp.sum(order.gate(cotangent), 0, dtype=FULL), qkv_bias_grad[0], up_bias_grad[0]]
    )
    biases_flip = plan.flip(biases)
    up_g = order.run(weight_halves, second, up_grad)
    mixed = plan.pick(branch, 0).astype(FULL) + sum(v.astype(FULL) for v in branch_two)
    mixed = (tokens.astype(FULL) + mixed + (out_bias + down_bias)).astype(LOW)
    biases = biases + biases_flip
    biases_hop = plan.hop_y(biases)
    mixed, qkv_flip, biases_hop, back_g = order.wait(mixed, qkv_flip, biases_hop, back_g)

    qkv_c, qkv_x, qkv_y = plan.collect_one(qkv_g[0], qkv_flip)
    up_flip = plan.flip(order.gate(up_g[1]))
    turned_back, settle_back = plan.turn_back(back_g)
    up_flip = order.wait(up_flip)
    grads = (qkv_grad, up_grad, qkv_w, up_w, x, mean, inv, par)
    sums_far, row_far = None, 0.0
    if first_tiles is not None:
        mine_far, sums_far, row_far = order.run(input_grads, *grads, first_tiles, 1, part)
        mine_one = plan.sum_one(mine_far[0])
    qkv_x, qkv_y = order.wait(qkv_x, qkv_y)

    qkv_low, qkv_high, qkv_y, qkv_x = plan.collect_two(qkv_c, qkv_x, qkv_y)
    mine, sums, row_sums = order.run(input_grads, *grads, rest_tiles, parts, part_cols)
    mine, sums, row_sums = plan.to_parts(mine), plan.to_parts(sums), row_sums + row_far
    if first_tiles is None:
        mine_one = plan.sum_one(plan.pick_around(mine, 2))
    turned_back = settle_back(order.wait(turned_back))
    back_joined = plan.join(turned_back)
    mine_one, qkv_x, qkv_y = order.wait(mine_one, qkv_x, qkv_y)

    mine_two = plan.sum_two(mine, mine_one)
    up_c, up_x, up_y = plan.collect_one(up_g[0], order.gate(up_flip))
    back_joined, up_x, up_y = order.wait(back_joined, up_x, up_y)

    up_low, up_high, up_y, up_x = plan.collect_two(up_c, up_x, up_y)
    turned_qkv, settle_qkv = plan.turn_back(
        order.gate(plan.collect_end(qkv_low, qkv_high, qkv_y, qkv_x))
    )
    out_g, down_g = plan.join_end(
        turned_back, back_joined, (attn_cols, turned_back.shape[1] - attn_cols), True
    )
    out_g, down_g, up_x, up_y, turned_qkv, mine_two = order.wait(
        out_g, down_g, up_x, up_y, turned_qkv, mine_two
    )

    turned_up, settle_up = plan.turn_back(plan.collect_end(up_low, up_high, up_y, up_x))
    turned_qkv = settle_qkv(turned_qkv)
    qkv_joined = plan.join(turned_qkv)
    biases = biases + biases_hop
    biases_join = plan.join(order.gate(biases))
    row_sums = jnp.sum(row_sums, 2).reshape(-1)
    own_sums = [plan.pick_around(sums, n).reshape(-1) for n in range(plan.nc)]
    if sums_far is not None:
        own_sums[2] = sums_far[0].reshape(-1)
    own_sums = [jnp.concatenate([v, row_sums]) for v in own_sums]
    sums_moved = [plan.roll(own_sums[n], n) for n in range(1, plan.nc)]
    biases_join, turned_up, qkv_joined, sums_moved = order.wait(
        biases_join, turned_up, qkv_joined, sums_moved
    )
    biases = biases + sum(biases_join)
    bias_grads, settle_biases = plan.turn_back(biases[part:])

    turned_up = settle_up(turned_up)
    up_joined = plan.join(turned_up)
    sums = own_sums[0] + sum(sums_moved)
    norm_sums, grad_stats = sums[: 4 * part], sums[4 * part :].reshape(2, rows, 1)
    norm_sums = norm_sums + plan.flip(norm_sums)
    norm_sums = norm_sums + plan.hop_y(norm_sums)
    norm_sums = norm_sums + sum(plan.join(norm_sums))
    mine = plan.pick(mine, 0).astype(FULL) + sum(v.astype(FULL) for v in mine_two)
    mean, inv = mean[:, :1], inv[:, :1]
    own_normed = (tokens.astype(FULL) - mean) * inv
    input_grad = cotangent.astype(FULL) + inv * (
        mine - grad_stats[0] / width - own_normed * (grad_stats[1] / width)
    )
    qkv_g = plan.join_end(turned_qkv, qkv_joined, (qkv_cols,), False)[0]
    input_grad, qkv_g, norm_sums, up_joined, bias_grads = order.wait(
        input_grad, qkv_g, norm_sums, up_joined, bias_grads
    )

    up_g = plan.join_end(turned_up, up_joined, (up_cols,), False)[0]
    bias_grads = settle_biases(bias_grads)
    norm_sums = norm_sums.reshape(4, part)
    output_bias_grad = biases[:part]
    return (
        mixed,
        input_grad,
        norm_sums[0],
        norm_sums[1],
        norm_sums[2],
        norm_sums[3],
        qkv_g,
        bias_grads[:qkv_cols],
        out_g,
        output_bias_grad,
        up_g,
        bias_grads[qkv_cols:],
        down_g,
        output_bias_grad,
    )


def solution(mesh):
    in_specs = (
        P(("dp", "row"), "col"),
        P(("dp", "col"), None),
        P("col"),
        P("col"),
        P("col"),
        P("col"),
        P("col", "row"),
        P("row"),
        P("row", "col"),
        P("col"),
        P("col", "row"),
        P("row"),
        P("row", "col"),
        P("col"),
        P(("dp", "row"), "col"),
    )
    out_specs = (
        P(("dp", "row"), "col"),
        P(("dp", "row"), "col"),
        P("col"),
        P("col"),
        P("col"),
        P("col"),
        P("col", "row"),
        P("row"),
        P("row", "col"),
        P("col"),
        P("col", "row"),
        P("row"),
        P("row", "col"),
        P("col"),
    )
    return jax.shard_map(local, mesh=mesh, in_specs=in_specs, out_specs=out_specs, check_vma=False)
```

```python
import functools

import jax
import jax.numpy as jnp
from jax import lax
from jax.experimental import pallas as pl
from jax.experimental.pallas import tpu as pltpu
from jax.sharding import PartitionSpec as P

LEN = 1024
HEAD_DIM = 256
ROTARY = 64


EPS = 1e-05
BASE = 10000.0
LOW = jnp.bfloat16
FULL = jnp.float32


SCOPED = 48 * 2**20
SPAN = 256


def params(count=1):
    return pltpu.CompilerParams(
        dimension_semantics=("arbitrary",) * count, vmem_limit_bytes=SCOPED
    )


CHEAP = pl.CostEstimate(flops=10**8, bytes_accessed=10**5, transcendentals=0)


def nn(a, b):
    return jnp.dot(a, b, preferred_element_type=FULL)


def nt(a, b):
    return lax.dot_general(a, b, (((1,), (1,)), ((), ())), preferred_element_type=FULL)


def tn(a, b):
    return lax.dot_general(a, b, (((0,), (0,)), ((), ())), preferred_element_type=FULL)


def whole(shape):
    return pl.BlockSpec(shape, lambda *_: (0,) * len(shape))


def norm_kernel(x_ref, par_ref, first_ref, second_ref, mean_ref, inv_ref):
    x = x_ref[...].astype(FULL)
    width = x.shape[1]
    mean = jnp.sum(x, 1, keepdims=True) / width
    centred = x - mean
    variance = jnp.sum(centred * centred, 1, keepdims=True) / width
    inv = lax.rsqrt(variance + EPS)
    normed = centred * inv
    first_ref[...] = (normed * par_ref[0:1, :] + par_ref[1:2, :]).astype(LOW)
    second_ref[...] = (normed * par_ref[2:3, :] + par_ref[3:4, :]).astype(LOW)
    mean_ref[...] = jnp.broadcast_to(mean, mean_ref.shape)
    inv_ref[...] = jnp.broadcast_to(inv, inv_ref.shape)


def norms(x, par, rows):
    width = x.shape[1]
    tile = 128
    wide = pl.BlockSpec((tile, width), lambda i: (i, 0))
    thin = pl.BlockSpec((tile, 128), lambda i: (i, 0))
    return pl.pallas_call(
        norm_kernel,
        grid=(rows // tile,),
        in_specs=[wide, whole(par.shape)],
        out_specs=[wide, wide, thin, thin],
        out_shape=[jax.ShapeDtypeStruct((rows, width), LOW)] * 2
        + [jax.ShapeDtypeStruct((rows, 128), FULL)] * 2,
        compiler_params=params(),
        cost_estimate=CHEAP,
        name="norms",
    )(x, par)


def turn_features(value, table_ref, at, sign):
    half = ROTARY // 2
    head = value[:, :128]
    cosine = table_ref[0, at, :]
    down = table_ref[1, at, :] * sign
    up = table_ref[2, at, :] * sign
    head = head * cosine + pltpu.roll(head, 128 - half, 1) * down + pltpu.roll(head, half, 1) * up
    return jnp.concatenate([head, value[:, 128:]], 1)


def nn2(x_ref, at, near_ref, far_ref):
    half = near_ref.shape[0]
    return nn(x_ref[at, :half], near_ref[...]) + nn(x_ref[at, half:], far_ref[...])


def column_pair(weight, cols, skip=0):
    rows = weight[0].shape[0]
    return [pl.BlockSpec((rows, cols), lambda j: (0, j + skip))] * 2


def qkv_kernel(x_ref, near_ref, far_ref, b_ref, table_ref, out_ref):
    rows = x_ref.shape[0]
    kind = lax.rem(pl.program_id(0), 3)
    for m in range(rows // SPAN):
        at = pl.ds(m * SPAN, SPAN)
        place = pl.ds(m * SPAN % LEN, SPAN)
        value = nn2(x_ref, at, near_ref, far_ref) + b_ref[...]
        turned = turn_features(value, table_ref, place, 1.0)
        out_ref[0, at, :] = jnp.where(kind == 2, value, turned).astype(LOW)


def project_qkv(first, weight, bias, table):
    rows = first.shape[0]
    tiles = weight[0].shape[1] // HEAD_DIM
    return pl.pallas_call(
        qkv_kernel,
        grid=(tiles,),
        in_specs=[
            whole(first.shape),
            *column_pair(weight, HEAD_DIM),
            pl.BlockSpec((1, HEAD_DIM), lambda j: (0, j)),
            whole(table.shape),
        ],
        out_specs=pl.BlockSpec((1, rows, HEAD_DIM), lambda j: (j, 0, 0)),
        out_shape=jax.ShapeDtypeStruct((tiles, rows, HEAD_DIM), LOW),
        compiler_params=params(),
        cost_estimate=CHEAP,
        name="project_qkv",
    )(first, *weight, bias.reshape(1, -1), table)


def key_range(i):
    low = max(0, (i * SPAN - 511) // SPAN)
    return low * SPAN, (i + 1) * SPAN


def masked(query, keys, seg_col, seg_row, start, low):
    raw = nt(query, keys) * HEAD_DIM ** (-0.5)
    shape = raw.shape
    q_at = lax.broadcasted_iota(jnp.int32, shape, 0) + (start - low)
    k_at = lax.broadcasted_iota(jnp.int32, shape, 1)
    return jnp.where((q_at >= k_at) & (seg_col == seg_row), raw, -1e30)


def attend_kernel(q_ref, k_ref, v_ref, col_ref, row_ref, out_ref, log_ref):
    for i in range(LEN // SPAN):
        low, high = key_range(i)
        at = pl.ds(i * SPAN, SPAN)
        span = pl.ds(low, high - low)
        scores = masked(
            q_ref[0, at, :], k_ref[0, span, :], col_ref[0, at, 0:1], row_ref[0, :, span], i * SPAN, low
        )
        peak = jnp.max(scores, 1, keepdims=True)
        expos = jnp.exp(scores - peak)
        total = jnp.sum(expos, 1, keepdims=True)
        probs = (expos * (1.0 / total)).astype(LOW)
        out_ref[at, :] = nn(probs, v_ref[0, span, :]).astype(LOW)
        log_ref[0, at, :] = jnp.broadcast_to(peak + jnp.log(total), (SPAN, 128))


def attend(qkv, seg_col, seg_row):
    tiles, rows, _ = qkv.shape
    heads, seqs = tiles // 3, rows // LEN

    def part(kind):
        return pl.BlockSpec((1, LEN, HEAD_DIM), lambda h, s: (3 * h + kind, s, 0))

    return pl.pallas_call(
        attend_kernel,
        grid=(heads, seqs),
        in_specs=[
            part(0),
            part(1),
            part(2),
            pl.BlockSpec((1, LEN, 128), lambda h, s: (s, 0, 0)),
            pl.BlockSpec((1, 1, LEN), lambda h, s: (s, 0, 0)),
        ],
        out_specs=[
            pl.BlockSpec((LEN, HEAD_DIM), lambda h, s: (s, h)),
            pl.BlockSpec((1, LEN, 128), lambda h, s: (h, s, 0)),
        ],
        out_shape=[
            jax.ShapeDtypeStruct((rows, heads * HEAD_DIM), LOW),
            jax.ShapeDtypeStruct((heads, rows, 128), FULL),
        ],
        compiler_params=params(2),
        cost_estimate=CHEAP,
        name="attend",
    )(qkv, qkv, qkv, seg_col, seg_row)


def attend_back_kernel(
    q_ref, k_ref, v_ref, g_ref, log_ref, col_ref, row_ref, table_ref, out_ref, sum_ref, dk_ref, dv_ref
):
    @pl.when(pl.program_id(1) == 0)
    def _():
        sum_ref[...] = jnp.zeros_like(sum_ref)

    def put(at, kind, value):
        value = value.astype(LOW)
        span = pl.ds(kind * HEAD_DIM, HEAD_DIM)
        out_ref[at, span] = value
        sum_ref[:, span] += jnp.sum(value.astype(FULL), 0, keepdims=True)

    dk_ref[...] = jnp.zeros_like(dk_ref)
    dv_ref[...] = jnp.zeros_like(dv_ref)
    for i in range(LEN // SPAN):
        low, high = key_range(i)
        at = pl.ds(i * SPAN, SPAN)
        span = pl.ds(low, high - low)
        query, keys, grad = q_ref[0, at, :], k_ref[0, span, :], g_ref[at, :]
        scores = masked(
            query, keys, col_ref[0, at, 0:1], row_ref[0, :, span], i * SPAN, low
        )
        probs = jnp.exp(scores - log_ref[0, at, 0:1])
        probs_grad = nt(grad, v_ref[0, span, :])
        inner = jnp.sum(probs * probs_grad, 1, keepdims=True)
        raw_grad = (probs * (probs_grad - inner) * HEAD_DIM ** (-0.5)).astype(LOW)
        dv_ref[span, :] += tn(probs.astype(LOW), grad)
        dk_ref[span, :] += tn(raw_grad, query)
        dq = nn(raw_grad, keys)
        put(at, 0, turn_features(dq, table_ref, at, -1.0))
    for i in range(LEN // SPAN):
        at = pl.ds(i * SPAN, SPAN)
        put(at, 1, turn_features(dk_ref[at, :], table_ref, at, -1.0))
        put(at, 2, dv_ref[at, :])


def attend_back(qkv, grad, logs, seg_col, seg_row, table):
    tiles, rows, _ = qkv.shape
    heads, seqs = tiles // 3, rows // LEN

    def part(kind):
        return pl.BlockSpec((1, LEN, HEAD_DIM), lambda h, s: (3 * h + kind, s, 0))

    return pl.pallas_call(
        attend_back_kernel,
        grid=(heads, seqs),
        in_specs=[
            part(0),
            part(1),
            part(2),
            pl.BlockSpec((LEN, HEAD_DIM), lambda h, s: (s, h)),
            pl.BlockSpec((1, LEN, 128), lambda h, s: (h, s, 0)),
            pl.BlockSpec((1, LEN, 128), lambda h, s: (s, 0, 0)),
            pl.BlockSpec((1, 1, LEN), lambda h, s: (s, 0, 0)),
            whole(table.shape),
        ],
        out_specs=[
            pl.BlockSpec((LEN, 3 * HEAD_DIM), lambda h, s: (s, h)),
            pl.BlockSpec((1, 3 * HEAD_DIM), lambda h, s: (0, h)),
        ],
        out_shape=[
            jax.ShapeDtypeStruct((rows, tiles * HEAD_DIM), LOW),
            jax.ShapeDtypeStruct((1, tiles * HEAD_DIM), FULL),
        ],
        scratch_shapes=[pltpu.VMEM((LEN, HEAD_DIM), FULL)] * 2,
        compiler_params=params(2),
        cost_estimate=CHEAP,
        name="attend_back",
    )(qkv, qkv, qkv, grad, logs, seg_col, seg_row, table)


def up_kernel(x_ref, near_ref, far_ref, b_ref, act_ref, slope_ref):
    rows = x_ref.shape[0]
    for m in range(rows // SPAN):
        at = pl.ds(m * SPAN, SPAN)
        value = nn2(x_ref, at, near_ref, far_ref) + b_ref[...]
        share = 0.5 * (1.0 + lax.erf(value * 0.5**0.5))
        act_ref[at, :] = (value * share).astype(LOW)
        bell = jnp.exp(value * value * -0.5) * 0.3989422804014327
        slope_ref[at, :] = (share + value * bell).astype(LOW)


def project_up(second, weight, bias):
    rows = second.shape[0]
    cols = weight[0].shape[1]
    tall = pl.BlockSpec((rows, SPAN), lambda j: (0, j))
    return pl.pallas_call(
        up_kernel,
        grid=(cols // SPAN,),
        in_specs=[
            whole(second.shape),
            *column_pair(weight, SPAN),
            pl.BlockSpec((1, SPAN), lambda j: (0, j)),
        ],
        out_specs=[tall, tall],
        out_shape=[jax.ShapeDtypeStruct((rows, cols), LOW)] * 2,
        compiler_params=params(),
        cost_estimate=CHEAP,
        name="project_up",
    )(second, *weight, bias.reshape(1, -1))


def row_pair(weight, row=lambda j, t: t[0, j]):
    rows, cols = weight[0].shape
    count = rows // SPAN
    return [
        pl.BlockSpec((SPAN, cols), lambda j, t: (jnp.minimum(row(j, t), count - 1), 0)),
        pl.BlockSpec((SPAN, cols), lambda j, t: (jnp.maximum(row(j, t) - count, 0), 0)),
    ]


def either(place, near_ref, far_ref, count, body):
    @pl.when(place < count)
    def _():
        body(near_ref)

    @pl.when(place >= count)
    def _():
        body(far_ref)


def back_kernel(tiles_ref, x_ref, near_ref, far_ref, out_ref, *, count):
    def body(w_ref):
        for m in range(x_ref.shape[0] // SPAN):
            at = pl.ds(m * SPAN, SPAN)
            out_ref[0, at, :] = nt(x_ref[at, :], w_ref[...]).astype(LOW)

    either(tiles_ref[0, pl.program_id(0)], near_ref, far_ref, count, body)


def project_back(hidden, weight, tiles, parts, part):
    rows = hidden.shape[0]
    return pl.pallas_call(
        functools.partial(back_kernel, count=weight[0].shape[0] // SPAN),
        grid_spec=pltpu.PrefetchScalarGridSpec(
            num_scalar_prefetch=1,
            grid=(tiles.shape[1],),
            in_specs=[whole(hidden.shape), *row_pair(weight)],
            out_specs=pl.BlockSpec((1, rows, SPAN), lambda j, t: (t[1, j], 0, t[2, j])),
        ),
        out_shape=jax.ShapeDtypeStruct((parts, rows, part), LOW),
        compiler_params=params(),
        cost_estimate=CHEAP,
        name="project_back",
    )(tiles, hidden, *weight)


def plain_kernel(x_ref, near_ref, far_ref, out_ref):
    for m in range(x_ref.shape[0] // SPAN):
        at = pl.ds(m * SPAN, SPAN)
        out_ref[at, :] = nn2(x_ref, at, near_ref, far_ref).astype(LOW)


def slope_kernel(x_ref, near_ref, far_ref, slope_ref, out_ref, sum_ref):
    total = jnp.zeros(sum_ref.shape, FULL)
    for m in range(x_ref.shape[0] // SPAN):
        at = pl.ds(m * SPAN, SPAN)
        value = nn2(x_ref, at, near_ref, far_ref) * slope_ref[at, :].astype(FULL)
        value = value.astype(LOW)
        out_ref[at, :] = value
        total = total + jnp.sum(value.astype(FULL), 0, keepdims=True)
    sum_ref[...] = total


def attn_grads(grad, weight, cols):
    rows = grad.shape[0]
    return pl.pallas_call(
        plain_kernel,
        grid=(cols // SPAN,),
        in_specs=[whole(grad.shape), *column_pair(weight, SPAN)],
        out_specs=pl.BlockSpec((rows, SPAN), lambda j: (0, j)),
        out_shape=jax.ShapeDtypeStruct((rows, cols), LOW),
        compiler_params=params(),
        cost_estimate=CHEAP,
        name="attn_grads",
    )(grad, *weight)


def up_grads(grad, weight, slope):
    rows, cols = slope.shape
    skip = (weight[0].shape[1] - cols) // SPAN
    tall = pl.BlockSpec((rows, SPAN), lambda j: (0, j))
    return pl.pallas_call(
        slope_kernel,
        grid=(cols // SPAN,),
        in_specs=[whole(grad.shape), *column_pair(weight, SPAN, skip), tall],
        out_specs=[tall, pl.BlockSpec((1, SPAN), lambda j: (0, j))],
        out_shape=[jax.ShapeDtypeStruct((rows, cols), LOW), jax.ShapeDtypeStruct((1, cols), FULL)],
        compiler_params=params(),
        cost_estimate=CHEAP,
        name="up_grads",
    )(grad, *weight, slope)


def input_kernel(
    tiles_ref, qg_ref, ug_ref, qn_ref, qf_ref, un_ref, uf_ref, x_ref, mean_ref, inv_ref, par_ref,
    out_ref, sums_ref, row_ref, *, count
):
    @pl.when(pl.program_id(0) == 0)
    def _():
        row_ref[...] = jnp.zeros_like(row_ref)

    def body(w_refs):
        wq_ref, wu_ref = w_refs
        sums = [jnp.zeros((1, SPAN), FULL) for _ in range(4)]
        for m in range(qg_ref.shape[0] // SPAN):
            at = pl.ds(m * SPAN, SPAN)
            first_grad = nt(qg_ref[at, :], wq_ref[...])
            second_grad = nt(ug_ref[at, :], wu_ref[...])
            normed = (x_ref[at, :].astype(FULL) - mean_ref[at, 0:1]) * inv_ref[at, 0:1]
            total = first_grad * par_ref[0:1, :] + second_grad * par_ref[2:3, :]
            out_ref[0, at, :] = total.astype(LOW)
            for n, value in enumerate((first_grad * normed, first_grad, second_grad * normed, second_grad)):
                sums[n] = sums[n] + jnp.sum(value, 0, keepdims=True)
            for n, value in enumerate((total, total * normed)):
                row_ref[n, at, :] += sum(value[:, o : o + 128] for o in range(0, SPAN, 128))
        sums_ref[0] = jnp.concatenate(sums, 0)

    either(tiles_ref[0, pl.program_id(0)], (qn_ref, un_ref), (qf_ref, uf_ref), count, body)


def input_grads(qkv_grad, up_grad, qkv_weight, up_weight, x, mean, inv, par, tiles, parts, part):
    rows = qkv_grad.shape[0]
    return pl.pallas_call(
        functools.partial(input_kernel, count=qkv_weight[0].shape[0] // SPAN),
        grid_spec=pltpu.PrefetchScalarGridSpec(
            num_scalar_prefetch=1,
            grid=(tiles.shape[1],),
            in_specs=[
                whole(qkv_grad.shape),
                whole(up_grad.shape),
                *row_pair(qkv_weight),
                *row_pair(up_weight),
                pl.BlockSpec((rows, SPAN), lambda j, t: (0, t[0, j])),
                whole(mean.shape),
                whole(inv.shape),
                pl.BlockSpec((4, SPAN), lambda j, t: (0, t[0, j])),
            ],
            out_specs=[
                pl.BlockSpec((1, rows, SPAN), lambda j, t: (t[1, j], 0, t[2, j])),
                pl.BlockSpec((1, 4, SPAN), lambda j, t: (t[1, j], 0, t[2, j])),
                whole((2, rows, 128)),
            ],
        ),
        out_shape=[
            jax.ShapeDtypeStruct((parts, rows, part), LOW),
            jax.ShapeDtypeStruct((parts, 4, part), FULL),
            jax.ShapeDtypeStruct((2, rows, 128), FULL),
        ],
        compiler_params=params(),
        cost_estimate=CHEAP,
        name="input_grads",
    )(tiles, qkv_grad, up_grad, *qkv_weight, *up_weight, x, mean, inv, par)


def weight_kernel(spots_ref, a_ref, b_ref, out_ref):
    out_ref[...] = tn(a_ref[...], b_ref[...]).astype(LOW)


def weight_grads(a, b, spots):
    rows, width = a.shape
    cols = b.shape[1]
    return pl.pallas_call(
        weight_kernel,
        grid_spec=pltpu.PrefetchScalarGridSpec(
            num_scalar_prefetch=1,
            grid=(width // SPAN,),
            in_specs=[pl.BlockSpec((rows, SPAN), lambda j, t: (0, j)), whole(b.shape)],
            out_specs=pl.BlockSpec((SPAN, cols), lambda j, t: (t[j], 0)),
        ),
        out_shape=jax.ShapeDtypeStruct((width, cols), LOW),
        compiler_params=params(),
        cost_estimate=CHEAP,
        name="weight_grads",
    )(spots, a, b)


def halves_kernel(a_ref, b_ref, near_ref, far_ref, *, count):
    value = tn(a_ref[...], b_ref[...]).astype(LOW)
    j = pl.program_id(0)

    @pl.when(j < count)
    def _():
        near_ref[...] = value

    @pl.when(j >= count)
    def _():
        far_ref[...] = value


def weight_halves(a, b):
    rows, width = a.shape
    cols = b.shape[1]
    count = width // SPAN // 2
    return pl.pallas_call(
        functools.partial(halves_kernel, count=count),
        grid=(2 * count,),
        in_specs=[pl.BlockSpec((rows, SPAN), lambda j: (0, j)), whole(b.shape)],
        out_specs=[
            pl.BlockSpec((SPAN, cols), lambda j: (jnp.minimum(j, count - 1), 0)),
            pl.BlockSpec((SPAN, cols), lambda j: (jnp.maximum(j - count, 0), 0)),
        ],
        out_shape=[jax.ShapeDtypeStruct((width // 2, cols), LOW)] * 2,
        compiler_params=params(),
        cost_estimate=CHEAP,
        name="weight_halves",
    )(a, b)


def reorder_kernel(spots_ref, x_ref, near_ref, far_ref):
    half = pl.num_programs(0) // 2

    @pl.when(pl.program_id(0) < half)
    def _():
        near_ref[...] = x_ref[...]

    @pl.when(pl.program_id(0) >= half)
    def _():
        far_ref[...] = x_ref[...]


def reordered(x, spots):
    rows, cols = x.shape
    count = rows // SPAN
    return pl.pallas_call(
        reorder_kernel,
        grid_spec=pltpu.PrefetchScalarGridSpec(
            num_scalar_prefetch=1,
            grid=(count,),
            in_specs=[pl.BlockSpec((SPAN, cols), lambda j, t: (t[j], 0))],
            out_specs=row_pair([jax.ShapeDtypeStruct((rows // 2, cols), LOW)], lambda j, t: j),
        ),
        out_shape=[jax.ShapeDtypeStruct((rows // 2, cols), LOW)] * 2,
        compiler_params=params(),
        cost_estimate=CHEAP,
        name="reorder",
    )(spots, x)


def rotary_table():
    half = ROTARY // 2
    places = jnp.arange(LEN).astype(FULL)
    freqs = BASE ** (-(jnp.arange(half).astype(FULL) * 2.0) / ROTARY)
    angles = places[:, None] * freqs[None, :]
    cosine, sine = jnp.cos(angles), jnp.sin(angles)
    rest = 128 - ROTARY
    zeros = jnp.zeros_like(sine)
    pad = jnp.zeros((LEN, rest), FULL)
    return jnp.stack(
        [
            jnp.concatenate([cosine, cosine, pad + 1.0], 1),
            jnp.concatenate([-sine, zeros, pad], 1),
            jnp.concatenate([zeros, sine, pad], 1),
        ]
    )


def arrange_kernel(table_ref, *refs):
    out_ref = refs[-1]
    source = table_ref[0, pl.program_id(0)]
    for n, x_ref in enumerate(refs[:-1]):

        @pl.when(source == n)
        def _():
            out_ref[...] = x_ref[...]


def arranged(blocks, table, piece):
    rows = blocks[0].shape[0]
    count = table.shape[1]
    at = jnp.arange(count, dtype=jnp.int32)
    used = table[0][None, :] == jnp.arange(len(blocks), dtype=jnp.int32)[:, None]
    before = used[:, None, :] & (at[None, None, :] <= at[None, :, None])
    last = jnp.max(jnp.where(before, at[None, None, :], -1), 2, keepdims=True)
    spots = jnp.sum(jnp.where(last == at[None, None, :], table[1][None, None, :], 0), 2)
    table = jnp.concatenate([table, spots], 0)

    def spec(n):
        return pl.BlockSpec((rows, piece), lambda i, t: (0, t[2 + n, i]))

    return pl.pallas_call(
        arrange_kernel,
        grid_spec=pltpu.PrefetchScalarGridSpec(
            num_scalar_prefetch=1,
            grid=(count,),
            in_specs=[spec(n) for n in range(len(blocks))],
            out_specs=pl.BlockSpec((rows, piece), lambda i, t: (0, i)),
        ),
        out_shape=jax.ShapeDtypeStruct((rows, count * piece), blocks[0].dtype),
        compiler_params=params(),
        cost_estimate=CHEAP,
        name="arrange",
    )(table, *blocks)


def join_kernel(spot_ref, *refs, count, cuts, turn):
    ins, outs = refs[:count], refs[count:]
    source = spot_ref[pl.program_id(0)]
    for n, x_ref in enumerate(ins):

        @pl.when(source == n)
        def _():
            for out_ref, start in zip(outs, cuts):
                if not turn:
                    out_ref[...] = x_ref[:, start : start + out_ref.shape[1]].astype(FULL)
                    continue
                for o in range(0, out_ref.shape[0], SPAN):
                    value = x_ref[:, start + o : start + o + SPAN].astype(FULL)
                    out_ref[o : o + SPAN, :] = value.T


def joined(pieces, spots, widths, turn):
    piece, cols = pieces[0].shape
    count = len(pieces)
    cuts = [sum(widths[:n]) for n in range(len(widths))]
    if turn:
        specs = [pl.BlockSpec((w, piece), lambda h, t: (0, h)) for w in widths]
        shapes = [jax.ShapeDtypeStruct((w, piece * count), FULL) for w in widths]
    else:
        specs = [pl.BlockSpec((piece, w), lambda h, t: (h, 0)) for w in widths]
        shapes = [jax.ShapeDtypeStruct((piece * count, w), FULL) for w in widths]
    return pl.pallas_call(
        functools.partial(join_kernel, count=count, cuts=cuts, turn=turn),
        grid_spec=pltpu.PrefetchScalarGridSpec(
            num_scalar_prefetch=1,
            grid=(count,),
            in_specs=[whole((piece, cols))] * count,
            out_specs=specs,
        ),
        out_shape=shapes,
        compiler_params=params(),
        cost_estimate=CHEAP,
        name="join",
    )(spots, *pieces)


def attach_kernel(x_ref, small_ref, out_ref):
    rows = x_ref.shape[0]
    out_ref[:rows, :] = x_ref[...]
    out_ref[rows:, :] = small_ref[...]


def attach(x, small):
    rows = x.shape[0] + small.shape[0]
    return pl.pallas_call(
        attach_kernel,
        in_specs=[pl.BlockSpec(memory_space=pltpu.VMEM)] * 2,
        out_specs=pl.BlockSpec(memory_space=pltpu.VMEM),
        out_shape=jax.ShapeDtypeStruct((rows, x.shape[1]), x.dtype),
        compiler_params=pltpu.CompilerParams(vmem_limit_bytes=SCOPED),
        cost_estimate=CHEAP,
        name="attach",
    )(x, small)


def swapped(v):
    return (v & 1) * 2 + (v >> 1)


def mixed_bits(v):
    return ((v & 1) ^ (v >> 1)) * 2 + (v >> 1)


class Order:
    def __init__(self):
        self.token, self.needs = (), ()

    def gate(self, *xs):
        out = lax.optimization_barrier(tuple(xs) + self.token)[: len(xs)]
        return out[0] if len(xs) == 1 else out

    def wait(self, *xs):
        out = self.gate(xs)
        self.token = tuple(jax.tree.leaves(out))
        return out[0] if len(xs) == 1 else out

    def need(self, *xs):
        self.needs += tuple(jax.tree.leaves(xs))

    def run(self, function, first, *rest):
        first = lax.optimization_barrier((first,) + self.token + self.needs)[0]
        out = function(first, *rest)
        self.token, self.needs = (out[0],) if isinstance(out, (tuple, list)) else (out,), ()
        return out


class Plan:
    def __init__(self, part):
        self.nd, self.nr, self.nc = (lax.axis_size(a) for a in ("dp", "row", "col"))
        self.d, self.r, self.c = (lax.axis_index(a) for a in ("dp", "row", "col"))
        self.part = part
        self.piece = part // self.nd
        self.ny = self.nr // 2
        spots = [(r, c) for r in range(self.nr) for c in range(self.nc)]
        goal = {(r, c): -r % 4 ^ swapped(c) for r, c in spots}
        self.pairs = [(r * self.nc + c, goal[r, c] * self.nc + swapped(r)) for r, c in spots]
        self.plane_pairs = [(r * self.nc + c, goal[r, c] * self.nc + c) for r, c in spots]
        self.line_pairs = [(goal[r, c] * self.nc + c, goal[r, c] * self.nc + swapped(r)) for r, c in spots]
        e = jnp.arange(2 * self.nd * self.ny, dtype=jnp.int32)
        self.straight = jnp.arange(part * self.nc // SPAN, dtype=jnp.int32)
        k, step, y = e // (self.nd * self.ny), e // self.ny % self.nd, e % self.ny
        self.places = jnp.stack(
            [swapped(self.r ^ (2 * y + k) ^ mixed_bits(self.c)), lax.rem(self.d - step + self.nd, self.nd)]
        ).astype(jnp.int32)
        self.blocks = (self.places[1] * self.nr + (self.r ^ (2 * y + k))).astype(jnp.int32)

    def move(self, x, pairs):
        moved = lax.ppermute(x, ("row", "col"), [(a, b) for a, b in pairs if a != b])
        here = self.r * self.nc + self.c
        stays = [here == a for a, b in pairs if a == b]

        def settle(moved, cut=lambda v: v):
            if not stays:
                return cut(moved)
            return jnp.where(functools.reduce(jnp.logical_or, stays), cut(x), cut(moved))

        return moved, settle

    def turn(self, x):
        return self.move(x, self.pairs)

    def turn_back(self, x):
        return self.move(x, [(b, a) for a, b in self.pairs])

    def turn_plane(self, x):
        return self.move(x, self.plane_pairs)

    def turn_line(self, x):
        return self.move(x, self.line_pairs)

    def cross(self, x):
        spots = [(r, c) for r in range(self.nr) for c in range(self.nc)]
        return self.move(x, [(r * self.nc + c, c * self.nc + swapped(r)) for r, c in spots])

    def gather_plane(self, own):
        value = lax.all_gather(own, ("dp", "row"), axis=0, tiled=True)
        if self.piece == SPAN:
            return value

        return self.chunks_of(value, self.blocks)

    def chunks_of(self, value, order):
        return jnp.concatenate(
            [
                lax.dynamic_slice_in_dim(value, order[i] * self.piece, self.piece, 0)
                for i in range(order.shape[0])
            ],
            0,
        )

    def plane_order(self):
        return self.blocks if self.piece == SPAN else self.straight

    def flip(self, x):
        return lax.ppermute(x, "row", [(r, r ^ 1) for r in range(self.nr)])

    def hop_y(self, x):
        return lax.ppermute(x, "row", [(r, r ^ 2) for r in range(self.nr)])

    def hop_x(self, x, s):
        return lax.ppermute(x, "dp", [(d, (d + s) % self.nd) for d in range(self.nd)])

    def roll(self, x, s):
        return lax.ppermute(x, "col", [(i, (i + s) % self.nc) for i in range(self.nc)])

    def rolls(self, x):
        return self.roll(x, 1), self.roll(x, -1)

    def two_away(self, ahead, behind):
        return (
            lax.ppermute(ahead, "col", [(1, 2), (2, 3)]),
            lax.ppermute(behind, "col", [(2, 1), (1, 0)]),
        )

    def arrange(self, own, one, two):
        away = lax.rem(self.c - self.places[0] + self.nc, self.nc)
        right = jnp.where(self.c >= 2, 2, 4)
        table = jnp.stack([jnp.where(away == 2, right, away), self.places[1]])
        blocks = [own, one[0], two[0], one[1], two[1]]
        if self.piece % 128 == 0:
            return arranged(blocks, table, self.piece)
        blocks = jnp.stack(blocks)
        chunks = [
            lax.dynamic_slice(
                blocks, [table[0, i], 0, table[1, i] * self.piece], (1, own.shape[0], self.piece)
            )[0]
            for i in range(table.shape[1])
        ]
        return jnp.concatenate(chunks, -1)

    def tiles(self):
        if self.piece != SPAN:
            e = self.straight
            return None, jnp.stack([e, 0 * e, e])
        far = jnp.array([2, 0, 1, 3], jnp.int32)
        far, step = jnp.repeat(far, self.nd), jnp.tile(jnp.arange(self.nd, dtype=jnp.int32), 4)
        q = self.r ^ mixed_bits(self.c) ^ swapped(far ^ self.c)
        block = ((q & 1) * self.nd + step) * self.ny + (q >> 1)
        place = lax.rem(self.d - step + self.nd, self.nd)
        table = jnp.stack([block, far ^ self.c, place]).astype(jnp.int32)
        first = table[:, : self.nd].at[1].set(0)
        return first, table[:, self.nd :]

    def to_parts(self, value):
        if value.shape[0] == self.nc:
            return value
        parts = []
        for j in range(self.nc):
            x = self.r ^ mixed_bits(self.c) ^ swapped(j)
            pieces = []
            for h in range(self.nd):
                s = lax.rem(self.d - h + self.nd, self.nd)
                at = ((lax.rem(x, 2) * self.nd + s) * self.ny + x // 2) * self.piece
                pieces.append(lax.dynamic_slice_in_dim(value[0], at, self.piece, 1))
            parts.append(jnp.concatenate(pieces, -1))
        return jnp.stack(parts)

    def own_piece(self, block):
        return lax.dynamic_slice_in_dim(block, self.d * self.piece, self.piece, 0)

    def spread_one(self, own):
        return [self.hop_x(own, s) for s in range(1, self.nd)], self.hop_y(own)

    def spread_two(self, by_x, by_y):
        half = self.piece // 2
        return [
            (self.hop_y(x[:half]), self.hop_x(by_y[half:], s + 1)) for s, x in enumerate(by_x)
        ]

    def spread_end(self, own, by_x, by_y, both):
        chunks = [own, by_y]
        for x, pair in zip(by_x, both):
            chunks += [x, *pair]
        return jnp.concatenate(chunks, 0)

    def sum_plane_grad(self, grad):
        if self.piece != SPAN:
            count = self.blocks.shape[0]
            place = self.blocks[None, :] == jnp.arange(count, dtype=jnp.int32)[:, None]
            grad = self.chunks_of(grad, jnp.argmax(place, 1).astype(jnp.int32))
        return lax.psum_scatter(grad, ("dp", "row"), scatter_dimension=0, tiled=True)

    def core_order(self):
        count = self.straight.shape[0]
        return lax.rem(self.straight + lax.rem(self.r, 2) * (count // 2), count)

    def sum_cores(self, grad):
        pairs = [[r, r + 1] for r in range(0, self.nr, 2)]
        return lax.psum_scatter(
            grad, "row", scatter_dimension=0, axis_index_groups=pairs, tiled=True
        )

    def collect_one(self, near, flipped):
        shape = (self.nd, self.ny, 2, self.piece // 2, near.shape[1])
        near = total(near, flipped).reshape(shape)
        by_x = [self.hop_x(near[s, :, 0], -s) for s in range(1, self.nd)]
        by_y = self.hop_y(near[:, 1, 1])
        return near, by_x, by_y

    def collect_two(self, near, by_x, by_y):
        low = total(near[0, :, 0], *by_x)
        high = total(near[:, 0, 1], by_y)
        return low, high, self.hop_y(low[1]), [self.hop_x(high[s], -s) for s in range(1, self.nd)]

    def collect_end(self, low, high, by_y, by_x):
        return jnp.concatenate([total(low[0], by_y), total(high[0], *by_x)], 0)

    def join(self, mine):
        return [self.hop_x(mine, s) for s in range(1, self.nd)]

    def join_end(self, mine, others, widths, turn):
        places = jnp.arange(self.nd)
        spots = lax.rem(self.d - places + self.nd, self.nd).astype(jnp.int32)
        pieces = [mine, *others]
        if turn and self.piece % 128:
            first, second = joined(pieces, spots, widths, False)
            return first.T, second.T
        return joined(pieces, spots, widths, turn)

    def pick(self, parts, offset):
        j = jnp.clip(self.c + offset, 0, self.nc - 1)
        return lax.dynamic_index_in_dim(parts, j, 0, False)

    def pick_around(self, parts, offset):
        j = lax.rem(self.c + offset + self.nc, self.nc)
        return lax.dynamic_index_in_dim(parts, j, 0, False)

    def sum_one(self, far):
        return (
            lax.ppermute(far, "col", [(0, 1), (1, 2)]),
            lax.ppermute(far, "col", [(3, 2), (2, 1)]),
        )

    def sum_two(self, parts, moved):
        return (
            self.roll(total(self.pick_around(parts, 1), moved[0]), 1),
            self.roll(total(self.pick_around(parts, -1), moved[1]), -1),
        )


def total(*values):
    return sum(v.astype(FULL) for v in values).astype(LOW)


def split_exact(value):
    parts = []
    for _ in range(3):
        part = lax.reduce_precision(value, 8, 7)
        parts.append(part.astype(LOW))
        value = value - part
    return jnp.concatenate(parts, 0)


def local(
    tokens,
    segment_ids,
    norm1_gain,
    norm1_bias,
    norm2_gain,
    norm2_bias,
    qkv_weight,
    qkv_bias,
    out_weight,
    out_bias,
    up_weight,
    up_bias,
    down_weight,
    down_bias,
    cotangent,
):
    rows, part = tokens.shape
    plan, order = Plan(part), Order()
    width = part * plan.nc
    first_tiles, rest_tiles = plan.tiles()
    parts = plan.nc if plan.piece == SPAN else 1
    part_cols = width // parts
    qkv_cols = qkv_weight.shape[1]
    attn_cols = out_weight.shape[0]
    up_cols = up_weight.shape[1]

    small = split_exact(jnp.stack([norm1_gain, norm1_bias, norm2_gain, norm2_bias]))
    own = attach(tokens, jnp.concatenate([small, jnp.zeros((16 - small.shape[0], part), LOW)], 0))
    crossed = jnp.concatenate([segment_ids.astype(FULL).reshape(-1), qkv_bias, up_bias])
    crossed, settle_crossed = plan.cross(crossed)
    one = plan.rolls(own)
    rest = jnp.concatenate(
        [
            plan.own_piece(up_weight),
            plan.own_piece(out_weight.T),
            plan.own_piece(down_weight.T),
        ],
        1,
    )
    rest, settle_rest = plan.turn_plane(rest)
    turned_qkv, settle_qkv = plan.turn(plan.own_piece(qkv_weight))
    table = rotary_table()
    turned_qkv, table, crossed, rest, one = order.wait(turned_qkv, table, crossed, rest, one)

    two = plan.two_away(*one)
    turned_up, settle_up = plan.turn_line(settle_rest(rest, lambda v: v[:, :up_cols]))
    turned_qkv = settle_qkv(turned_qkv)
    qkv_x, qkv_y = plan.spread_one(turned_qkv)
    qkv_x, qkv_y = order.wait(qkv_x, qkv_y)

    qkv_both = order.wait(plan.spread_two(qkv_x, qkv_y))
    qkv_near = plan.spread_end(turned_qkv, qkv_x, qkv_y, qkv_both)
    back_own = settle_rest(rest, lambda v: v[:, up_cols:])
    qkv_near, back_own, turned_up = order.wait(qkv_near, back_own, turned_up)
    up_all = plan.gather_plane(settle_up(turned_up))
    two = order.wait(two)

    qkv_far = plan.flip(order.gate(qkv_near))
    turned_back, settle_back = plan.turn_line(order.gate(back_own))
    x = order.run(plan.arrange, own, one, two)
    small = x[rows : rows + 12].astype(FULL)
    par = (small[0:4] + small[4:8]) + small[8:12]
    first, second, mean, inv = order.run(norms, x, par, rows)
    qkv_far = order.wait(qkv_far)
    crossed = settle_crossed(crossed)
    segs = crossed[: segment_ids.size].astype(jnp.int32).reshape(segment_ids.shape)
    biases = crossed[segment_ids.size :]
    seg_col = jnp.broadcast_to(segs[:, :, None], segs.shape + (128,))
    seg_row = segs[:, None, :]
    qkv_w = (qkv_near, qkv_far)
    qkv = order.run(project_qkv, first, qkv_w, biases[:qkv_cols], table)
    turned_back = order.wait(turned_back)

    turned_back = settle_back(turned_back)
    back_x, back_y = plan.spread_one(turned_back)
    grad_one = plan.rolls(order.gate(cotangent))
    attn, logs = order.run(attend, qkv, seg_col, seg_row)
    up_w = order.run(reordered, up_all, plan.plane_order())
    back_x, back_y = order.wait(back_x, back_y)

    back_both = plan.spread_two(back_x, back_y)
    act, slope = order.run(project_up, second, up_w, biases[qkv_cols:])
    hidden = jnp.concatenate([attn, act], 1)
    hidden, back_both, grad_one = order.wait(hidden, back_both, grad_one)

    back_near = plan.spread_end(turned_back, back_x, back_y, back_both)
    back_far = plan.flip(back_near)
    grad_two = plan.two_away(*grad_one)
    back_far = order.wait(back_far)
    back_w = (back_near, back_far)

    if first_tiles is not None:
        branch_far = order.run(project_back, hidden, back_w, first_tiles, 1, part)[0]
        branch_one = plan.sum_one(branch_far)
    branch = plan.to_parts(order.run(project_back, hidden, back_w, rest_tiles, parts, part_cols))
    if first_tiles is None:
        branch_one = plan.sum_one(plan.pick_around(branch, 2))
    order.need(grad_two)
    grad = order.run(plan.arrange, cotangent, grad_one, grad_two)
    back_g = order.run(weight_grads, grad, hidden, plan.plane_order())
    branch_one = order.wait(branch_one)

    branch_two = plan.sum_two(branch, branch_one)
    back_g = plan.sum_plane_grad(order.gate(back_g))
    attn_grad = order.run(attn_grads, grad, back_w, attn_cols)
    up_grad, up_bias_grad = order.run(up_grads, grad, back_w, slope)
    qkv_grad, qkv_bias_grad = order.run(
        attend_back, qkv, attn_grad, logs, seg_col, seg_row, table
    )
    qkv_g = order.run(weight_halves, first, qkv_grad)
    branch_two = order.wait(branch_two)

    qkv_flip = plan.flip(order.gate(qkv_g[1]))
    biases = jnp.concatenate(
        [jnp.sum(order.gate(cotangent), 0, dtype=FULL), qkv_bias_grad[0], up_bias_grad[0]]
    )
    biases_flip = plan.flip(biases)
    up_g = order.run(weight_halves, second, up_grad)
    mixed = plan.pick(branch, 0).astype(FULL) + sum(v.astype(FULL) for v in branch_two)
    mixed = (tokens.astype(FULL) + mixed + (out_bias + down_bias)).astype(LOW)
    biases = biases + biases_flip
    biases_hop = plan.hop_y(biases)
    mixed, qkv_flip, biases_hop, back_g = order.wait(mixed, qkv_flip, biases_hop, back_g)

    qkv_c, qkv_x, qkv_y = plan.collect_one(qkv_g[0], qkv_flip)
    up_flip = plan.flip(order.gate(up_g[1]))
    turned_back, settle_back = plan.turn_back(back_g)
    up_flip = order.wait(up_flip)
    grads = (qkv_grad, up_grad, qkv_w, up_w, x, mean, inv, par)
    sums_far, row_far = None, 0.0
    if first_tiles is not None:
        mine_far, sums_far, row_far = order.run(input_grads, *grads, first_tiles, 1, part)
        mine_one = plan.sum_one(mine_far[0])
    turned_back, qkv_x, qkv_y = order.wait(turned_back, qkv_x, qkv_y)

    qkv_low, qkv_high, qkv_y, qkv_x = plan.collect_two(qkv_c, qkv_x, qkv_y)
    turned_back = settle_back(turned_back)
    back_joined = plan.join(turned_back)
    mine, sums, row_sums = order.run(input_grads, *grads, rest_tiles, parts, part_cols)
    mine, sums, row_sums = plan.to_parts(mine), plan.to_parts(sums), row_sums + row_far
    if first_tiles is None:
        mine_one = plan.sum_one(plan.pick_around(mine, 2))
    mine_one, qkv_x, qkv_y = order.wait(mine_one, qkv_x, qkv_y)

    mine_two = plan.sum_two(mine, mine_one)
    up_c, up_x, up_y = plan.collect_one(up_g[0], order.gate(up_flip))
    back_joined, up_x, up_y = order.wait(back_joined, up_x, up_y)

    up_low, up_high, up_y, up_x = plan.collect_two(up_c, up_x, up_y)
    turned_qkv, settle_qkv = plan.turn_back(
        order.gate(plan.collect_end(qkv_low, qkv_high, qkv_y, qkv_x))
    )
    out_g, down_g = plan.join_end(
        turned_back, back_joined, (attn_cols, turned_back.shape[1] - attn_cols), True
    )
    out_g, down_g, up_x, up_y, turned_qkv, mine_two = order.wait(
        out_g, down_g, up_x, up_y, turned_qkv, mine_two
    )

    turned_up, settle_up = plan.turn_back(plan.collect_end(up_low, up_high, up_y, up_x))
    turned_qkv = settle_qkv(turned_qkv)
    qkv_joined = plan.join(turned_qkv)
    biases = biases + biases_hop
    biases_join = plan.join(order.gate(biases))
    row_sums = jnp.sum(row_sums, 2).reshape(-1)
    own_sums = [plan.pick_around(sums, n).reshape(-1) for n in range(plan.nc)]
    if sums_far is not None:
        own_sums[2] = sums_far[0].reshape(-1)
    own_sums = [jnp.concatenate([v, row_sums]) for v in own_sums]
    sums_moved = [plan.roll(own_sums[n], n) for n in range(1, plan.nc)]
    biases_join, turned_up, qkv_joined, sums_moved = order.wait(
        biases_join, turned_up, qkv_joined, sums_moved
    )
    biases = biases + sum(biases_join)
    bias_grads, settle_biases = plan.turn_back(biases[part:])

    turned_up = settle_up(turned_up)
    up_joined = plan.join(turned_up)
    sums = own_sums[0] + sum(sums_moved)
    norm_sums, grad_stats = sums[: 4 * part], sums[4 * part :].reshape(2, rows, 1)
    norm_sums = norm_sums + plan.flip(norm_sums)
    norm_sums = norm_sums + plan.hop_y(norm_sums)
    norm_sums = norm_sums + sum(plan.join(norm_sums))
    mine = plan.pick(mine, 0).astype(FULL) + sum(v.astype(FULL) for v in mine_two)
    mean, inv = mean[:, :1], inv[:, :1]
    own_normed = (tokens.astype(FULL) - mean) * inv
    input_grad = cotangent.astype(FULL) + inv * (
        mine - grad_stats[0] / width - own_normed * (grad_stats[1] / width)
    )
    qkv_g = plan.join_end(turned_qkv, qkv_joined, (qkv_cols,), False)[0]
    input_grad, qkv_g, norm_sums, up_joined, bias_grads = order.wait(
        input_grad, qkv_g, norm_sums, up_joined, bias_grads
    )

    up_g = plan.join_end(turned_up, up_joined, (up_cols,), False)[0]
    bias_grads = settle_biases(bias_grads)
    norm_sums = norm_sums.reshape(4, part)
    output_bias_grad = biases[:part]
    return (
        mixed,
        input_grad,
        norm_sums[0],
        norm_sums[1],
        norm_sums[2],
        norm_sums[3],
        qkv_g,
        bias_grads[:qkv_cols],
        out_g,
        output_bias_grad,
        up_g,
        bias_grads[qkv_cols:],
        down_g,
        output_bias_grad,
    )


def solution(mesh):
    in_specs = (
        P(("dp", "row"), "col"),
        P(("dp", "col"), None),
        P("col"),
        P("col"),
        P("col"),
        P("col"),
        P("col", "row"),
        P("row"),
        P("row", "col"),
        P("col"),
        P("col", "row"),
        P("row"),
        P("row", "col"),
        P("col"),
        P(("dp", "row"), "col"),
    )
    out_specs = (
        P(("dp", "row"), "col"),
        P(("dp", "row"), "col"),
        P("col"),
        P("col"),
        P("col"),
        P("col"),
        P("col", "row"),
        P("row"),
        P("row", "col"),
        P("col"),
        P("col", "row"),
        P("row"),
        P("row", "col"),
        P("col"),
    )
    return jax.shard_map(local, mesh=mesh, in_specs=in_specs, out_specs=out_specs, check_vma=False)
```
